512 devices in a mesh: gx: 8 (over y), gy: 8 (over x, core), gz: 8 (over z).
Axes of the slice: x: 4, y: 8, z: 8, core: 2. Of those that a mesh axis runs over, the one named last changes fastest.
Arguments:
- right_side: float32 [64, 128, 1024], P('gx', 'gy', 'gz'), may hold values from -12 to 12
- face_coefficients: bfloat16 [3, 64, 128, 1024], P(None, 'gx', 'gy', 'gz'), may hold values from 0.25 to 4
- solid: int32 [64, 128, 1024], P('gx', 'gy', 'gz'), may hold values 0 or 1
Outputs:
- solution_field: float32 [64, 128, 1024], P('gx', 'gy', 'gz')
- residual: float32 [64, 128, 1024], P('gx', 'gy', 'gz')
- direction: float32 [64, 128, 1024], P('gx', 'gy', 'gz')
The draws below stay inside these ranges and needn't reach their ends.
All inputs are finite; a program needn't handle non-finite values. No bound on the sum of `solid` on one device may be relied on, other than what follows from the above.
Results may differ from the reference program's by a relative error of at most 0.0003.
Values may be sent and summed in bfloat16 or wider, within the bound.
No kernel may reach another device: no remote copies, remote signals or barrier semaphores. Data moves between devices by JAX's collectives and lax.ppermute only.
A program may use at most 64 MiB of HBM per device.

```python
import math
import jax
import jax.numpy as jnp
from jax import lax

LEVELS = 4
SWEEPS = 6
NX = 64
NY = 128
NZ = 1024


def draw_right_side(key, part):
    key = jax.random.fold_in(key, 11)
    key_cells, key_planes = jax.random.split(key)
    planes = jax.random.uniform(key_planes, (NZ,), jnp.float32)
    rising = jnp.arange(NX, dtype=jnp.float32) / NX
    scales = 0.3 * jnp.power(10.0, 0.5 * rising[:, None, None] + 0.5 * planes[None, None, :])
    cells = jax.random.truncated_normal(key_cells, -4.0, 4.0, (NX, NY, NZ), jnp.float32)
    return cells * scales


def set_ends(drawn, own_key, least, high):
    place = [jax.random.randint(jax.random.fold_in(own_key, axis), (), 0, length) for axis, length in enumerate(drawn.shape)]
    main_axis = drawn.shape.index(max(drawn.shape))
    neighbour = place[:main_axis] + [(place[main_axis] + 1) % drawn.shape[main_axis]] + place[main_axis + 1:]
    return drawn.at[tuple(place)].set(least).at[tuple(neighbour)].set(high)


def shard_levels(key, shape, pieces, least, high):
    factor_of, own = 1.0, jax.random.fold_in(key, 6)
    for dim, blocks in pieces:
        draws = jnp.exp(jax.random.uniform(jax.random.fold_in(own, dim), (blocks,), jnp.float32, least / len(pieces), high / len(pieces)))
        factor_of = factor_of * jnp.repeat(draws, shape[dim] // blocks).reshape([-1 if axis == dim else 1 for axis in range(len(shape))])
    return factor_of


def setup_inputs(seed: int = 0) -> dict:
    streams_of = jax.random.split(jax.random.key(seed), 4)
    right_side = draw_right_side(jax.random.fold_in(streams_of[3], 71), 0)
    face_coefficients = jnp.clip(jnp.exp(math.log(4.0) - 2.7725887 * jax.random.uniform(streams_of[1], (3, NX, NY, NZ), jnp.float32) ** shard_levels(streams_of[1], (3, NX, NY, NZ), ((1, 8), (2, 8), (3, 8)), -0.2, 0.2)), 0.25, 4.0).astype(jnp.bfloat16)
    solid = set_ends((jax.random.randint(streams_of[2], (NX, NY, NZ), 0, 4) < 1).astype(jnp.int32), jax.random.fold_in(streams_of[2], 1), 0, 1)
    return dict(right_side=right_side, face_coefficients=face_coefficients, solid=solid)


absorption = 0.001
relaxation = 0.8

def stencil(padded, grid_level):
    low_faces, high_faces, diagonal = grid_level
    centre = padded[1:-1, 1:-1, 1:-1]
    result = diagonal * centre
    result = result - low_faces[0] * padded[:-2, 1:-1, 1:-1] - high_faces[0] * padded[2:, 1:-1, 1:-1]
    result = result - low_faces[1] * padded[1:-1, :-2, 1:-1] - high_faces[1] * padded[1:-1, 2:, 1:-1]
    result = result - low_faces[2] * padded[1:-1, 1:-1, :-2] - high_faces[2] * padded[1:-1, 1:-1, 2:]
    return result

def padded_stencil(estimate, grid_level):
    return stencil(jnp.pad(estimate, 1), grid_level)

def fine_faces(rimmed, starts):
    low_list = []
    high_list = []
    for dimension in range(3):
        channel = rimmed[dimension]
        centre = channel[1:-1, 1:-1, 1:-1]
        previous = channel[tuple((slice(0, -2) if other == dimension else slice(1, -1) for other in range(3)))]
        following = channel[tuple((slice(2, None) if other == dimension else slice(1, -1) for other in range(3)))]
        position = lax.broadcasted_iota(jnp.int32, centre.shape, dimension) + starts[dimension]
        high_list.append(jnp.sqrt(centre * following))
        low_list.append(jnp.sqrt(centre * previous) + jnp.where(position == 0, centre, 0.0))
    return (jnp.stack(low_list), jnp.stack(high_list))

def diagonal_of(low_faces, high_faces, absorb_level):
    return absorb_level + low_faces[0] + high_faces[0] + low_faces[1] + high_faces[1] + low_faces[2] + high_faces[2]

def blocked(values):
    size_x, size_y, size_z = values.shape
    return values.reshape(size_x // 2, 2, size_y // 2, 2, size_z // 2, 2)

def coarsen(low_faces, high_faces):
    coarse_low = jnp.stack([0.25 * lax.optimization_barrier(jnp.sum(blocked(low_faces[0])[:, 0], axis=(2, 4))), 0.25 * lax.optimization_barrier(jnp.sum(blocked(low_faces[1])[:, :, :, 0], axis=(1, 4))), 0.25 * lax.optimization_barrier(jnp.sum(blocked(low_faces[2])[:, :, :, :, :, 0], axis=(1, 3)))])
    coarse_high = jnp.stack([0.25 * lax.optimization_barrier(jnp.sum(blocked(high_faces[0])[:, 1], axis=(2, 4))), 0.25 * lax.optimization_barrier(jnp.sum(blocked(high_faces[1])[:, :, :, 1], axis=(1, 4))), 0.25 * lax.optimization_barrier(jnp.sum(blocked(high_faces[2])[:, :, :, :, :, 1], axis=(1, 3)))])
    return (coarse_low, coarse_high)

def build_levels(rimmed, starts):
    low_faces, high_faces = fine_faces(rimmed, starts)
    levels = [(low_faces, high_faces, diagonal_of(low_faces, high_faces, absorption))]
    for depth_index in range(1, LEVELS):
        low_faces, high_faces = coarsen(low_faces, high_faces)
        levels.append((low_faces, high_faces, diagonal_of(low_faces, high_faces, absorption * 4.0 ** depth_index)))
    return levels

def restrict(values):
    return 0.5 * lax.optimization_barrier(jnp.sum(blocked(values), axis=(1, 3, 5)))

def prolong(values):
    return jnp.repeat(jnp.repeat(jnp.repeat(values, 2, axis=0), 2, axis=1), 2, axis=2)

def sweeps(source, grid_level, apply_fn):
    diagonal = grid_level[2]
    estimate = relaxation * source / diagonal
    for sweep_index in range(SWEEPS - 1):
        estimate = estimate + relaxation * (source - apply_fn(estimate, grid_level)) / diagonal
    return estimate

def cycle(levels, source, depth_index):
    grid_level = levels[depth_index]
    if depth_index == len(levels) - 1:
        return sweeps(source, grid_level, padded_stencil)
    diagonal = grid_level[2]
    smoothed = relaxation * source / diagonal
    leftover = source - padded_stencil(smoothed, grid_level)
    coarse = cycle(levels, restrict(leftover), depth_index + 1)
    corrected = smoothed + prolong(coarse)
    return corrected + relaxation * (source - padded_stencil(corrected, grid_level)) / diagonal

def reference(right_side, face_coefficients, solid):
    weight = 1.0 - 0.75 * solid.astype(jnp.float32)
    conductance = (face_coefficients.astype(jnp.float32) * weight[None]).astype(jnp.bfloat16)
    rimmed = jnp.pad(conductance, ((0, 0), (1, 1), (1, 1), (1, 1))).astype(jnp.float32)
    levels = build_levels(rimmed, (0, 0, 0))
    first_pre = cycle(levels, right_side, 0)
    projected = jnp.sum(right_side * first_pre)
    image_field = padded_stencil(first_pre, levels[0])
    curvature = jnp.sum(first_pre * image_field)
    step_size = projected / curvature
    solution_field = step_size * first_pre
    residual = right_side - step_size * image_field
    next_pre = cycle(levels, residual, 0)
    momentum = jnp.sum(residual * next_pre) / projected
    direction = next_pre + momentum * first_pre
    return (solution_field, residual, direction)
```

```python
import functools

import jax
import jax.numpy as jnp
from jax import lax
from jax.experimental import pallas as pl
from jax.experimental.pallas import tpu as pltpu
from jax.sharding import PartitionSpec as P

F32 = jnp.float32
BF16 = jnp.bfloat16
ABSORB = 0.001
RELAX = 0.8
KEEP = 0.2
SWEEPS = 6
VMEM_LIMIT = 24 * 1024 * 1024


def one_hot(rows, cols, rule, weight=1.0):
    r = lax.broadcasted_iota(jnp.int32, (rows, cols), 0)
    c = lax.broadcasted_iota(jnp.int32, (rows, cols), 1)
    return jnp.where(rule(r, c), weight, 0.0).astype(BF16)


def spread(values, matrix):
    high = values.astype(BF16)
    low = (values - high.astype(F32)).astype(BF16)
    return jnp.dot(high, matrix, preferred_element_type=F32) + jnp.dot(
        low, matrix, preferred_element_type=F32
    )


def pick(matrix, values):
    high = values.astype(BF16)
    low = (values - high.astype(F32)).astype(BF16)
    return jnp.dot(matrix, high, preferred_element_type=F32) + jnp.dot(
        matrix, low, preferred_element_type=F32
    )


def turn(values, shift, axis):
    return pltpu.roll(values, shift % values.shape[axis], axis)


def iota(shape, dim):
    return lax.broadcasted_iota(jnp.int32, shape, dim)


def plane_terms(v, f1, f2):
    return turn(v, 1, 0) * f1 + turn(v * f1, -1, 0) + turn(v, 1, 1) * f2 + turn(v * f2, -1, 1)


def neighbours(v_ref, f0_ref, f1_ref, f2_ref, p):
    return (
        f0_ref[p] * v_ref[p - 1]
        + f0_ref[p + 1] * v_ref[p + 1]
        + plane_terms(v_ref[p], f1_ref[p], f2_ref[p])
    )


def neighbours_3d(v, f0, f1, f2):
    zero = jnp.zeros_like(v[:1])
    up = f0 * v
    return (
        f0 * jnp.concatenate([zero, v[:-1]], 0)
        + jnp.concatenate([up[1:], zero], 0)
        + turn(v, 1, 1) * f1
        + turn(v * f1, -1, 1)
        + turn(v, 1, 2) * f2
        + turn(v * f2, -1, 2)
    )


def row_pairs(t_ref, values, both):
    out = []
    for half in range(2):
        t_ref[half] = values[:, 128 * half : 128 * half + 128]
        first = t_ref[half, pl.ds(0, 20, 2), :]
        out.append(first + t_ref[half, pl.ds(1, 20, 2), :] if both else first)
    return out


def put_rows(r_ref, q, halves):
    for half in range(2):
        r_ref[q, pl.ds(0, 20), pl.ds(128 * half, 128)] = halves[half]


def prepare_kernel(s_ref, fc_ref, solid_ref, out_ref):
    s = s_ref[...]
    high = s.astype(BF16)
    out_ref[:, 0] = high
    out_ref[:, 1] = (s - high.astype(F32)).astype(BF16)
    weight = 1.0 - 0.75 * solid_ref[...].astype(F32)
    for a in range(3):
        out_ref[:, 2 + a] = (fc_ref[a].astype(F32) * weight).astype(BF16)


def rim_kernel(own_ref, before_ref, after_ref, out_ref):
    lane = iota((16, 128), 1)

    def body(p, carry):
        rim = jnp.zeros((16, 128), F32)
        for f in range(5):
            out_ref[p, f] = own_ref[p, f]
            t = jnp.where(lane < 64, after_ref[p, f].astype(F32), before_ref[p, f].astype(F32))
            t = turn(t, 24 * f + 12, 1)
            rim = jnp.where((lane >= 24 * f) & (lane < 24 * f + 24), t, rim)
        out_ref[p, 5] = rim.astype(BF16)
        return carry

    lax.fori_loop(0, 8, body, 0)


def first_kernel(
    x_ref, ym_ref, yp_ref,
    s_ref, f0_ref, f1_ref, f2_ref, w_ref, d_ref,
    s1_ref, f10_ref, f11_ref, f12_ref, w1_ref, pay_ref,
    c0_ref, c1_ref, c2_ref, sm_ref, t_ref, r0_ref, r1_ref, r2_ref, rs_ref,
    l10_ref, l11_ref, l12_ref, sm1_ref, t1_ref, u_ref,
):
    at_x = lax.axis_index("gx") == 0
    at_y = lax.axis_index("gy") == 0
    at_z = lax.axis_index("gz") == 0
    lane = iota((40, 128), 1)
    side = (lane < 12) | (lane >= 116)

    def unpack(p, carry):
        tiles = []
        for f in range(6):
            column = jnp.concatenate(
                [ym_ref[p, f].astype(F32), x_ref[p, f].astype(F32), yp_ref[p, f].astype(F32)], 0
            )
            tiles.append(turn(column, -4, 0)[:40])
        rims = [
            jnp.where(side, turn(tiles[5], -(24 * f + 12), 1), 0.0) for f in range(5)
        ]
        s_ref[p, :, 0:128] = tiles[0] + tiles[1]
        s_ref[p, :, 128:256] = rims[0] + rims[1]
        for a, c_ref in enumerate((c0_ref, c1_ref, c2_ref)):
            c_ref[p, :, 0:128] = tiles[2 + a]
            c_ref[p, :, 128:256] = rims[2 + a]
        return carry

    lax.fori_loop(0, 32, unpack, 0)

    def faces(p, carry):
        before = jnp.maximum(p - 1, 0)
        f0_ref[p] = jnp.sqrt(c0_ref[p] * c0_ref[before])
        c1 = c1_ref[p]
        f1_ref[p] = jnp.sqrt(c1 * turn(c1, 1, 0))
        c2 = c2_ref[p]
        f2_ref[p] = jnp.sqrt(c2 * turn(c2, 1, 1))
        return carry

    lax.fori_loop(0, 32, faces, 0)
    f0_ref[32] = jnp.zeros((40, 256), F32)

    first_row = (iota((40, 256), 0) == 12) & at_y
    first_lane = (iota((40, 256), 1) == 0) & at_z
    for ref in (r0_ref, r1_ref, r2_ref, rs_ref):
        ref[...] = jnp.zeros_like(ref)

    def diagonals(q, carry):
        lows = []
        for i in range(2):
            p = 2 * q + i
            f0, f1, f2 = f0_ref[p], f1_ref[p], f2_ref[p]
            low0 = f0 + jnp.where((p == 12) & at_x, c0_ref[p], 0.0)
            low1 = f1 + jnp.where(first_row, c1_ref[p], 0.0)
            low2 = f2 + jnp.where(first_lane, c2_ref[p], 0.0)
            d = ABSORB + low0 + f0_ref[p + 1] + low1 + turn(f1, -1, 0) + low2 + turn(f2, -1, 1)
            w = RELAX / d
            d_ref[p] = d
            w_ref[p] = w
            sm_ref[p] = w * s_ref[p]
            lows.append((low0, low1, low2))
        put_rows(r0_ref, q, row_pairs(t_ref, lows[0][0], True))
        put_rows(r1_ref, q, row_pairs(t_ref, lows[0][1] + lows[1][1], False))
        put_rows(r2_ref, q, row_pairs(t_ref, lows[0][2] + lows[1][2], True))
        return carry

    lax.fori_loop(0, 16, diagonals, 0)

    def leftovers(q, carry):
        total = jnp.zeros((40, 256), F32)
        for i in range(2):
            p = 2 * q + i
            total += KEEP * s_ref[p] + neighbours(sm_ref, f0_ref, f1_ref, f2_ref, p)
        put_rows(rs_ref, q, row_pairs(t_ref, total, True))
        return carry

    lax.fori_loop(1, 15, leftovers, 0)

    pairs = one_hot(256, 128, lambda r, c: lax.shift_right_logical(r, 1) == c, 0.25)
    evens = one_hot(256, 128, lambda r, c: r == 2 * c, 0.25)
    l10_ref[pl.ds(0, 16)] = spread(r0_ref[...].reshape(384, 256), pairs).reshape(16, 24, 128)
    l11_ref[...] = spread(r1_ref[...].reshape(384, 256), pairs).reshape(16, 24, 128)
    l12_ref[...] = spread(r2_ref[...].reshape(384, 256), evens).reshape(16, 24, 128)
    s1_ref[...] = 2.0 * spread(rs_ref[...].reshape(384, 256), pairs).reshape(16, 24, 128)
    l10_ref[16] = jnp.zeros((24, 128), F32)

    first_row_1 = (iota((24, 128), 0) == 6) & at_y
    first_lane_1 = (iota((24, 128), 1) == 0) & at_z

    def faces_1(p, carry):
        f10_ref[p] = jnp.where((p == 6) & at_x, 0.0, l10_ref[p])
        f11_ref[p] = jnp.where(first_row_1, 0.0, l11_ref[p])
        f12_ref[p] = jnp.where(first_lane_1, 0.0, l12_ref[p])
        return carry

    lax.fori_loop(0, 16, faces_1, 0)
    f10_ref[16] = jnp.zeros((24, 128), F32)

    def diagonals_1(p, carry):
        d = (
            4.0 * ABSORB + l10_ref[p] + f10_ref[p + 1]
            + l11_ref[p] + turn(f11_ref[p], -1, 0)
            + l12_ref[p] + turn(f12_ref[p], -1, 1)
        )
        w = RELAX / d
        w1_ref[p] = w
        sm1_ref[p] = w * s1_ref[p]
        return carry

    lax.fori_loop(0, 16, diagonals_1, 0)

    def quad(values, both):
        t1_ref[...] = values
        first = t1_ref[pl.ds(6, 4, 2), :]
        return first + t1_ref[pl.ds(7, 4, 2), :] if both else first

    def leftover_1(p):
        return KEEP * s1_ref[p] + neighbours(sm1_ref, f10_ref, f11_ref, f12_ref, p)

    total = jnp.zeros((8, 128), F32)
    for f in range(4):
        for i in range(2):
            p = 6 + 2 * i
            if f == 0:
                part = quad(leftover_1(p) + leftover_1(p + 1), True)
            elif f == 1:
                part = quad(l10_ref[p], True)
            elif f == 2:
                part = quad(l11_ref[p] + l11_ref[p + 1], False)
            else:
                part = quad(l12_ref[p] + l12_ref[p + 1], True)
            u_ref[pl.ds(4 * i, 4), :] = part
        place = one_hot(
            128, 128,
            lambda r, c, f=f: (
                ((lax.shift_right_logical(r, 1) + 32 * f == c) if f < 3 else (r + 192 == 2 * c))
                & (r < 64)
            ),
            0.5 if f == 0 else 0.25,
        )
        total += spread(u_ref[...], place)
    pay_ref[...] = total


def solve_2(s2, level_2, level_3, t3_ref, e_ref):
    f0, f1, f2, w = level_2
    g0, g1, g2, w3 = level_3
    nx, ny, _ = s2.shape
    sm = w * s2
    left = KEEP * s2 + neighbours_3d(sm, f0, f1, f2)
    s3 = coarse_2(left.reshape(nx // 2, 2, ny, 128).sum(1), t3_ref, True, 0.5, False)
    e = w3 * s3
    for _ in range(SWEEPS - 1):
        e = KEEP * e + w3 * (s3 + neighbours_3d(e, g0, g1, g2))
    widen = one_hot(128, 128, lambda r, c: (r == lax.shift_right_logical(c, 1)) & (c < 64))
    wide = spread(e.reshape(nx * ny // 4, 128), widen).reshape(nx // 2, ny // 2, 128)
    for x in range(nx // 2):
        for i in range(2):
            e_ref[x, pl.ds(i, ny // 2, 2), :] = wide[x]
    e2 = e_ref[...]
    corrected = sm + jnp.concatenate([e2[:, None], e2[:, None]], 1).reshape(nx, ny, 128)
    return KEEP * corrected + w * (s2 + neighbours_3d(corrected, f0, f1, f2))


def coarse_2(values, t3_ref, both, weight, even):
    nx, ny, _ = values.shape
    t3_ref[...] = values
    first = t3_ref[:, pl.ds(0, ny // 2, 2), :]
    if both:
        first = first + t3_ref[:, pl.ds(1, ny // 2, 2), :]
    if even:
        rule = lambda r, c: (r == 2 * c) & (r < 64)
    else:
        rule = lambda r, c: (lax.shift_right_logical(r, 1) == c) & (r < 64)
    flat = spread(first.reshape(nx * ny // 2, 128), one_hot(128, 128, rule, weight))
    return flat.reshape(nx, ny // 2, 128)


def coefficients(low, mask_lane, absorb):
    shape = low[0].shape
    f0 = jnp.where(iota(shape, 0) == 0, 0.0, low[0])
    f1 = jnp.where(iota(shape, 1) == 0, 0.0, low[1])
    f2 = jnp.where((iota(shape, 2) == mask_lane) & (lax.axis_index("gz") == 0), 0.0, low[2])
    d = (
        absorb + low[0] + jnp.concatenate([f0[1:], jnp.zeros_like(f0[:1])], 0)
        + low[1] + turn(f1, -1, 1) + low[2] + turn(f2, -1, 2)
    )
    return f0, f1, f2, RELAX / d


def fetch_level_2(m2_ref, planes, pick_ref):
    gx, gy = lax.axis_index("gx"), lax.axis_index("gy")
    ny = m2_ref.shape[1]

    def source(c):
        return jnp.where(c < 96, 16, -48) + lax.shift_right_logical(c, 1)

    widen = one_hot(128, 128, lambda r, c: r == source(c))
    rows = one_hot(24, ny, lambda r, c: c == 4 * gy - 3 + lax.shift_right_logical(r, 1))
    for k in planes:
        pick_ref[k] = spread(pick(rows, m2_ref[2 * gx + k]), widen)


def widen_level_1(m1_ref, wide_ref, lo, hi):
    rows = 24 * (hi - lo)
    widen = one_hot(128, 256, lambda r, c: r == lax.shift_right_logical(c, 1))
    wide_ref[pl.ds(lo, hi - lo)] = spread(m1_ref[pl.ds(lo, hi - lo)].reshape(rows, 128), widen).reshape(
        hi - lo, 24, 256
    )


def double_rows(t_ref, wide_ref, q):
    for half in range(2):
        part = wide_ref[q, pl.ds(0, 20), pl.ds(128 * half, 128)]
        for i in range(2):
            t_ref[half, pl.ds(i, 20, 2), :] = part
    return jnp.concatenate([t_ref[0], t_ref[1]], 1)


def second_kernel(
    s_ref, f0_ref, f1_ref, f2_ref, w_ref, d_ref,
    s1_ref, f10_ref, f11_ref, f12_ref, w1_ref,
    own_ref, before_ref, after_ref,
    fp_out, im_out, im_ref, t1s_ref, f20_ref, f21_ref, f22_ref, w2_ref,
    f30_ref, f31_ref, f32_ref, w3_ref, pay_ref,
    v_ref, t3_ref, e_ref, m2_ref, pick_ref, corr1_ref, m1_ref, wide_ref, t_ref,
    corr_ref, fp_ref, sm_ref, rs_ref, sm1_ref, tq_ref,
):
    nx2, ny2 = f20_ref.shape[:2]
    lane8 = iota((8, 128), 1)
    row8 = iota((8, 128), 0)

    def assemble(x, carry):
        for pair in range(ny2 // 8):
            for f in range(4):
                tiles = []
                for j in range(2):
                    g = x * (ny2 // 4) + 2 * pair + j
                    t = jnp.where(
                        lane8 < 16,
                        turn(before_ref[g], -(32 * f + 16), 1),
                        jnp.where(
                            lane8 < 48,
                            turn(own_ref[g], 16 - 32 * f, 1),
                            turn(after_ref[g], 48 - 32 * f, 1),
                        ),
                    )
                    tiles.append(jnp.where(lane8 < 64, t, 0.0))
                rows = pl.ds(8 * pair, 8)
                v_ref[f, 2 * x, rows, :] = jnp.where(row8 < 4, tiles[0], turn(tiles[1], 4, 0))
                v_ref[f, 2 * x + 1, rows, :] = jnp.where(row8 < 4, turn(tiles[0], 4, 0), tiles[1])
        return carry

    lax.fori_loop(0, nx2 // 2, assemble, 0)

    s2 = v_ref[0]
    low = (v_ref[1], v_ref[2], v_ref[3])
    level_2 = coefficients(low, 16, 16.0 * ABSORB)
    f20_ref[...], f21_ref[...], f22_ref[...], w2_ref[...] = level_2
    halves = [t.reshape(nx2 // 2, 2, ny2, 128) for t in low]
    low_3 = (
        coarse_2(halves[0][:, 0], t3_ref, True, 0.25, False),
        coarse_2(halves[1].sum(1), t3_ref, False, 0.25, False),
        coarse_2(halves[2].sum(1), t3_ref, True, 0.25, True),
    )
    level_3 = coefficients(low_3, 8, 64.0 * ABSORB)
    f30_ref[...], f31_ref[...], f32_ref[...], w3_ref[...] = level_3
    m2_ref[...] = jnp.zeros_like(m2_ref)
    m2_ref[pl.ds(3, nx2)] = solve_2(s2, level_2, level_3, t3_ref, e_ref)
    fetch_level_2(m2_ref, range(8), pick_ref)

    def correct_1(p, carry):
        corr1_ref[p] = w1_ref[p] * s1_ref[p] + pick_ref[lax.shift_right_logical(p, 1)]
        return carry

    lax.fori_loop(0, 16, correct_1, 0)

    def relax_1(p, carry):
        m1_ref[p] = KEEP * corr1_ref[p] + w1_ref[p] * (
            s1_ref[p] + neighbours(corr1_ref, f10_ref, f11_ref, f12_ref, p)
        )
        return carry

    lax.fori_loop(2, 14, relax_1, 0)
    widen_level_1(m1_ref, wide_ref, 2, 14)

    def correct(q, carry):
        e = double_rows(t_ref, wide_ref, q)
        for i in range(2):
            p = 2 * q + i
            corr_ref[p] = w_ref[p] * s_ref[p] + e
        return carry

    lax.fori_loop(2, 14, correct, 0)

    def relax(p, carry):
        fp_ref[p] = KEEP * corr_ref[p] + w_ref[p] * (
            s_ref[p] + neighbours(corr_ref, f0_ref, f1_ref, f2_ref, p)
        )
        return carry

    lax.fori_loop(6, 26, relax, 0)

    def image(p, carry):
        im = d_ref[p] * fp_ref[p] - neighbours(fp_ref, f0_ref, f1_ref, f2_ref, p)
        im_ref[p] = im
        sm_ref[p] = w_ref[p] * im
        return carry

    lax.fori_loop(7, 25, image, 0)

    rs_ref[...] = jnp.zeros_like(rs_ref)
    inside = (iota((40, 128), 0) >= 12) & (iota((40, 128), 0) < 28)

    def leftovers(q, sums):
        total = jnp.zeros((40, 256), F32)
        for i in range(2):
            p = 2 * q + i
            left = KEEP * im_ref[p] + neighbours(sm_ref, f0_ref, f1_ref, f2_ref, p)
            total += left
            own = jnp.where(inside & (p >= 12) & (p < 20), 1.0, 0.0)
            fp, im = fp_ref[p, :, 0:128], im_ref[p, :, 0:128]
            sums = (
                sums[0] + own * s_ref[p, :, 0:128] * fp,
                sums[1] + own * fp * im,
                sums[2] + own * sm_ref[p, :, 0:128] * (im + left[:, 0:128]),
            )
        put_rows(rs_ref, q - 4, row_pairs(t_ref, total, True))
        return sums

    zero = jnp.zeros((40, 128), F32)
    sums = lax.fori_loop(4, 12, leftovers, (zero, zero, zero))

    for p in range(8):
        fp_out[p] = fp_ref[12 + p, pl.ds(12, 16), 0:128]
        im_out[p] = im_ref[12 + p, pl.ds(12, 16), 0:128]

    pairs = one_hot(256, 128, lambda r, c: lax.shift_right_logical(r, 1) == c, 0.5)
    t1s_ref[...] = jnp.zeros_like(t1s_ref)
    t1s_ref[pl.ds(4, 8)] = spread(rs_ref[...].reshape(192, 256), pairs).reshape(8, 24, 128)
    for p in range(5, 11):
        sm1_ref[p] = w1_ref[p] * t1s_ref[p]
    inside_1 = jnp.where(
        (iota((24, 128), 0) >= 6) & (iota((24, 128), 0) < 14) & (iota((24, 128), 1) < 64), 1.0, 0.0
    )
    second = jnp.zeros((24, 128), F32)
    pay = jnp.zeros((8, 128), F32)
    tq_ref[...] = jnp.zeros_like(tq_ref)
    for i in range(2):
        total = jnp.zeros((24, 128), F32)
        for j in range(2):
            p = 6 + 2 * i + j
            s1 = t1s_ref[p]
            left = KEEP * s1 + neighbours(sm1_ref, f10_ref, f11_ref, f12_ref, p)
            second += inside_1 * sm1_ref[p] * (s1 + left)
            total += left
        tq_ref[pl.ds(0, 24), :] = total
        tq_ref[pl.ds(24, 4), :] = tq_ref[pl.ds(6, 4, 2), :] + tq_ref[pl.ds(7, 4, 2), :]
        place = one_hot(
            128, 128,
            lambda r, c, i=i: (lax.shift_right_logical(r, 1) + 32 * i == c) & (r < 64), 0.5,
        )
        pay += spread(tq_ref[pl.ds(24, 8), :], place)
    scalars = (jnp.sum(sums[0]), jnp.sum(sums[1]), jnp.sum(sums[2]) + 2.0 * jnp.sum(second))
    for k, value in enumerate(scalars):
        pay = jnp.where((lane8 == 64 + k) & (row8 == 0), value, pay)
    pay_ref[...] = pay[:4]


def third_kernel(
    f0_ref, f1_ref, f2_ref, w_ref, f10_ref, f11_ref, f12_ref, w1_ref,
    im_ref, t1s_ref, f20_ref, f21_ref, f22_ref, w2_ref, f30_ref, f31_ref, f32_ref, w3_ref,
    own_ref, before_ref, after_ref,
    mi_out, scalar_out,
    v_ref, t3_ref, e_ref, m2_ref, pick_ref, corr1_ref, m1_ref, wide_ref, t_ref, corr_ref,
):
    nx2, ny2 = f20_ref.shape[:2]
    lane8 = iota((8, 128), 1)

    def assemble(x, acc):
        for pair in range(ny2 // 8):
            g = x * (ny2 // 8) + pair
            acc = acc + own_ref[g]
            for i in range(2):
                t = jnp.where(
                    lane8 < 16,
                    turn(before_ref[g], -(32 * i + 16), 1),
                    jnp.where(
                        lane8 < 48,
                        turn(own_ref[g], 16 - 32 * i, 1),
                        turn(after_ref[g], 48 - 32 * i, 1),
                    ),
                )
                v_ref[2 * x + i, pl.ds(8 * pair, 8), :] = jnp.where(lane8 < 64, t, 0.0)
        return acc

    acc = lax.fori_loop(0, nx2 // 2, assemble, jnp.zeros((8, 128), F32))
    s2 = v_ref[...]
    level_2 = (f20_ref[...], f21_ref[...], f22_ref[...], w2_ref[...])
    level_3 = (f30_ref[...], f31_ref[...], f32_ref[...], w3_ref[...])
    m2 = solve_2(s2, level_2, level_3, t3_ref, e_ref)
    lane3 = iota(s2.shape, 2)
    part = 4.0 * jnp.sum(jnp.where((lane3 >= 16) & (lane3 < 48), s2 * m2, 0.0))
    sums = jnp.sum(acc, axis=0, keepdims=True)
    scalar_out[...] = jnp.where(iota((1, 128), 1) == 67, part, sums)
    m2_ref[...] = jnp.zeros_like(m2_ref)
    m2_ref[pl.ds(3, nx2)] = m2
    fetch_level_2(m2_ref, range(2, 6), pick_ref)
    for p in range(4, 12):
        corr1_ref[p] = w1_ref[p] * t1s_ref[p] + pick_ref[p // 2]
    for p in range(5, 11):
        m1_ref[p] = KEEP * corr1_ref[p] + w1_ref[p] * (
            t1s_ref[p] + neighbours(corr1_ref, f10_ref, f11_ref, f12_ref, p)
        )
    widen_level_1(m1_ref, wide_ref, 5, 11)

    def correct(q, carry):
        e = double_rows(t_ref, wide_ref, q)
        for i in range(2):
            p = 2 * q + i
            corr_ref[p] = w_ref[p] * im_ref[p] + e
        return carry

    lax.fori_loop(5, 11, correct, 0)

    def relax(p, carry):
        corr_ref[p - 4] = KEEP * corr_ref[p] + w_ref[p] * (
            im_ref[p] + neighbours(corr_ref, f0_ref, f1_ref, f2_ref, p)
        )
        return carry

    for p in range(8):
        q = 12 + p
        mi = KEEP * corr_ref[q] + w_ref[q] * (
            im_ref[q] + neighbours(corr_ref, f0_ref, f1_ref, f2_ref, q)
        )
        corr_ref[p] = mi
        mi_out[p] = corr_ref[p, pl.ds(12, 16), 0:128]


def last_kernel(sums_ref, s_ref, fp_ref, im_ref, mi_ref, solution_ref, residual_ref, direction_ref):
    total = jnp.sum(sums_ref[...], axis=0)
    lane = iota((1, 128), 1)

    def value(lanes):
        keep = lane == lanes[0]
        for k in lanes[1:]:
            keep = keep | (lane == k)
        return jnp.sum(jnp.where(keep, total, 0.0), axis=1, keepdims=True)

    projected, curvature, product = value((64,)), value((65,)), value((66, 67))
    step = projected / curvature
    share = product / curvature
    for p in range(8):
        fp = fp_ref[p]
        solution_ref[p] = step * fp
        residual_ref[p] = s_ref[p] - step * im_ref[p]
        direction_ref[p] = step * (share * fp - mi_ref[p])


def call(kernel, inputs, outs, scratch=(), keep_in=(), keep_out=()):
    vmem = pl.BlockSpec(memory_space=pltpu.VMEM)
    inputs = [
        pltpu.with_memory_space_constraint(value, pltpu.VMEM) if i in keep_in else value
        for i, value in enumerate(inputs)
    ]
    shapes = [
        pltpu.VMEM(shape, dtype) if i in keep_out else jax.ShapeDtypeStruct(shape, dtype)
        for i, (shape, dtype) in enumerate(outs)
    ]
    return pl.pallas_call(
        kernel,
        out_shape=shapes,
        in_specs=[vmem] * len(inputs),
        out_specs=[vmem] * len(outs),
        scratch_shapes=[pltpu.VMEM(shape, F32) for shape in scratch],
        compiler_params=pltpu.CompilerParams(vmem_limit_bytes=VMEM_LIMIT),
    )(*inputs)


def shift_along(value, axis, by):
    size = lax.axis_size(axis)
    return lax.ppermute(value, axis, [(i, i + by) for i in range(size) if 0 <= i + by < size])


def gather_plane(value):
    peers = lax.axis_size(("gx", "gy"))
    copies = jnp.broadcast_to(value[None], (peers,) + value.shape)
    return lax.all_to_all(copies, ("gx", "gy"), 0, 0, tiled=True)


def local(right_side, face_coefficients, solid):
    nx2, ny2 = 2 * lax.axis_size("gx"), 4 * lax.axis_size("gy")
    (own,) = call(
        prepare_kernel, [right_side, face_coefficients, solid], [((8, 5, 16, 128), BF16)]
    )
    before, after = shift_along(own, "gz", 1), shift_along(own, "gz", -1)
    (own,) = call(rim_kernel, [own, before, after], [((8, 6, 16, 128), BF16)])
    block = jnp.concatenate(
        [
            shift_along(own[4:], "gx", 2),
            shift_along(own, "gx", 1),
            own,
            shift_along(own, "gx", -1),
            shift_along(own[:4], "gx", -2),
        ],
        axis=0,
    )
    before, after = shift_along(block, "gy", 1), shift_along(block, "gy", -1)

    fine, fine_up = (32, 40, 256), (33, 40, 256)
    mid, mid_up = (16, 24, 128), (17, 24, 128)
    rows = (16, 24, 256)
    *state, pay = call(
        first_kernel,
        [block, before, after],
        [(shape, F32) for shape in (fine, fine_up, fine, fine, fine, fine, mid, mid_up, mid, mid, mid, (8, 128))],
        [fine, fine, fine, fine, (2, 40, 128), rows, rows, rows, rows, mid_up, mid, mid, mid, (24, 128), (8, 128)],
        keep_out=range(11),
    )
    own = gather_plane(pay)
    before, after = shift_along(own, "gz", 1), shift_along(own, "gz", -1)
    level_2, level_3 = (nx2, ny2, 128), (nx2 // 2, ny2 // 2, 128)
    window = (nx2 + 6, ny2, 128)
    half = (nx2 // 2, ny2, 128)
    first_pre, image, *more, pay = call(
        second_kernel,
        [*state, own, before, after],
        [((8, 16, 128), F32)] * 2
        + [(shape, F32) for shape in (fine, mid, *[level_2] * 4, *[level_3] * 4, (4, 128))],
        [(4,) + level_2, half, half, window, (8, 24, 128), mid, mid, rows, (2, 40, 128),
         fine, fine, fine, (8, 24, 256), mid, (32, 128)],
        keep_in=range(11),
        keep_out=range(2, 12),
    )
    own = gather_plane(pay).reshape(nx2 * ny2 // 16, 8, 128)
    before, after = shift_along(own, "gz", 1), shift_along(own, "gz", -1)
    _, f0, f1, f2, w, _, _, f10, f11, f12, w1 = state
    mapped, sums = call(
        third_kernel,
        [f0, f1, f2, w, f10, f11, f12, w1, *more, own, before, after],
        [((8, 16, 128), F32), ((1, 128), F32)],
        [level_2, half, half, window, (8, 24, 128), mid, mid, rows, (2, 40, 128), fine],
        keep_in=range(18),
    )
    peers = lax.axis_size("gz")
    sums = lax.all_to_all(jnp.broadcast_to(sums[None], (peers, 1, 128)), "gz", 0, 0, tiled=True)
    return tuple(
        call(
            last_kernel,
            [sums, right_side, first_pre, image, mapped],
            [((8, 16, 128), F32)] * 3,
        )
    )


def solution(mesh):
    placed = P("gx", "gy", "gz")
    return jax.shard_map(
        local,
        mesh=mesh,
        in_specs=(placed, P(None, "gx", "gy", "gz"), placed),
        out_specs=(placed, placed, placed),
        check_vma=False,
    )
```

```python
import functools

import jax
import jax.numpy as jnp
from jax import lax
from jax.experimental import pallas as pl
from jax.experimental.pallas import tpu as pltpu
from jax.sharding import PartitionSpec as P

F32 = jnp.float32
BF16 = jnp.bfloat16
ABSORB = 0.001
RELAX = 0.8
KEEP = 0.2
SWEEPS = 6
VMEM_LIMIT = 24 * 1024 * 1024


def one_hot(rows, cols, rule, weight=1.0):
    r = lax.broadcasted_iota(jnp.int32, (rows, cols), 0)
    c = lax.broadcasted_iota(jnp.int32, (rows, cols), 1)
    return jnp.where(rule(r, c), weight, 0.0).astype(BF16)


def spread(values, matrix):
    high = values.astype(BF16)
    low = (values - high.astype(F32)).astype(BF16)
    return jnp.dot(high, matrix, preferred_element_type=F32) + jnp.dot(
        low, matrix, preferred_element_type=F32
    )


def pick(matrix, values):
    high = values.astype(BF16)
    low = (values - high.astype(F32)).astype(BF16)
    return jnp.dot(matrix, high, preferred_element_type=F32) + jnp.dot(
        matrix, low, preferred_element_type=F32
    )


def root(values):
    return values * lax.rsqrt(jnp.maximum(values, 1e-12))


def turn(values, shift, axis):
    return pltpu.roll(values, shift % values.shape[axis], axis)


def iota(shape, dim):
    return lax.broadcasted_iota(jnp.int32, shape, dim)


def plane_terms(v, f1, f2):
    return turn(v, 1, 0) * f1 + turn(v * f1, -1, 0) + turn(v, 1, 1) * f2 + turn(v * f2, -1, 1)


def neighbours(v_ref, f0_ref, f1_ref, f2_ref, p):
    return (
        f0_ref[p] * v_ref[p - 1]
        + f0_ref[p + 1] * v_ref[p + 1]
        + plane_terms(v_ref[p], f1_ref[p], f2_ref[p])
    )


def neighbours_3d(v, f0, f1, f2):
    zero = jnp.zeros_like(v[:1])
    up = f0 * v
    return (
        f0 * jnp.concatenate([zero, v[:-1]], 0)
        + jnp.concatenate([up[1:], zero], 0)
        + turn(v, 1, 1) * f1
        + turn(v * f1, -1, 1)
        + turn(v, 1, 2) * f2
        + turn(v * f2, -1, 2)
    )


def row_pairs(t_ref, values, both):
    out = []
    for half in range(2):
        t_ref[half] = values[:, 128 * half : 128 * half + 128]
        first = t_ref[half, pl.ds(0, 20, 2), :]
        out.append(first + t_ref[half, pl.ds(1, 20, 2), :] if both else first)
    return out


def put_rows(r_ref, q, halves):
    for half in range(2):
        r_ref[q, pl.ds(0, 20), pl.ds(128 * half, 128)] = halves[half]


def prepare_kernel(s_hbm, fc_hbm, solid_hbm, out_ref, s_ref, fc_ref, solid_ref, sems):
    copies = [
        pltpu.make_async_copy(source, target, sems.at[i])
        for i, (source, target) in enumerate(
            ((s_hbm, s_ref), (fc_hbm, fc_ref), (solid_hbm, solid_ref))
        )
    ]
    for copy in copies:
        copy.start()
    for copy in copies:
        copy.wait()
    s = s_ref[...]
    high = s.astype(BF16)
    out_ref[:, 0] = high
    out_ref[:, 1] = (s - high.astype(F32)).astype(BF16)
    weight = 1.0 - 0.75 * solid_ref[...].astype(F32)
    for a in range(3):
        out_ref[:, 2 + a] = (fc_ref[a].astype(F32) * weight).astype(BF16)


def rim_kernel(own_ref, before_ref, after_ref, out_ref):
    lane = iota((16, 128), 1)

    def body(p, carry):
        rim = jnp.zeros((16, 128), F32)
        for f in range(5):
            out_ref[p, f] = own_ref[p, f]
            t = jnp.where(lane < 64, after_ref[p, f].astype(F32), before_ref[p, f].astype(F32))
            t = turn(t, 24 * f + 12, 1)
            rim = jnp.where((lane >= 24 * f) & (lane < 24 * f + 24), t, rim)
        out_ref[p, 5] = rim.astype(BF16)
        return carry

    lax.fori_loop(0, 8, body, 0)


def first_kernel(
    x_ref, ym_ref, yp_ref,
    s_ref, f0_ref, f1_ref, f2_ref, w_ref, d_ref,
    s1_ref, f10_ref, f11_ref, f12_ref, w1_ref, up_ref, down_ref, pay_ref,
    c0_ref, c1_ref, c2_ref, sm_ref, t_ref, r0_ref, r1_ref, r2_ref, rs_ref,
    l10_ref, l11_ref, l12_ref, sm1_ref, t1_ref, u_ref,
):
    at_x = lax.axis_index("gx") == 0
    at_y = lax.axis_index("gy") == 0
    at_z = lax.axis_index("gz") == 0
    lane = iota((40, 128), 1)
    side = (lane < 12) | (lane >= 116)

    def unpack(p, carry):
        tiles = []
        for f in range(6):
            column = jnp.concatenate(
                [ym_ref[p, f].astype(F32), x_ref[p, f].astype(F32), yp_ref[p, f].astype(F32)], 0
            )
            tiles.append(turn(column, -4, 0)[:40])
        rims = [
            jnp.where(side, turn(tiles[5], -(24 * f + 12), 1), 0.0) for f in range(5)
        ]
        s_ref[p, :, 0:128] = tiles[0] + tiles[1]
        s_ref[p, :, 128:256] = rims[0] + rims[1]
        for a, c_ref in enumerate((c0_ref, c1_ref, c2_ref)):
            c_ref[p, :, 0:128] = tiles[2 + a]
            c_ref[p, :, 128:256] = rims[2 + a]
        return carry

    lax.fori_loop(0, 24, unpack, 0)

    def faces(p, carry):
        before = jnp.maximum(p - 1, 0)
        f0_ref[p] = root(c0_ref[p] * c0_ref[before])
        c1 = c1_ref[p]
        f1_ref[p] = root(c1 * turn(c1, 1, 0))
        c2 = c2_ref[p]
        f2_ref[p] = root(c2 * turn(c2, 1, 1))
        return carry

    lax.fori_loop(0, 24, faces, 0)
    f0_ref[24] = jnp.zeros((40, 256), F32)

    first_row = (iota((40, 256), 0) == 12) & at_y
    first_lane = (iota((40, 256), 1) == 0) & at_z
    for ref in (r0_ref, r1_ref, r2_ref, rs_ref):
        ref[...] = jnp.zeros_like(ref)

    def diagonals(q, carry):
        lows = []
        for i in range(2):
            p = 2 * q + i
            f0, f1, f2 = f0_ref[p], f1_ref[p], f2_ref[p]
            low0 = f0 + jnp.where((p == 8) & at_x, c0_ref[p], 0.0)
            low1 = f1 + jnp.where(first_row, c1_ref[p], 0.0)
            low2 = f2 + jnp.where(first_lane, c2_ref[p], 0.0)
            d = ABSORB + low0 + f0_ref[p + 1] + low1 + turn(f1, -1, 0) + low2 + turn(f2, -1, 1)
            w = RELAX / d
            d_ref[p] = d
            w_ref[p] = w
            sm_ref[p] = w * s_ref[p]
            lows.append((low0, low1, low2))
        put_rows(r0_ref, q, row_pairs(t_ref, lows[0][0], True))
        put_rows(r1_ref, q, row_pairs(t_ref, lows[0][1] + lows[1][1], False))
        put_rows(r2_ref, q, row_pairs(t_ref, lows[0][2] + lows[1][2], True))
        return carry

    lax.fori_loop(0, 12, diagonals, 0)

    def leftovers(q, carry):
        total = jnp.zeros((40, 256), F32)
        for i in range(2):
            p = 2 * q + i
            total += KEEP * s_ref[p] + neighbours(sm_ref, f0_ref, f1_ref, f2_ref, p)
        put_rows(rs_ref, q, row_pairs(t_ref, total, True))
        return carry

    lax.fori_loop(1, 11, leftovers, 0)

    pairs = one_hot(256, 128, lambda r, c: lax.shift_right_logical(r, 1) == c, 0.25)
    evens = one_hot(256, 128, lambda r, c: r == 2 * c, 0.25)
    for target, source, matrix in (
        (l10_ref, r0_ref, pairs), (l11_ref, r1_ref, pairs), (l12_ref, r2_ref, evens), (s1_ref, rs_ref, pairs)
    ):
        target[pl.ds(0, 2)] = jnp.zeros((2, 24, 128), F32)
        target[pl.ds(14, 2)] = jnp.zeros((2, 24, 128), F32)
        value = spread(source[...].reshape(288, 256), matrix).reshape(12, 24, 128)
        target[pl.ds(2, 12)] = 2.0 * value if target is s1_ref else value

    first_row_1 = (iota((24, 128), 0) == 6) & at_y
    first_lane_1 = (iota((24, 128), 1) == 0) & at_z

    def faces_1(p, carry):
        f10_ref[p] = jnp.where((p == 6) & at_x, 0.0, l10_ref[p])
        f11_ref[p] = jnp.where(first_row_1, 0.0, l11_ref[p])
        f12_ref[p] = jnp.where(first_lane_1, 0.0, l12_ref[p])
        return carry

    lax.fori_loop(0, 16, faces_1, 0)
    f10_ref[16] = jnp.zeros((24, 128), F32)

    def diagonals_1(p, carry):
        d = (
            4.0 * ABSORB + l10_ref[p] + f10_ref[p + 1]
            + l11_ref[p] + turn(f11_ref[p], -1, 0)
            + l12_ref[p] + turn(f12_ref[p], -1, 1)
        )
        w = RELAX / d
        w1_ref[p] = w
        sm1_ref[p] = w * s1_ref[p]
        return carry

    lax.fori_loop(2, 14, diagonals_1, 0)
    for i, ref in enumerate((s1_ref, w1_ref, f10_ref)):
        up_ref[pl.ds(2 * i, 2)] = ref[pl.ds(5, 2)]
        down_ref[pl.ds(2 * i, 2)] = ref[pl.ds(9, 2)]

    def quad(values, both):
        t1_ref[...] = values
        first = t1_ref[pl.ds(6, 4, 2), :]
        return first + t1_ref[pl.ds(7, 4, 2), :] if both else first

    def leftover_1(p):
        return KEEP * s1_ref[p] + neighbours(sm1_ref, f10_ref, f11_ref, f12_ref, p)

    total = jnp.zeros((8, 128), F32)
    for f in range(4):
        for i in range(2):
            p = 6 + 2 * i
            if f == 0:
                part = quad(leftover_1(p) + leftover_1(p + 1), True)
            elif f == 1:
                part = quad(l10_ref[p], True)
            elif f == 2:
                part = quad(l11_ref[p] + l11_ref[p + 1], False)
            else:
                part = quad(l12_ref[p] + l12_ref[p + 1], True)
            u_ref[pl.ds(4 * i, 4), :] = part
        place = one_hot(
            128, 128,
            lambda r, c, f=f: (
                ((lax.shift_right_logical(r, 1) + 32 * f == c) if f < 3 else (r + 192 == 2 * c))
                & (r < 64)
            ),
            0.5 if f == 0 else 0.25,
        )
        total += spread(u_ref[...], place)
    pay_ref[...] = total


def solve_2(s2, level_2, level_3, t3_ref, e_ref):
    f0, f1, f2, w = level_2
    g0, g1, g2, w3 = level_3
    nx, ny, _ = s2.shape
    sm = w * s2
    left = KEEP * s2 + neighbours_3d(sm, f0, f1, f2)
    s3 = coarse_2(left.reshape(nx // 2, 2, ny, 128).sum(1), t3_ref, True, 0.5, False)
    e = w3 * s3
    for _ in range(SWEEPS - 1):
        e = KEEP * e + w3 * (s3 + neighbours_3d(e, g0, g1, g2))
    widen = one_hot(128, 128, lambda r, c: (r == lax.shift_right_logical(c, 1)) & (c < 64))
    wide = spread(e.reshape(nx * ny // 4, 128), widen).reshape(nx // 2, ny // 2, 128)
    for x in range(nx // 2):
        for i in range(2):
            e_ref[x, pl.ds(i, ny // 2, 2), :] = wide[x]
    e2 = e_ref[...]
    corrected = sm + jnp.concatenate([e2[:, None], e2[:, None]], 1).reshape(nx, ny, 128)
    return KEEP * corrected + w * (s2 + neighbours_3d(corrected, f0, f1, f2))


def coarse_2(values, t3_ref, both, weight, even):
    nx, ny, _ = values.shape
    t3_ref[...] = values
    first = t3_ref[:, pl.ds(0, ny // 2, 2), :]
    if both:
        first = first + t3_ref[:, pl.ds(1, ny // 2, 2), :]
    if even:
        rule = lambda r, c: (r == 2 * c) & (r < 64)
    else:
        rule = lambda r, c: (lax.shift_right_logical(r, 1) == c) & (r < 64)
    flat = spread(first.reshape(nx * ny // 2, 128), one_hot(128, 128, rule, weight))
    return flat.reshape(nx, ny // 2, 128)


def coefficients(low, mask_lane, absorb):
    shape = low[0].shape
    f0 = jnp.where(iota(shape, 0) == 0, 0.0, low[0])
    f1 = jnp.where(iota(shape, 1) == 0, 0.0, low[1])
    f2 = jnp.where((iota(shape, 2) == mask_lane) & (lax.axis_index("gz") == 0), 0.0, low[2])
    d = (
        absorb + low[0] + jnp.concatenate([f0[1:], jnp.zeros_like(f0[:1])], 0)
        + low[1] + turn(f1, -1, 1) + low[2] + turn(f2, -1, 2)
    )
    return f0, f1, f2, RELAX / d


def fetch_level_2(m2_ref, planes, pick_ref):
    gx, gy = lax.axis_index("gx"), lax.axis_index("gy")
    ny = m2_ref.shape[1]

    def source(c):
        return jnp.where(c < 96, 16, -48) + lax.shift_right_logical(c, 1)

    widen = one_hot(128, 128, lambda r, c: r == source(c))
    rows = one_hot(24, ny, lambda r, c: c == 4 * gy - 3 + lax.shift_right_logical(r, 1))
    for k in planes:
        pick_ref[k] = spread(pick(rows, m2_ref[2 * gx + k]), widen)


def widen_level_1(m1_ref, wide_ref, lo, hi):
    rows = 24 * (hi - lo)
    widen = one_hot(128, 256, lambda r, c: r == lax.shift_right_logical(c, 1))
    wide_ref[pl.ds(lo, hi - lo)] = spread(m1_ref[pl.ds(lo, hi - lo)].reshape(rows, 128), widen).reshape(
        hi - lo, 24, 256
    )


def double_rows(t_ref, wide_ref, q):
    for half in range(2):
        part = wide_ref[q, pl.ds(0, 20), pl.ds(128 * half, 128)]
        for i in range(2):
            t_ref[half, pl.ds(i, 20, 2), :] = part
    return jnp.concatenate([t_ref[0], t_ref[1]], 1)


def second_kernel(
    s_ref, f0_ref, f1_ref, f2_ref, w_ref, d_ref,
    s1_ref, f10_ref, f11_ref, f12_ref, w1_ref,
    low_ref, high_ref, own_ref, before_ref, after_ref,
    fp_out, im_out, im_ref, t1s_ref, f20_ref, f21_ref, f22_ref, w2_ref,
    f30_ref, f31_ref, f32_ref, w3_ref, pay_ref,
    v_ref, t3_ref, e_ref, m2_ref, pick_ref, corr1_ref, m1_ref, wide_ref, t_ref,
    corr_ref, fp_ref, sm_ref, rs_ref, sm1_ref, tq_ref,
):
    nx2, ny2 = f20_ref.shape[:2]
    lane8 = iota((8, 128), 1)
    row8 = iota((8, 128), 0)

    def assemble(x, carry):
        for pair in range(ny2 // 8):
            for f in range(4):
                tiles = []
                for j in range(2):
                    g = x * (ny2 // 4) + 2 * pair + j
                    t = jnp.where(
                        lane8 < 16,
                        turn(before_ref[g], -(32 * f + 16), 1),
                        jnp.where(
                            lane8 < 48,
                            turn(own_ref[g], 16 - 32 * f, 1),
                            turn(after_ref[g], 48 - 32 * f, 1),
                        ),
                    )
                    tiles.append(jnp.where(lane8 < 64, t, 0.0))
                rows = pl.ds(8 * pair, 8)
                v_ref[f, 2 * x, rows, :] = jnp.where(row8 < 4, tiles[0], turn(tiles[1], 4, 0))
                v_ref[f, 2 * x + 1, rows, :] = jnp.where(row8 < 4, turn(tiles[0], 4, 0), tiles[1])
        return carry

    lax.fori_loop(0, nx2 // 2, assemble, 0)

    s2 = v_ref[0]
    low = (v_ref[1], v_ref[2], v_ref[3])
    level_2 = coefficients(low, 16, 16.0 * ABSORB)
    f20_ref[...], f21_ref[...], f22_ref[...], w2_ref[...] = level_2
    halves = [t.reshape(nx2 // 2, 2, ny2, 128) for t in low]
    low_3 = (
        coarse_2(halves[0][:, 0], t3_ref, True, 0.25, False),
        coarse_2(halves[1].sum(1), t3_ref, False, 0.25, False),
        coarse_2(halves[2].sum(1), t3_ref, True, 0.25, True),
    )
    level_3 = coefficients(low_3, 8, 64.0 * ABSORB)
    f30_ref[...], f31_ref[...], f32_ref[...], w3_ref[...] = level_3
    m2_ref[...] = jnp.zeros_like(m2_ref)
    m2_ref[pl.ds(3, nx2)] = solve_2(s2, level_2, level_3, t3_ref, e_ref)
    fetch_level_2(m2_ref, range(8), pick_ref)

    def correct_1(p, carry):
        corr1_ref[p] = w1_ref[p] * s1_ref[p] + pick_ref[lax.shift_right_logical(p, 1)]
        return carry

    lax.fori_loop(3, 13, correct_1, 0)
    for k in range(2):
        corr1_ref[1 + k] = low_ref[2 + k] * low_ref[k] + pick_ref[(1 + k) // 2]
        corr1_ref[13 + k] = high_ref[2 + k] * high_ref[k] + pick_ref[(13 + k) // 2]

    def relax_1(p, carry):
        m1_ref[p] = KEEP * corr1_ref[p] + w1_ref[p] * (
            s1_ref[p] + neighbours(corr1_ref, f10_ref, f11_ref, f12_ref, p)
        )
        return carry

    lax.fori_loop(3, 13, relax_1, 0)
    for p, source, w, face, next_face in (
        (2, low_ref[1], low_ref[3], low_ref[5], f10_ref[3]),
        (13, high_ref[0], high_ref[2], f10_ref[13], high_ref[5]),
    ):
        m1_ref[p] = KEEP * corr1_ref[p] + w * (
            source + face * corr1_ref[p - 1] + next_face * corr1_ref[p + 1]
            + plane_terms(corr1_ref[p], f11_ref[p], f12_ref[p])
        )
    widen_level_1(m1_ref, wide_ref, 2, 14)

    def correct(q, carry):
        e = double_rows(t_ref, wide_ref, q)
        for i in range(2):
            p = 2 * q + i - 4
            corr_ref[p] = w_ref[p] * s_ref[p] + e
        return carry

    lax.fori_loop(2, 14, correct, 0)

    def relax(p, carry):
        fp_ref[p] = KEEP * corr_ref[p] + w_ref[p] * (
            s_ref[p] + neighbours(corr_ref, f0_ref, f1_ref, f2_ref, p)
        )
        return carry

    lax.fori_loop(2, 22, relax, 0)

    def image(p, carry):
        im = d_ref[p] * fp_ref[p] - neighbours(fp_ref, f0_ref, f1_ref, f2_ref, p)
        im_ref[p] = im
        sm_ref[p] = w_ref[p] * im
        return carry

    lax.fori_loop(3, 21, image, 0)

    rs_ref[...] = jnp.zeros_like(rs_ref)
    inside = (iota((40, 128), 0) >= 12) & (iota((40, 128), 0) < 28)

    def leftovers(q, sums):
        total = jnp.zeros((40, 256), F32)
        for i in range(2):
            p = 2 * q + i - 4
            left = KEEP * im_ref[p] + neighbours(sm_ref, f0_ref, f1_ref, f2_ref, p)
            total += left
            own = jnp.where(inside & (p >= 8) & (p < 16), 1.0, 0.0)
            fp, im = fp_ref[p, :, 0:128], im_ref[p, :, 0:128]
            sums = (
                sums[0] + own * s_ref[p, :, 0:128] * fp,
                sums[1] + own * fp * im,
                sums[2] + own * sm_ref[p, :, 0:128] * (im + left[:, 0:128]),
            )
        put_rows(rs_ref, q - 4, row_pairs(t_ref, total, True))
        return sums

    zero = jnp.zeros((40, 128), F32)
    sums = lax.fori_loop(4, 12, leftovers, (zero, zero, zero))

    for p in range(8):
        fp_out[p] = fp_ref[8 + p, pl.ds(12, 16), 0:128]
        im_out[p] = im_ref[8 + p, pl.ds(12, 16), 0:128]

    pairs = one_hot(256, 128, lambda r, c: lax.shift_right_logical(r, 1) == c, 0.5)
    t1s_ref[...] = jnp.zeros_like(t1s_ref)
    t1s_ref[pl.ds(4, 8)] = spread(rs_ref[...].reshape(192, 256), pairs).reshape(8, 24, 128)
    for p in range(5, 11):
        sm1_ref[p] = w1_ref[p] * t1s_ref[p]
    inside_1 = jnp.where(
        (iota((24, 128), 0) >= 6) & (iota((24, 128), 0) < 14) & (iota((24, 128), 1) < 64), 1.0, 0.0
    )
    second = jnp.zeros((24, 128), F32)
    pay = jnp.zeros((8, 128), F32)
    tq_ref[...] = jnp.zeros_like(tq_ref)
    for i in range(2):
        total = jnp.zeros((24, 128), F32)
        for j in range(2):
            p = 6 + 2 * i + j
            s1 = t1s_ref[p]
            left = KEEP * s1 + neighbours(sm1_ref, f10_ref, f11_ref, f12_ref, p)
            second += inside_1 * sm1_ref[p] * (s1 + left)
            total += left
        tq_ref[pl.ds(0, 24), :] = total
        tq_ref[pl.ds(24, 4), :] = tq_ref[pl.ds(6, 4, 2), :] + tq_ref[pl.ds(7, 4, 2), :]
        place = one_hot(
            128, 128,
            lambda r, c, i=i: (lax.shift_right_logical(r, 1) + 32 * i == c) & (r < 64), 0.5,
        )
        pay += spread(tq_ref[pl.ds(24, 8), :], place)
    scalars = (jnp.sum(sums[0]), jnp.sum(sums[1]), jnp.sum(sums[2]) + 2.0 * jnp.sum(second))
    for k, value in enumerate(scalars):
        pay = jnp.where((lane8 == 64 + k) & (row8 == 0), value, pay)
    pay_ref[...] = pay[:4]


def third_kernel(
    f0_ref, f1_ref, f2_ref, w_ref, f10_ref, f11_ref, f12_ref, w1_ref,
    im_ref, t1s_ref, f20_ref, f21_ref, f22_ref, w2_ref, f30_ref, f31_ref, f32_ref, w3_ref,
    own_ref, before_ref, after_ref,
    mi_out, scalar_out,
    v_ref, t3_ref, e_ref, m2_ref, pick_ref, corr1_ref, m1_ref, wide_ref, t_ref, corr_ref,
):
    nx2, ny2 = f20_ref.shape[:2]
    lane8 = iota((8, 128), 1)

    def assemble(x, acc):
        for pair in range(ny2 // 8):
            g = x * (ny2 // 8) + pair
            acc = acc + own_ref[g]
            for i in range(2):
                t = jnp.where(
                    lane8 < 16,
                    turn(before_ref[g], -(32 * i + 16), 1),
                    jnp.where(
                        lane8 < 48,
                        turn(own_ref[g], 16 - 32 * i, 1),
                        turn(after_ref[g], 48 - 32 * i, 1),
                    ),
                )
                v_ref[2 * x + i, pl.ds(8 * pair, 8), :] = jnp.where(lane8 < 64, t, 0.0)
        return acc

    acc = lax.fori_loop(0, nx2 // 2, assemble, jnp.zeros((8, 128), F32))
    s2 = v_ref[...]
    level_2 = (f20_ref[...], f21_ref[...], f22_ref[...], w2_ref[...])
    level_3 = (f30_ref[...], f31_ref[...], f32_ref[...], w3_ref[...])
    m2 = solve_2(s2, level_2, level_3, t3_ref, e_ref)
    lane3 = iota(s2.shape, 2)
    part = 4.0 * jnp.sum(jnp.where((lane3 >= 16) & (lane3 < 48), s2 * m2, 0.0))
    sums = jnp.sum(acc, axis=0, keepdims=True)
    scalar_out[...] = jnp.where(iota((1, 128), 1) == 67, part, sums)
    m2_ref[...] = jnp.zeros_like(m2_ref)
    m2_ref[pl.ds(3, nx2)] = m2
    fetch_level_2(m2_ref, range(2, 6), pick_ref)
    for p in range(4, 12):
        corr1_ref[p] = w1_ref[p] * t1s_ref[p] + pick_ref[p // 2]
    for p in range(5, 11):
        m1_ref[p] = KEEP * corr1_ref[p] + w1_ref[p] * (
            t1s_ref[p] + neighbours(corr1_ref, f10_ref, f11_ref, f12_ref, p)
        )
    widen_level_1(m1_ref, wide_ref, 5, 11)

    def correct(q, carry):
        e = double_rows(t_ref, wide_ref, q)
        for i in range(2):
            p = 2 * q + i - 4
            corr_ref[p] = w_ref[p] * im_ref[p] + e
        return carry

    lax.fori_loop(5, 11, correct, 0)

    for p in range(8):
        q = 8 + p
        mi = KEEP * corr_ref[q] + w_ref[q] * (
            im_ref[q] + neighbours(corr_ref, f0_ref, f1_ref, f2_ref, q)
        )
        t_ref[0] = mi[:, 0:128]
        mi_out[p] = t_ref[0, pl.ds(12, 16), :]


def last_kernel(sums_ref, s_ref, fp_ref, im_ref, mi_ref, solution_ref, residual_ref, direction_ref):
    total = jnp.sum(sums_ref[...], axis=0)
    lane = iota((1, 128), 1)

    def value(lanes):
        keep = lane == lanes[0]
        for k in lanes[1:]:
            keep = keep | (lane == k)
        return jnp.sum(jnp.where(keep, total, 0.0), axis=1, keepdims=True)

    projected, curvature, product = value((64,)), value((65,)), value((66, 67))
    step = projected / curvature
    share = product / curvature
    for p in range(8):
        fp = fp_ref[p]
        solution_ref[p] = step * fp
        residual_ref[p] = s_ref[p] - step * im_ref[p]
        direction_ref[p] = step * (share * fp - mi_ref[p])


def call(kernel, inputs, outs, scratch=(), keep_in=(), keep_out=(), space=pltpu.VMEM):
    vmem = pl.BlockSpec(memory_space=pltpu.VMEM)
    inputs = [
        pltpu.with_memory_space_constraint(value, pltpu.VMEM) if i in keep_in else value
        for i, value in enumerate(inputs)
    ]
    shapes = [
        pltpu.VMEM(shape, dtype) if i in keep_out else jax.ShapeDtypeStruct(shape, dtype)
        for i, (shape, dtype) in enumerate(outs)
    ]
    return pl.pallas_call(
        kernel,
        out_shape=shapes,
        in_specs=[pl.BlockSpec(memory_space=space)] * len(inputs),
        out_specs=[vmem] * len(outs),
        scratch_shapes=[pltpu.VMEM(shape, F32) if isinstance(shape, tuple) else shape for shape in scratch],
        compiler_params=pltpu.CompilerParams(vmem_limit_bytes=VMEM_LIMIT),
    )(*inputs)


def shift_along(value, axis, by):
    size = lax.axis_size(axis)
    return lax.ppermute(value, axis, [(i, i + by) for i in range(size) if 0 <= i + by < size])


def gather_plane(value):
    peers = lax.axis_size(("gx", "gy"))
    copies = jnp.broadcast_to(value[None], (peers,) + value.shape)
    return lax.all_to_all(copies, ("gx", "gy"), 0, 0, tiled=True)


def local(right_side, face_coefficients, solid):
    nx2, ny2 = 2 * lax.axis_size("gx"), 4 * lax.axis_size("gy")
    (own,) = call(
        prepare_kernel,
        [right_side, face_coefficients, solid],
        [((8, 5, 16, 128), BF16)],
        [
            (8, 16, 128),
            pltpu.VMEM((3, 8, 16, 128), BF16),
            pltpu.VMEM((8, 16, 128), jnp.int32),
            pltpu.SemaphoreType.DMA((3,)),
        ],
        space=pltpu.HBM,
    )
    before, after = shift_along(own, "gz", 1), shift_along(own, "gz", -1)
    (own,) = call(rim_kernel, [own, before, after], [((8, 6, 16, 128), BF16)])
    block = jnp.concatenate([shift_along(own, "gx", 1), own, shift_along(own, "gx", -1)], axis=0)
    before, after = shift_along(block, "gy", 1), shift_along(block, "gy", -1)

    fine, fine_up = (24, 40, 256), (25, 40, 256)
    mid, mid_up = (16, 24, 128), (17, 24, 128)
    rows, wide, edge = (12, 24, 256), (16, 24, 256), (6, 24, 128)
    *state, up, down, pay = call(
        first_kernel,
        [block, before, after],
        [(shape, F32) for shape in (fine, fine_up, fine, fine, fine, fine, mid, mid_up, mid, mid, mid, edge, edge, (8, 128))],
        [fine, fine, fine, fine, (2, 40, 128), rows, rows, rows, rows, mid, mid, mid, mid, (24, 128), (8, 128)],
        keep_out=range(11),
    )
    low, high = shift_along(up, "gx", 1), shift_along(down, "gx", -1)
    own = gather_plane(pay)
    before, after = shift_along(own, "gz", 1), shift_along(own, "gz", -1)
    level_2, level_3 = (nx2, ny2, 128), (nx2 // 2, ny2 // 2, 128)
    window = (nx2 + 6, ny2, 128)
    half = (nx2 // 2, ny2, 128)
    first_pre, image, *more, pay = call(
        second_kernel,
        [*state, low, high, own, before, after],
        [((8, 16, 128), F32)] * 2
        + [(shape, F32) for shape in (fine, mid, *[level_2] * 4, *[level_3] * 4, (4, 128))],
        [(4,) + level_2, half, half, window, (8, 24, 128), mid, mid, wide, (2, 40, 128),
         fine, fine, fine, (8, 24, 256), mid, (32, 128)],
        keep_in=range(11),
        keep_out=range(2, 12),
    )
    own = gather_plane(pay).reshape(nx2 * ny2 // 16, 8, 128)
    before, after = shift_along(own, "gz", 1), shift_along(own, "gz", -1)
    _, f0, f1, f2, w, _, _, f10, f11, f12, w1 = state
    mapped, sums = call(
        third_kernel,
        [f0, f1, f2, w, f10, f11, f12, w1, *more, own, before, after],
        [((8, 16, 128), F32), ((1, 128), F32)],
        [level_2, half, half, window, (8, 24, 128), mid, mid, wide, (2, 40, 128), fine],
        keep_in=range(18),
    )
    peers = lax.axis_size("gz")
    sums = lax.all_to_all(jnp.broadcast_to(sums[None], (peers, 1, 128)), "gz", 0, 0, tiled=True)
    return tuple(
        call(
            last_kernel,
            [sums, right_side, first_pre, image, mapped],
            [((8, 16, 128), F32)] * 3,
        )
    )


def solution(mesh):
    placed = P("gx", "gy", "gz")
    return jax.shard_map(
        local,
        mesh=mesh,
        in_specs=(placed, P(None, "gx", "gy", "gz"), placed),
        out_specs=(placed, placed, placed),
        check_vma=False,
    )
```

```python
import functools

import jax
import jax.numpy as jnp
from jax import lax
from jax.experimental import pallas as pl
from jax.experimental.pallas import tpu as pltpu
from jax.sharding import PartitionSpec as P

F32 = jnp.float32
BF16 = jnp.bfloat16
ABSORB = 0.001
RELAX = 0.8
KEEP = 0.2
SWEEPS = 6
VMEM_LIMIT = 24 * 1024 * 1024


def one_hot(rows, cols, rule, weight=1.0):
    r = lax.broadcasted_iota(jnp.int32, (rows, cols), 0)
    c = lax.broadcasted_iota(jnp.int32, (rows, cols), 1)
    return jnp.where(rule(r, c), weight, 0.0).astype(BF16)


def spread(values, matrix):
    high = values.astype(BF16)
    low = (values - high.astype(F32)).astype(BF16)
    return jnp.dot(high, matrix, preferred_element_type=F32) + jnp.dot(
        low, matrix, preferred_element_type=F32
    )


def pick(matrix, values):
    high = values.astype(BF16)
    low = (values - high.astype(F32)).astype(BF16)
    return jnp.dot(matrix, high, preferred_element_type=F32) + jnp.dot(
        matrix, low, preferred_element_type=F32
    )


def root(values):
    return values * lax.rsqrt(jnp.maximum(values, 1e-12))


def turn(values, shift, axis):
    return pltpu.roll(values, shift % values.shape[axis], axis)


def iota(shape, dim):
    return lax.broadcasted_iota(jnp.int32, shape, dim)


def plane_terms(v, f1, f2):
    return turn(v, 1, 0) * f1 + turn(v * f1, -1, 0) + turn(v, 1, 1) * f2 + turn(v * f2, -1, 1)


def neighbours(v_ref, f0_ref, f1_ref, f2_ref, p):
    return (
        f0_ref[p] * v_ref[p - 1]
        + f0_ref[p + 1] * v_ref[p + 1]
        + plane_terms(v_ref[p], f1_ref[p], f2_ref[p])
    )


def neighbours_3d(v, f0, f1, f2):
    zero = jnp.zeros_like(v[:1])
    up = f0 * v
    return (
        f0 * jnp.concatenate([zero, v[:-1]], 0)
        + jnp.concatenate([up[1:], zero], 0)
        + turn(v, 1, 1) * f1
        + turn(v * f1, -1, 1)
        + turn(v, 1, 2) * f2
        + turn(v * f2, -1, 2)
    )


def row_pairs(t_ref, values, both):
    out = []
    for half in range(2):
        t_ref[half] = values[:, 128 * half : 128 * half + 128]
        first = t_ref[half, pl.ds(0, 20, 2), :]
        out.append(first + t_ref[half, pl.ds(1, 20, 2), :] if both else first)
    return out


def put_rows(r_ref, q, halves):
    for half in range(2):
        r_ref[q, pl.ds(0, 20), pl.ds(128 * half, 128)] = halves[half]


def prepare_kernel(s_hbm, fc_hbm, solid_hbm, out_ref, ends_ref, s_ref, fc_ref, solid_ref, sems):
    copies = [
        pltpu.make_async_copy(source, target, sems.at[i])
        for i, (source, target) in enumerate(
            ((s_hbm, s_ref), (fc_hbm, fc_ref), (solid_hbm, solid_ref))
        )
    ]
    for copy in copies:
        copy.start()
    for copy in copies:
        copy.wait()
    s = s_ref[...]
    high = s.astype(BF16)
    out_ref[:, 0] = high
    out_ref[:, 1] = (s - high.astype(F32)).astype(BF16)
    weight = 1.0 - 0.75 * solid_ref[...].astype(F32)
    for a in range(3):
        out_ref[:, 2 + a] = (fc_ref[a].astype(F32) * weight).astype(BF16)
    lane = iota((16, 128), 1)

    def body(p, carry):
        ends = jnp.zeros((16, 128), F32)
        for f in range(5):
            t = turn(out_ref[p, f].astype(F32), 24 * f + 12, 1)
            ends = jnp.where((lane >= 24 * f) & (lane < 24 * f + 24), t, ends)
        ends_ref[p] = ends.astype(BF16)
        return carry

    lax.fori_loop(0, 8, body, 0, unroll=4)


def rim_kernel(own_ref, before_ref, after_ref, out_ref):
    lane = iota((8, 16, 128), 2)
    last = jnp.zeros((8, 16, 128), jnp.bool_)
    for f in range(5):
        last = last | ((lane >= 24 * f) & (lane < 24 * f + 12))
    out_ref[:, 0:5] = own_ref[...]
    rim = jnp.where(last, before_ref[...].astype(F32), after_ref[...].astype(F32))
    out_ref[:, 5] = rim.astype(BF16)


def first_kernel(
    x_ref, ym_ref, yp_ref,
    s_ref, f0_ref, f1_ref, f2_ref, w_ref, d_ref,
    s1_ref, f10_ref, f11_ref, f12_ref, w1_ref, up_ref, down_ref, pay_ref,
    c0_ref, c1_ref, c2_ref, sm_ref, t_ref, r0_ref, r1_ref, r2_ref, rs_ref,
    l10_ref, l11_ref, l12_ref, sm1_ref, t1_ref, u_ref,
):
    at_x = lax.axis_index("gx") == 0
    at_y = lax.axis_index("gy") == 0
    at_z = lax.axis_index("gz") == 0
    lane = iota((40, 128), 1)
    side = (lane < 12) | (lane >= 116)

    def unpack(p, carry):
        tiles = []
        for f in range(6):
            column = jnp.concatenate(
                [ym_ref[p, f].astype(F32), x_ref[p, f].astype(F32), yp_ref[p, f].astype(F32)], 0
            )
            tiles.append(turn(column, -4, 0)[:40])
        rims = [
            jnp.where(side, turn(tiles[5], -(24 * f + 12), 1), 0.0) for f in range(5)
        ]
        s_ref[p, :, 0:128] = tiles[0] + tiles[1]
        s_ref[p, :, 128:256] = rims[0] + rims[1]
        for a, c_ref in enumerate((c0_ref, c1_ref, c2_ref)):
            c_ref[p, :, 0:128] = tiles[2 + a]
            c_ref[p, :, 128:256] = rims[2 + a]
        return carry

    lax.fori_loop(0, 24, unpack, 0, unroll=4)

    def faces(p, carry):
        before = jnp.maximum(p - 1, 0)
        f0_ref[p] = root(c0_ref[p] * c0_ref[before])
        c1 = c1_ref[p]
        f1_ref[p] = root(c1 * turn(c1, 1, 0))
        c2 = c2_ref[p]
        f2_ref[p] = root(c2 * turn(c2, 1, 1))
        return carry

    lax.fori_loop(0, 24, faces, 0, unroll=4)
    f0_ref[24] = jnp.zeros((40, 256), F32)

    first_row = (iota((40, 256), 0) == 12) & at_y
    first_lane = (iota((40, 256), 1) == 0) & at_z
    for ref in (r0_ref, r1_ref, r2_ref, rs_ref):
        ref[...] = jnp.zeros_like(ref)

    def diagonals(q, carry):
        lows = []
        for i in range(2):
            p = 2 * q + i
            f0, f1, f2 = f0_ref[p], f1_ref[p], f2_ref[p]
            low0 = f0 + jnp.where((p == 8) & at_x, c0_ref[p], 0.0)
            low1 = f1 + jnp.where(first_row, c1_ref[p], 0.0)
            low2 = f2 + jnp.where(first_lane, c2_ref[p], 0.0)
            d = ABSORB + low0 + f0_ref[p + 1] + low1 + turn(f1, -1, 0) + low2 + turn(f2, -1, 1)
            w = RELAX / d
            d_ref[p] = d
            w_ref[p] = w
            sm_ref[p] = w * s_ref[p]
            lows.append((low0, low1, low2))
        put_rows(r0_ref, q, row_pairs(t_ref, lows[0][0], True))
        put_rows(r1_ref, q, row_pairs(t_ref, lows[0][1] + lows[1][1], False))
        put_rows(r2_ref, q, row_pairs(t_ref, lows[0][2] + lows[1][2], True))
        return carry

    lax.fori_loop(0, 12, diagonals, 0, unroll=2)

    def leftovers(q, carry):
        total = jnp.zeros((40, 256), F32)
        for i in range(2):
            p = 2 * q + i
            total += KEEP * s_ref[p] + neighbours(sm_ref, f0_ref, f1_ref, f2_ref, p)
        put_rows(rs_ref, q, row_pairs(t_ref, total, True))
        return carry

    lax.fori_loop(1, 11, leftovers, 0, unroll=2)

    pairs = one_hot(256, 128, lambda r, c: lax.shift_right_logical(r, 1) == c, 0.25)
    evens = one_hot(256, 128, lambda r, c: r == 2 * c, 0.25)
    for target, source, matrix in (
        (l10_ref, r0_ref, pairs), (l11_ref, r1_ref, pairs), (l12_ref, r2_ref, evens), (s1_ref, rs_ref, pairs)
    ):
        target[pl.ds(0, 2)] = jnp.zeros((2, 24, 128), F32)
        target[pl.ds(14, 2)] = jnp.zeros((2, 24, 128), F32)
        value = spread(source[...].reshape(288, 256), matrix).reshape(12, 24, 128)
        target[pl.ds(2, 12)] = 2.0 * value if target is s1_ref else value

    first_row_1 = (iota((24, 128), 0) == 6) & at_y
    first_lane_1 = (iota((24, 128), 1) == 0) & at_z

    def faces_1(p, carry):
        f10_ref[p] = jnp.where((p == 6) & at_x, 0.0, l10_ref[p])
        f11_ref[p] = jnp.where(first_row_1, 0.0, l11_ref[p])
        f12_ref[p] = jnp.where(first_lane_1, 0.0, l12_ref[p])
        return carry

    lax.fori_loop(0, 16, faces_1, 0, unroll=4)
    f10_ref[16] = jnp.zeros((24, 128), F32)

    def diagonals_1(p, carry):
        d = (
            4.0 * ABSORB + l10_ref[p] + f10_ref[p + 1]
            + l11_ref[p] + turn(f11_ref[p], -1, 0)
            + l12_ref[p] + turn(f12_ref[p], -1, 1)
        )
        w = RELAX / d
        w1_ref[p] = w
        sm1_ref[p] = w * s1_ref[p]
        return carry

    lax.fori_loop(2, 14, diagonals_1, 0, unroll=4)
    for i, ref in enumerate((s1_ref, w1_ref, f10_ref)):
        up_ref[pl.ds(2 * i, 2)] = ref[pl.ds(5, 2)]
        down_ref[pl.ds(2 * i, 2)] = ref[pl.ds(9, 2)]

    def quad(values, both):
        t1_ref[...] = values
        first = t1_ref[pl.ds(6, 4, 2), :]
        return first + t1_ref[pl.ds(7, 4, 2), :] if both else first

    def leftover_1(p):
        return KEEP * s1_ref[p] + neighbours(sm1_ref, f10_ref, f11_ref, f12_ref, p)

    row8, lane8 = iota((8, 128), 0), iota((8, 128), 1)
    narrow = one_hot(128, 128, lambda r, c: (lax.shift_right_logical(r, 1) == c) & (r < 64))
    narrow_even = one_hot(128, 128, lambda r, c: (r == 2 * c) & (r < 64))
    total = jnp.zeros((8, 128), F32)
    for f in range(4):
        for i in range(2):
            p = 6 + 2 * i
            if f == 0:
                part = quad(leftover_1(p) + leftover_1(p + 1), True)
            elif f == 1:
                part = quad(l10_ref[p], True)
            elif f == 2:
                part = quad(l11_ref[p] + l11_ref[p + 1], False)
            else:
                part = quad(l12_ref[p] + l12_ref[p + 1], True)
            u_ref[f, pl.ds(4 * i, 4), :] = part * (0.5 if f == 0 else 0.25)
        part = spread(u_ref[f], narrow_even if f == 3 else narrow)
        for i in range(2):
            for h in range(2):
                to = 32 * f + 16 * i
                moved = turn(turn(part, 4 * (h - i), 0), to - 16 * h, 1)
                here = (lax.shift_right_logical(row8, 2) == h) & (lane8 >= to) & (lane8 < to + 16)
                total = jnp.where(here, moved, total)
    pay_ref[...] = total


def window(pieces, to, lane):
    out = jnp.zeros(pieces[0].shape, F32)
    for k, piece in enumerate(pieces):
        out = jnp.where((lane >= 16 * k) & (lane < 16 * k + 16), turn(piece, 16 * k - to, 1), out)
    return out


def solve_2(s2, level_2, level_3, t3_ref, e_ref):
    f0, f1, f2, w = level_2
    g0, g1, g2, w3 = level_3
    nx, ny, _ = s2.shape
    sm = w * s2
    left = KEEP * s2 + neighbours_3d(sm, f0, f1, f2)
    s3 = coarse_2(left.reshape(nx // 2, 2, ny, 128).sum(1), t3_ref, True, 0.5, False)
    e = w3 * s3
    for _ in range(SWEEPS - 1):
        e = KEEP * e + w3 * (s3 + neighbours_3d(e, g0, g1, g2))
    widen = one_hot(128, 128, lambda r, c: (r == lax.shift_right_logical(c, 1)) & (c < 64))
    wide = spread(e.reshape(nx * ny // 4, 128), widen).reshape(nx // 2, ny // 2, 128)
    for x in range(nx // 2):
        for i in range(2):
            e_ref[x, pl.ds(i, ny // 2, 2), :] = wide[x]
    e2 = e_ref[...]
    corrected = sm + jnp.concatenate([e2[:, None], e2[:, None]], 1).reshape(nx, ny, 128)
    return KEEP * corrected + w * (s2 + neighbours_3d(corrected, f0, f1, f2))


def coarse_2(values, t3_ref, both, weight, even):
    nx, ny, _ = values.shape
    t3_ref[...] = values
    first = t3_ref[:, pl.ds(0, ny // 2, 2), :]
    if both:
        first = first + t3_ref[:, pl.ds(1, ny // 2, 2), :]
    if even:
        rule = lambda r, c: (r == 2 * c) & (r < 64)
    else:
        rule = lambda r, c: (lax.shift_right_logical(r, 1) == c) & (r < 64)
    flat = spread(first.reshape(nx * ny // 2, 128), one_hot(128, 128, rule, weight))
    return flat.reshape(nx, ny // 2, 128)


def coefficients(low, mask_lane, absorb):
    shape = low[0].shape
    f0 = jnp.where(iota(shape, 0) == 0, 0.0, low[0])
    f1 = jnp.where(iota(shape, 1) == 0, 0.0, low[1])
    f2 = jnp.where((iota(shape, 2) == mask_lane) & (lax.axis_index("gz") == 0), 0.0, low[2])
    d = (
        absorb + low[0] + jnp.concatenate([f0[1:], jnp.zeros_like(f0[:1])], 0)
        + low[1] + turn(f1, -1, 1) + low[2] + turn(f2, -1, 2)
    )
    return f0, f1, f2, RELAX / d


def fetch_level_2(m2_ref, planes, pick_ref):
    gx, gy = lax.axis_index("gx"), lax.axis_index("gy")
    ny = m2_ref.shape[1]

    def source(c):
        return jnp.where(c < 96, 16, -48) + lax.shift_right_logical(c, 1)

    widen = one_hot(128, 128, lambda r, c: r == source(c))
    rows = one_hot(24, ny, lambda r, c: c == 4 * gy - 3 + lax.shift_right_logical(r, 1))
    for k in planes:
        pick_ref[k] = spread(pick(rows, m2_ref[2 * gx + k]), widen)


def widen_level_1(m1_ref, wide_ref, lo, hi):
    rows = 24 * (hi - lo)
    widen = one_hot(128, 256, lambda r, c: r == lax.shift_right_logical(c, 1))
    wide_ref[pl.ds(lo, hi - lo)] = spread(m1_ref[pl.ds(lo, hi - lo)].reshape(rows, 128), widen).reshape(
        hi - lo, 24, 256
    )


def double_rows(t_ref, wide_ref, q):
    for half in range(2):
        part = wide_ref[q, pl.ds(0, 20), pl.ds(128 * half, 128)]
        for i in range(2):
            t_ref[half, pl.ds(i, 20, 2), :] = part
    return jnp.concatenate([t_ref[0], t_ref[1]], 1)


def second_kernel(
    s_ref, f0_ref, f1_ref, f2_ref, w_ref, d_ref,
    s1_ref, f10_ref, f11_ref, f12_ref, w1_ref,
    low_ref, high_ref, before_ref, own0_ref, own1_ref, after_ref,
    fp_out, im_out, im_ref, t1s_ref, f20_ref, f21_ref, f22_ref, w2_ref,
    f30_ref, f31_ref, f32_ref, w3_ref, pay_ref,
    v_ref, t3_ref, e_ref, m2_ref, pick_ref, corr1_ref, m1_ref, wide_ref, t_ref,
    corr_ref, fp_ref, sm_ref, rs_ref, sm1_ref, tq_ref,
):
    nx2, ny2 = f20_ref.shape[:2]
    lane8 = iota((8, 128), 1)
    row8 = iota((8, 128), 0)

    def assemble(x, carry):
        for pair in range(ny2 // 8):
            g = x * (ny2 // 8) + pair
            pieces = [ref[g] for ref in (before_ref, own0_ref, own1_ref, after_ref)]
            for f in range(4):
                for i in range(2):
                    v_ref[f, 2 * x + i, pl.ds(8 * pair, 8), :] = window(pieces, 32 * f + 16 * i, lane8)
        return carry

    lax.fori_loop(0, nx2 // 2, assemble, 0)

    s2 = v_ref[0]
    low = (v_ref[1], v_ref[2], v_ref[3])
    level_2 = coefficients(low, 16, 16.0 * ABSORB)
    f20_ref[...], f21_ref[...], f22_ref[...], w2_ref[...] = level_2
    halves = [t.reshape(nx2 // 2, 2, ny2, 128) for t in low]
    low_3 = (
        coarse_2(halves[0][:, 0], t3_ref, True, 0.25, False),
        coarse_2(halves[1].sum(1), t3_ref, False, 0.25, False),
        coarse_2(halves[2].sum(1), t3_ref, True, 0.25, True),
    )
    level_3 = coefficients(low_3, 8, 64.0 * ABSORB)
    f30_ref[...], f31_ref[...], f32_ref[...], w3_ref[...] = level_3
    m2_ref[...] = jnp.zeros_like(m2_ref)
    m2_ref[pl.ds(3, nx2)] = solve_2(s2, level_2, level_3, t3_ref, e_ref)
    fetch_level_2(m2_ref, range(8), pick_ref)

    def correct_1(p, carry):
        corr1_ref[p] = w1_ref[p] * s1_ref[p] + pick_ref[lax.shift_right_logical(p, 1)]
        return carry

    lax.fori_loop(3, 13, correct_1, 0, unroll=5)
    for k in range(2):
        corr1_ref[1 + k] = low_ref[2 + k] * low_ref[k] + pick_ref[(1 + k) // 2]
        corr1_ref[13 + k] = high_ref[2 + k] * high_ref[k] + pick_ref[(13 + k) // 2]

    def relax_1(p, carry):
        m1_ref[p] = KEEP * corr1_ref[p] + w1_ref[p] * (
            s1_ref[p] + neighbours(corr1_ref, f10_ref, f11_ref, f12_ref, p)
        )
        return carry

    lax.fori_loop(3, 13, relax_1, 0, unroll=5)
    for p, source, w, face, next_face in (
        (2, low_ref[1], low_ref[3], low_ref[5], f10_ref[3]),
        (13, high_ref[0], high_ref[2], f10_ref[13], high_ref[5]),
    ):
        m1_ref[p] = KEEP * corr1_ref[p] + w * (
            source + face * corr1_ref[p - 1] + next_face * corr1_ref[p + 1]
            + plane_terms(corr1_ref[p], f11_ref[p], f12_ref[p])
        )
    widen_level_1(m1_ref, wide_ref, 2, 14)

    def correct(q, carry):
        e = double_rows(t_ref, wide_ref, q)
        for i in range(2):
            p = 2 * q + i - 4
            corr_ref[p] = w_ref[p] * s_ref[p] + e
        return carry

    lax.fori_loop(2, 14, correct, 0, unroll=2)

    def relax(p, carry):
        fp_ref[p] = KEEP * corr_ref[p] + w_ref[p] * (
            s_ref[p] + neighbours(corr_ref, f0_ref, f1_ref, f2_ref, p)
        )
        return carry

    lax.fori_loop(2, 22, relax, 0, unroll=4)

    def image(p, carry):
        im = d_ref[p] * fp_ref[p] - neighbours(fp_ref, f0_ref, f1_ref, f2_ref, p)
        im_ref[p] = im
        sm_ref[p] = w_ref[p] * im
        return carry

    lax.fori_loop(3, 21, image, 0, unroll=3)

    rs_ref[...] = jnp.zeros_like(rs_ref)
    inside = (iota((40, 128), 0) >= 12) & (iota((40, 128), 0) < 28)

    def leftovers(q, sums):
        total = jnp.zeros((40, 256), F32)
        for i in range(2):
            p = 2 * q + i - 4
            left = KEEP * im_ref[p] + neighbours(sm_ref, f0_ref, f1_ref, f2_ref, p)
            total += left
            own = jnp.where(inside & (p >= 8) & (p < 16), 1.0, 0.0)
            fp, im = fp_ref[p, :, 0:128], im_ref[p, :, 0:128]
            sums = (
                sums[0] + own * s_ref[p, :, 0:128] * fp,
                sums[1] + own * fp * im,
                sums[2] + own * sm_ref[p, :, 0:128] * (im + left[:, 0:128]),
            )
        put_rows(rs_ref, q - 4, row_pairs(t_ref, total, True))
        return sums

    zero = jnp.zeros((40, 128), F32)
    sums = lax.fori_loop(4, 12, leftovers, (zero, zero, zero), unroll=2)

    for p in range(8):
        fp_out[p] = fp_ref[8 + p, pl.ds(12, 16), 0:128]
        im_out[p] = im_ref[8 + p, pl.ds(12, 16), 0:128]

    pairs = one_hot(256, 128, lambda r, c: lax.shift_right_logical(r, 1) == c, 0.5)
    t1s_ref[...] = jnp.zeros_like(t1s_ref)
    t1s_ref[pl.ds(4, 8)] = spread(rs_ref[...].reshape(192, 256), pairs).reshape(8, 24, 128)
    for p in range(5, 11):
        sm1_ref[p] = w1_ref[p] * t1s_ref[p]
    inside_1 = jnp.where(
        (iota((24, 128), 0) >= 6) & (iota((24, 128), 0) < 14) & (iota((24, 128), 1) < 64), 1.0, 0.0
    )
    second = jnp.zeros((24, 128), F32)
    halves = [jnp.zeros((8, 128), F32)] * 2
    tq_ref[...] = jnp.zeros_like(tq_ref)
    for i in range(2):
        total = jnp.zeros((24, 128), F32)
        for j in range(2):
            p = 6 + 2 * i + j
            s1 = t1s_ref[p]
            left = KEEP * s1 + neighbours(sm1_ref, f10_ref, f11_ref, f12_ref, p)
            second += inside_1 * sm1_ref[p] * (s1 + left)
            total += left
        tq_ref[pl.ds(0, 24), :] = total
        tq_ref[pl.ds(24, 4), :] = tq_ref[pl.ds(6, 4, 2), :] + tq_ref[pl.ds(7, 4, 2), :]
        for h in range(2):
            place = one_hot(
                128, 128,
                lambda r, c, i=i, h=h: (lax.shift_right_logical(r, 1) - 16 * h == (c & 15))
                & (r < 64) & ((lax.shift_right_logical(c, 4) & 1) == i), 0.5,
            )
            halves[h] += spread(tq_ref[pl.ds(24, 8), :], place)
    scalars = (jnp.sum(sums[0]), jnp.sum(sums[1]), jnp.sum(sums[2]) + 2.0 * jnp.sum(second))
    mine = lax.shift_right_logical(lane8, 5) == row8
    pay = jnp.zeros((8, 128), F32)
    for h in range(2):
        line = jnp.sum(jnp.where(mine, halves[h], 0.0), axis=0, keepdims=True)
        pay = jnp.where(row8 == h, line, pay)
    for k, value in enumerate(scalars):
        pay = jnp.where((lane8 == k) & (row8 == 2), value, pay)
    pay_ref[...] = pay[:4]


def third_kernel(
    f0_ref, f1_ref, f2_ref, w_ref, f10_ref, f11_ref, f12_ref, w1_ref,
    im_ref, t1s_ref, f20_ref, f21_ref, f22_ref, w2_ref, f30_ref, f31_ref, f32_ref, w3_ref,
    before_ref, own0_ref, own1_ref, after_ref, parts_ref,
    mi_out, scalar_out,
    v_ref, t3_ref, e_ref, m2_ref, pick_ref, corr1_ref, m1_ref, wide_ref, t_ref, corr_ref,
):
    nx2, ny2 = f20_ref.shape[:2]
    lane = iota((ny2 // 4, 128), 1)

    def assemble(x, carry):
        pieces = [ref[x] for ref in (before_ref, own0_ref, own1_ref, after_ref)]
        for i in range(2):
            for j in range(4):
                v_ref[2 * x + i, pl.ds(j, ny2 // 4, 4), :] = window(pieces, 32 * j + 16 * i, lane)
        return carry

    lax.fori_loop(0, nx2 // 2, assemble, 0, unroll=2)
    s2 = v_ref[...]
    level_2 = (f20_ref[...], f21_ref[...], f22_ref[...], w2_ref[...])
    level_3 = (f30_ref[...], f31_ref[...], f32_ref[...], w3_ref[...])
    m2 = solve_2(s2, level_2, level_3, t3_ref, e_ref)
    lane3 = iota(s2.shape, 2)
    part = 4.0 * jnp.sum(jnp.where((lane3 >= 16) & (lane3 < 48), s2 * m2, 0.0))
    sums = jnp.sum(jnp.sum(parts_ref[...], axis=0), axis=0, keepdims=True)
    scalar_out[...] = jnp.where(iota((1, 128), 1) == 3, part, sums)
    m2_ref[...] = jnp.zeros_like(m2_ref)
    m2_ref[pl.ds(3, nx2)] = m2
    fetch_level_2(m2_ref, range(2, 6), pick_ref)
    for p in range(4, 12):
        corr1_ref[p] = w1_ref[p] * t1s_ref[p] + pick_ref[p // 2]
    for p in range(5, 11):
        m1_ref[p] = KEEP * corr1_ref[p] + w1_ref[p] * (
            t1s_ref[p] + neighbours(corr1_ref, f10_ref, f11_ref, f12_ref, p)
        )
    widen_level_1(m1_ref, wide_ref, 5, 11)

    def correct(q, carry):
        e = double_rows(t_ref, wide_ref, q)
        for i in range(2):
            p = 2 * q + i - 4
            corr_ref[p] = w_ref[p] * im_ref[p] + e
        return carry

    lax.fori_loop(5, 11, correct, 0, unroll=2)

    for p in range(8):
        q = 8 + p
        mi = KEEP * corr_ref[q] + w_ref[q] * (
            im_ref[q] + neighbours(corr_ref, f0_ref, f1_ref, f2_ref, q)
        )
        t_ref[0] = mi[:, 0:128]
        mi_out[p] = t_ref[0, pl.ds(12, 16), :]


def last_kernel(sums_ref, s_ref, fp_ref, im_ref, mi_ref, solution_ref, residual_ref, direction_ref):
    total = jnp.sum(sums_ref[...], axis=0)
    lane = iota((1, 128), 1)

    def value(lanes):
        keep = lane == lanes[0]
        for k in lanes[1:]:
            keep = keep | (lane == k)
        return jnp.sum(jnp.where(keep, total, 0.0), axis=1, keepdims=True)

    projected, curvature, product = value((0,)), value((1,)), value((2, 3))
    step = projected / curvature
    share = product / curvature
    for p in range(8):
        fp = fp_ref[p]
        solution_ref[p] = step * fp
        residual_ref[p] = s_ref[p] - step * im_ref[p]
        direction_ref[p] = step * (share * fp - mi_ref[p])


def call(kernel, inputs, outs, scratch=(), keep_in=(), keep_out=(), space=pltpu.VMEM):
    vmem = pl.BlockSpec(memory_space=pltpu.VMEM)
    inputs = [
        pltpu.with_memory_space_constraint(value, space) if i in keep_in else value
        for i, value in enumerate(inputs)
    ]
    shapes = [
        pltpu.VMEM(shape, dtype) if i in keep_out else jax.ShapeDtypeStruct(shape, dtype)
        for i, (shape, dtype) in enumerate(outs)
    ]
    return pl.pallas_call(
        kernel,
        out_shape=shapes,
        in_specs=[pl.BlockSpec(memory_space=space)] * len(inputs),
        out_specs=[vmem] * len(outs),
        scratch_shapes=[pltpu.VMEM(shape, F32) if isinstance(shape, tuple) else shape for shape in scratch],
        compiler_params=pltpu.CompilerParams(vmem_limit_bytes=VMEM_LIMIT),
    )(*inputs)


def shift_along(value, axis, by):
    size = lax.axis_size(axis)
    return lax.ppermute(value, axis, [(i, i + by) for i in range(size) if 0 <= i + by < size])


def gather_plane(value):
    peers = lax.axis_size(("gx", "gy"))
    copies = jnp.broadcast_to(value.reshape(1, 1, -1), (peers, 1, value.size))
    return lax.all_to_all(copies, ("gx", "gy"), 0, 0, tiled=True)


def local(right_side, face_coefficients, solid):
    nx2, ny2 = 2 * lax.axis_size("gx"), 4 * lax.axis_size("gy")
    own, ends = call(
        prepare_kernel,
        [right_side, face_coefficients, solid],
        [((8, 5, 16, 128), BF16), ((8, 16, 128), BF16)],
        [
            (8, 16, 128),
            pltpu.VMEM((3, 8, 16, 128), BF16),
            pltpu.VMEM((8, 16, 128), jnp.int32),
            pltpu.SemaphoreType.DMA((3,)),
        ],
        keep_in=range(3),
        space=pltpu.HBM,
    )
    before, after = shift_along(ends, "gz", 1), shift_along(ends, "gz", -1)
    (own,) = call(rim_kernel, [own, before, after], [((8, 6, 16, 128), BF16)])
    block = jnp.concatenate([shift_along(own, "gx", 1), own, shift_along(own, "gx", -1)], axis=0)
    before, after = shift_along(block, "gy", 1), shift_along(block, "gy", -1)

    fine, fine_up = (24, 40, 256), (25, 40, 256)
    mid, mid_up = (16, 24, 128), (17, 24, 128)
    rows, wide, edge = (12, 24, 256), (16, 24, 256), (6, 24, 128)
    *state, up, down, pay = call(
        first_kernel,
        [block, before, after],
        [(shape, F32) for shape in (fine, fine_up, fine, fine, fine, fine, mid, mid_up, mid, mid, mid, edge, edge, (8, 128))],
        [fine, fine, fine, fine, (2, 40, 128), rows, rows, rows, rows, mid, mid, mid, mid, (24, 128), (4, 8, 128)],
        keep_out=range(11),
    )
    low, high = shift_along(up, "gx", 1), shift_along(down, "gx", -1)
    own = gather_plane(pay)
    pairs = (nx2 * ny2 // 16, 8, 128)
    own0, own1 = own[..., :512].reshape(pairs), own[..., 512:].reshape(pairs)
    before, after = shift_along(own1, "gz", 1), shift_along(own0, "gz", -1)
    level_2, level_3 = (nx2, ny2, 128), (nx2 // 2, ny2 // 2, 128)
    window = (nx2 + 6, ny2, 128)
    half = (nx2 // 2, ny2, 128)
    first_pre, image, *more, pay = call(
        second_kernel,
        [*state, low, high, before, own0, own1, after],
        [((8, 16, 128), F32)] * 2
        + [(shape, F32) for shape in (fine, mid, *[level_2] * 4, *[level_3] * 4, (4, 128))],
        [(4,) + level_2, half, half, window, (8, 24, 128), mid, mid, wide, (2, 40, 128),
         fine, fine, fine, (8, 24, 256), mid, (32, 128)],
        keep_in=range(11),
        keep_out=range(2, 12),
    )
    own = gather_plane(pay)
    plane = (nx2 // 2, ny2 // 4, 128)
    own0, own1, parts = (own[..., 128 * k : 128 * k + 128].reshape(plane) for k in range(3))
    before, after = shift_along(own1, "gz", 1), shift_along(own0, "gz", -1)
    _, f0, f1, f2, w, _, _, f10, f11, f12, w1 = state
    mapped, sums = call(
        third_kernel,
        [f0, f1, f2, w, f10, f11, f12, w1, *more, before, own0, own1, after, parts],
        [((8, 16, 128), F32), ((1, 128), F32)],
        [level_2, half, half, window, (8, 24, 128), mid, mid, wide, (2, 40, 128), fine],
        keep_in=range(18),
    )
    peers = lax.axis_size("gz")
    sums = lax.all_to_all(jnp.broadcast_to(sums[None], (peers, 1, 128)), "gz", 0, 0, tiled=True)
    return tuple(
        call(
            last_kernel,
            [sums, right_side, first_pre, image, mapped],
            [((8, 16, 128), F32)] * 3,
        )
    )


def solution(mesh):
    placed = P("gx", "gy", "gz")
    return jax.shard_map(
        local,
        mesh=mesh,
        in_specs=(placed, P(None, "gx", "gy", "gz"), placed),
        out_specs=(placed, placed, placed),
        check_vma=False,
    )
```

```python
import functools

import jax
import jax.numpy as jnp
from jax import lax
from jax.experimental import pallas as pl
from jax.experimental.pallas import tpu as pltpu
from jax.sharding import PartitionSpec as P

F32 = jnp.float32
BF16 = jnp.bfloat16
ABSORB = 0.001
RELAX = 0.8
KEEP = 0.2
SWEEPS = 6
VMEM_LIMIT = 24 * 1024 * 1024


def one_hot(rows, cols, rule, weight=1.0):
    r = lax.broadcasted_iota(jnp.int32, (rows, cols), 0)
    c = lax.broadcasted_iota(jnp.int32, (rows, cols), 1)
    return jnp.where(rule(r, c), weight, 0.0).astype(BF16)


def spread(values, matrix):
    high = values.astype(BF16)
    low = (values - high.astype(F32)).astype(BF16)
    return jnp.dot(high, matrix, preferred_element_type=F32) + jnp.dot(
        low, matrix, preferred_element_type=F32
    )


def pick(matrix, values):
    high = values.astype(BF16)
    low = (values - high.astype(F32)).astype(BF16)
    return jnp.dot(matrix, high, preferred_element_type=F32) + jnp.dot(
        matrix, low, preferred_element_type=F32
    )


def root(values):
    return values * lax.rsqrt(jnp.maximum(values, 1e-12))


def turn(values, shift, axis):
    return pltpu.roll(values, shift % values.shape[axis], axis)


def iota(shape, dim):
    return lax.broadcasted_iota(jnp.int32, shape, dim)


def plane_terms(v, f1, f2):
    return turn(v, 1, 0) * f1 + turn(v * f1, -1, 0) + turn(v, 1, 1) * f2 + turn(v * f2, -1, 1)


def neighbours(v_ref, f0_ref, f1_ref, f2_ref, p):
    return (
        f0_ref[p] * v_ref[p - 1]
        + f0_ref[p + 1] * v_ref[p + 1]
        + plane_terms(v_ref[p], f1_ref[p], f2_ref[p])
    )


def neighbours_3d(v, f0, f1, f2):
    zero = jnp.zeros_like(v[:1])
    up = f0 * v
    return (
        f0 * jnp.concatenate([zero, v[:-1]], 0)
        + jnp.concatenate([up[1:], zero], 0)
        + turn(v, 1, 1) * f1
        + turn(v * f1, -1, 1)
        + turn(v, 1, 2) * f2
        + turn(v * f2, -1, 2)
    )


def row_pairs(t_ref, values, both):
    out = []
    pairs = values.shape[0] // 2
    for half in range(2):
        t_ref[half] = values[:, 128 * half : 128 * half + 128]
        first = t_ref[half, pl.ds(0, pairs, 2), :]
        out.append(first + t_ref[half, pl.ds(1, pairs, 2), :] if both else first)
    return out


def put_rows(r_ref, q, halves):
    for half in range(2):
        r_ref[q, pl.ds(0, halves[half].shape[0]), pl.ds(128 * half, 128)] = halves[half]


def prepare_kernel(s_hbm, fc_hbm, solid_hbm, out_ref, ends_ref, s_ref, fc_ref, solid_ref, sems):
    copies = [
        pltpu.make_async_copy(source, target, sems.at[i])
        for i, (source, target) in enumerate(
            ((s_hbm, s_ref), (fc_hbm, fc_ref), (solid_hbm, solid_ref))
        )
    ]
    for copy in copies:
        copy.start()
    for copy in copies:
        copy.wait()
    s = s_ref[...]
    high = s.astype(BF16)
    out_ref[:, 0] = high
    out_ref[:, 1] = (s - high.astype(F32)).astype(BF16)
    weight = 1.0 - 0.75 * solid_ref[...].astype(F32)
    for a in range(3):
        out_ref[:, 2 + a] = (fc_ref[a].astype(F32) * weight).astype(BF16)
    lane = iota((16, 128), 1)

    def body(p, carry):
        ends = jnp.zeros((16, 128), F32)
        for f in range(5):
            t = turn(out_ref[p, f].astype(F32), 24 * f + 12, 1)
            ends = jnp.where((lane >= 24 * f) & (lane < 24 * f + 24), t, ends)
        ends_ref[p] = ends.astype(BF16)
        return carry

    lax.fori_loop(0, 8, body, 0, unroll=4)


def rim_kernel(own_ref, before_ref, after_ref, out_ref):
    lane = iota((8, 16, 128), 2)
    last = jnp.zeros((8, 16, 128), jnp.bool_)
    for f in range(5):
        last = last | ((lane >= 24 * f) & (lane < 24 * f + 12))
    out_ref[:, 0:5] = own_ref[...]
    rim = jnp.where(last, before_ref[...].astype(F32), after_ref[...].astype(F32))
    out_ref[:, 5] = rim.astype(BF16)


def fine_kernel(thin, x_ref, ym_ref, yp_ref, *refs):
    if thin:
        (up_ref, down_ref, pay_ref,
         s_ref, f0_ref, f1_ref, f2_ref, s1_ref, f10_ref, f11_ref, f12_ref, w1_ref, *refs) = refs
    else:
        s_ref, f0_ref, f1_ref, f2_ref, w_ref, d_ref, s1_ref, f10_ref, f11_ref, f12_ref, w1_ref, *refs = refs
    (c0_ref, c1_ref, c2_ref, sm_ref, t_ref, r0_ref, r1_ref, r2_ref, rs_ref,
     l10_ref, l11_ref, l12_ref, *refs) = refs
    planes = range(4, 20) if thin else range(24)
    rows, rows_1 = s_ref.shape[1], s1_ref.shape[1]
    own = 4 if thin else 12
    shape, shape_1 = (rows, 256), (rows_1, 128)
    at_x = lax.axis_index("gx") == 0
    at_y = lax.axis_index("gy") == 0
    at_z = lax.axis_index("gz") == 0
    lane = iota((rows, 128), 1)
    side = (lane < 12) | (lane >= 116)

    def unpack(p, carry):
        tiles = []
        for f in range(6):
            before, after = ym_ref[p, f].astype(F32), yp_ref[p, f].astype(F32)
            if thin:
                before, after = before[8:], after[:8]
            column = jnp.concatenate([before, x_ref[p, f].astype(F32), after], 0)
            tiles.append(turn(column, -4, 0)[:rows])
        rims = [
            jnp.where(side, turn(tiles[5], -(24 * f + 12), 1), 0.0) for f in range(5)
        ]
        s_ref[p, :, 0:128] = tiles[0] + tiles[1]
        s_ref[p, :, 128:256] = rims[0] + rims[1]
        for a, c_ref in enumerate((c0_ref, c1_ref, c2_ref)):
            c_ref[p, :, 0:128] = tiles[2 + a]
            c_ref[p, :, 128:256] = rims[2 + a]
        return carry

    lax.fori_loop(planes.start, planes.stop, unpack, 0, unroll=4)

    def faces(p, carry):
        before = jnp.maximum(p - 1, planes.start)
        f0_ref[p] = root(c0_ref[p] * c0_ref[before])
        c1 = c1_ref[p]
        f1_ref[p] = root(c1 * turn(c1, 1, 0))
        c2 = c2_ref[p]
        f2_ref[p] = root(c2 * turn(c2, 1, 1))
        return carry

    lax.fori_loop(planes.start, planes.stop, faces, 0, unroll=4)
    f0_ref[planes.stop] = jnp.zeros(shape, F32)

    first_row = (iota(shape, 0) == own) & at_y
    first_lane = (iota(shape, 1) == 0) & at_z
    for ref in (r0_ref, r1_ref, r2_ref, rs_ref):
        ref[...] = jnp.zeros_like(ref)

    def diagonals(q, carry):
        lows = []
        for i in range(2):
            p = 2 * q + i
            f0, f1, f2 = f0_ref[p], f1_ref[p], f2_ref[p]
            low0 = f0 + jnp.where((p == 8) & at_x, c0_ref[p], 0.0)
            low1 = f1 + jnp.where(first_row, c1_ref[p], 0.0)
            low2 = f2 + jnp.where(first_lane, c2_ref[p], 0.0)
            d = ABSORB + low0 + f0_ref[p + 1] + low1 + turn(f1, -1, 0) + low2 + turn(f2, -1, 1)
            w = RELAX / d
            if not thin:
                d_ref[p] = d
                w_ref[p] = w
            sm_ref[p] = w * s_ref[p]
            lows.append((low0, low1, low2))
        put_rows(r0_ref, q, row_pairs(t_ref, lows[0][0], True))
        put_rows(r1_ref, q, row_pairs(t_ref, lows[0][1] + lows[1][1], False))
        put_rows(r2_ref, q, row_pairs(t_ref, lows[0][2] + lows[1][2], True))
        return carry

    lax.fori_loop(planes.start // 2, planes.stop // 2, diagonals, 0, unroll=2)

    def leftovers(q, carry):
        total = jnp.zeros(shape, F32)
        for i in range(2):
            p = 2 * q + i
            total += KEEP * s_ref[p] + neighbours(sm_ref, f0_ref, f1_ref, f2_ref, p)
        put_rows(rs_ref, q, row_pairs(t_ref, total, True))
        return carry

    lax.fori_loop(planes.start // 2 + 1, planes.stop // 2 - 1, leftovers, 0, unroll=2)

    pairs = one_hot(256, 128, lambda r, c: lax.shift_right_logical(r, 1) == c, 0.25)
    evens = one_hot(256, 128, lambda r, c: r == 2 * c, 0.25)
    first, count = planes.start // 2, len(planes) // 2
    for target, source, matrix in (
        (l10_ref, r0_ref, pairs), (l11_ref, r1_ref, pairs), (l12_ref, r2_ref, evens), (s1_ref, rs_ref, pairs)
    ):
        target[...] = jnp.zeros_like(target)
        value = spread(source[pl.ds(first, count)].reshape(count * rows_1, 256), matrix)
        value = value.reshape(count, rows_1, 128)
        target[pl.ds(first + 2, count)] = 2.0 * value if target is s1_ref else value

    first_row_1 = (iota(shape_1, 0) == own // 2) & at_y
    first_lane_1 = (iota(shape_1, 1) == 0) & at_z
    planes_1 = range(first + 2, first + 2 + count)

    def faces_1(p, carry):
        f10_ref[p] = jnp.where((p == 6) & at_x, 0.0, l10_ref[p])
        f11_ref[p] = jnp.where(first_row_1, 0.0, l11_ref[p])
        f12_ref[p] = jnp.where(first_lane_1, 0.0, l12_ref[p])
        return carry

    lax.fori_loop(planes_1.start, planes_1.stop, faces_1, 0, unroll=4)
    f10_ref[planes_1.stop] = jnp.zeros(shape_1, F32)

    def diagonals_1(p, carry):
        d = (
            4.0 * ABSORB + l10_ref[p] + f10_ref[p + 1]
            + l11_ref[p] + turn(f11_ref[p], -1, 0)
            + l12_ref[p] + turn(f12_ref[p], -1, 1)
        )
        w1_ref[p] = RELAX / d
        return carry

    lax.fori_loop(planes_1.start, planes_1.stop, diagonals_1, 0, unroll=4)
    if thin:
        pack_level_2(
            up_ref, down_ref, pay_ref, s1_ref, f10_ref, f11_ref, f12_ref, w1_ref, l10_ref, l11_ref, l12_ref, *refs
        )


def pack_level_2(
    up_ref, down_ref, pay_ref, s1_ref, f10_ref, f11_ref, f12_ref, w1_ref, l10_ref, l11_ref, l12_ref,
    sm1_ref, t1_ref, u_ref,
):
    for target, start in ((up_ref, 5), (down_ref, 9)):
        target[...] = jnp.zeros_like(target)
        for i, ref in enumerate((s1_ref, w1_ref, f10_ref)):
            for k in range(2):
                target[2 * i + k, pl.ds(4, 12), :] = ref[start + k, pl.ds(0, 12), :]
    for p in range(5, 11):
        sm1_ref[p] = w1_ref[p] * s1_ref[p]

    def quad(values, both):
        t1_ref[...] = values
        first = t1_ref[pl.ds(2, 4, 2), :]
        return first + t1_ref[pl.ds(3, 4, 2), :] if both else first

    def leftover_1(p):
        return KEEP * s1_ref[p] + neighbours(sm1_ref, f10_ref, f11_ref, f12_ref, p)

    row8, lane8 = iota((8, 128), 0), iota((8, 128), 1)
    narrow = one_hot(128, 128, lambda r, c: (lax.shift_right_logical(r, 1) == c) & (r < 64))
    narrow_even = one_hot(128, 128, lambda r, c: (r == 2 * c) & (r < 64))
    total = jnp.zeros((8, 128), F32)
    for f in range(4):
        for i in range(2):
            p = 6 + 2 * i
            if f == 0:
                part = quad(leftover_1(p) + leftover_1(p + 1), True)
            elif f == 1:
                part = quad(l10_ref[p], True)
            elif f == 2:
                part = quad(l11_ref[p] + l11_ref[p + 1], False)
            else:
                part = quad(l12_ref[p] + l12_ref[p + 1], True)
            u_ref[f, pl.ds(4 * i, 4), :] = part * (0.5 if f == 0 else 0.25)
        part = spread(u_ref[f], narrow_even if f == 3 else narrow)
        for i in range(2):
            for h in range(2):
                to = 32 * f + 16 * i
                moved = turn(turn(part, 4 * (h - i), 0), to - 16 * h, 1)
                here = (lax.shift_right_logical(row8, 2) == h) & (lane8 >= to) & (lane8 < to + 16)
                total = jnp.where(here, moved, total)
    pay_ref[...] = total


def window(pieces, to, lane):
    out = pieces[3]
    for k in range(3):
        start = (to + 16 * k) % 128
        here = (lane >= start) & (lane < start + 16)
        out = jnp.where(here, pieces[k], out)
    return jnp.where(lane < 64, turn(out, -to, 1), 0.0)


def solve_2(s2, level_2, level_3, t3_ref, e_ref):
    f0, f1, f2, w = level_2
    g0, g1, g2, w3 = level_3
    nx, ny, _ = s2.shape
    sm = w * s2
    left = KEEP * s2 + neighbours_3d(sm, f0, f1, f2)
    s3 = coarse_2(left.reshape(nx // 2, 2, ny, 128).sum(1), t3_ref, True, 0.5, False)
    e = w3 * s3
    for _ in range(SWEEPS - 1):
        e = KEEP * e + w3 * (s3 + neighbours_3d(e, g0, g1, g2))
    widen = one_hot(128, 128, lambda r, c: (r == lax.shift_right_logical(c, 1)) & (c < 64))
    wide = spread(e.reshape(nx * ny // 4, 128), widen).reshape(nx // 2, ny // 2, 128)
    for x in range(nx // 2):
        for i in range(2):
            e_ref[x, pl.ds(i, ny // 2, 2), :] = wide[x]
    e2 = e_ref[...]
    corrected = sm + jnp.concatenate([e2[:, None], e2[:, None]], 1).reshape(nx, ny, 128)
    return KEEP * corrected + w * (s2 + neighbours_3d(corrected, f0, f1, f2))


def coarse_2(values, t3_ref, both, weight, even):
    nx, ny, _ = values.shape
    t3_ref[...] = values
    first = t3_ref[:, pl.ds(0, ny // 2, 2), :]
    if both:
        first = first + t3_ref[:, pl.ds(1, ny // 2, 2), :]
    if even:
        rule = lambda r, c: (r == 2 * c) & (r < 64)
    else:
        rule = lambda r, c: (lax.shift_right_logical(r, 1) == c) & (r < 64)
    flat = spread(first.reshape(nx * ny // 2, 128), one_hot(128, 128, rule, weight))
    return flat.reshape(nx, ny // 2, 128)


def coefficients(low, mask_lane, absorb):
    shape = low[0].shape
    f0 = jnp.where(iota(shape, 0) == 0, 0.0, low[0])
    f1 = jnp.where(iota(shape, 1) == 0, 0.0, low[1])
    f2 = jnp.where((iota(shape, 2) == mask_lane) & (lax.axis_index("gz") == 0), 0.0, low[2])
    d = (
        absorb + low[0] + jnp.concatenate([f0[1:], jnp.zeros_like(f0[:1])], 0)
        + low[1] + turn(f1, -1, 1) + low[2] + turn(f2, -1, 2)
    )
    return f0, f1, f2, RELAX / d


def fetch_level_2(m2_ref, planes, pick_ref):
    gx, gy = lax.axis_index("gx"), lax.axis_index("gy")
    ny = m2_ref.shape[1]

    def source(c):
        return jnp.where(c < 96, 16, -48) + lax.shift_right_logical(c, 1)

    widen = one_hot(128, 128, lambda r, c: r == source(c))
    rows = one_hot(24, ny, lambda r, c: c == 4 * gy - 3 + lax.shift_right_logical(r, 1))
    for k in planes:
        pick_ref[k] = spread(pick(rows, m2_ref[2 * gx + k]), widen)


def widen_level_1(m1_ref, wide_ref, lo, hi):
    rows = 24 * (hi - lo)
    widen = one_hot(128, 256, lambda r, c: r == lax.shift_right_logical(c, 1))
    wide_ref[pl.ds(lo, hi - lo)] = spread(m1_ref[pl.ds(lo, hi - lo)].reshape(rows, 128), widen).reshape(
        hi - lo, 24, 256
    )


def double_rows(t_ref, wide_ref, q):
    for half in range(2):
        part = wide_ref[q, pl.ds(0, 20), pl.ds(128 * half, 128)]
        for i in range(2):
            t_ref[half, pl.ds(i, 20, 2), :] = part
    return jnp.concatenate([t_ref[0], t_ref[1]], 1)


def second_kernel(
    s_ref, f0_ref, f1_ref, f2_ref, w_ref, d_ref,
    s1_ref, f10_ref, f11_ref, f12_ref, w1_ref,
    low_ref, high_ref, before_ref, own0_ref, own1_ref, after_ref,
    fp_out, im_out, im_ref, t1s_ref, f20_ref, f21_ref, f22_ref, w2_ref,
    f30_ref, f31_ref, f32_ref, w3_ref, pay_ref,
    v_ref, t3_ref, e_ref, m2_ref, pick_ref, corr1_ref, m1_ref, wide_ref, t_ref,
    corr_ref, fp_ref, sm_ref, rs_ref, sm1_ref, tq_ref,
):
    nx2, ny2 = f20_ref.shape[:2]
    lane8 = iota((8, 128), 1)
    row8 = iota((8, 128), 0)

    def assemble(x, carry):
        for pair in range(ny2 // 8):
            g = x * (ny2 // 8) + pair
            pieces = [turn(ref[g], 16 * k, 1) for k, ref in enumerate((before_ref, own0_ref, own1_ref, after_ref))]
            for f in range(4):
                for i in range(2):
                    v_ref[f, 2 * x + i, pl.ds(8 * pair, 8), :] = window(pieces, 32 * f + 16 * i, lane8)
        return carry

    lax.fori_loop(0, nx2 // 2, assemble, 0, unroll=2)

    s2 = v_ref[0]
    low = (v_ref[1], v_ref[2], v_ref[3])
    level_2 = coefficients(low, 16, 16.0 * ABSORB)
    f20_ref[...], f21_ref[...], f22_ref[...], w2_ref[...] = level_2
    halves = [t.reshape(nx2 // 2, 2, ny2, 128) for t in low]
    low_3 = (
        coarse_2(halves[0][:, 0], t3_ref, True, 0.25, False),
        coarse_2(halves[1].sum(1), t3_ref, False, 0.25, False),
        coarse_2(halves[2].sum(1), t3_ref, True, 0.25, True),
    )
    level_3 = coefficients(low_3, 8, 64.0 * ABSORB)
    f30_ref[...], f31_ref[...], f32_ref[...], w3_ref[...] = level_3
    m2_ref[...] = jnp.zeros_like(m2_ref)
    m2_ref[pl.ds(3, nx2)] = solve_2(s2, level_2, level_3, t3_ref, e_ref)
    fetch_level_2(m2_ref, range(8), pick_ref)

    def correct_1(p, carry):
        corr1_ref[p] = w1_ref[p] * s1_ref[p] + pick_ref[lax.shift_right_logical(p, 1)]
        return carry

    lax.fori_loop(3, 13, correct_1, 0, unroll=5)
    for k in range(2):
        corr1_ref[1 + k] = low_ref[2 + k] * low_ref[k] + pick_ref[(1 + k) // 2]
        corr1_ref[13 + k] = high_ref[2 + k] * high_ref[k] + pick_ref[(13 + k) // 2]

    def relax_1(p, carry):
        m1_ref[p] = KEEP * corr1_ref[p] + w1_ref[p] * (
            s1_ref[p] + neighbours(corr1_ref, f10_ref, f11_ref, f12_ref, p)
        )
        return carry

    lax.fori_loop(3, 13, relax_1, 0, unroll=5)
    for p, source, w, face, next_face in (
        (2, low_ref[1], low_ref[3], low_ref[5], f10_ref[3]),
        (13, high_ref[0], high_ref[2], f10_ref[13], high_ref[5]),
    ):
        m1_ref[p] = KEEP * corr1_ref[p] + w * (
            source + face * corr1_ref[p - 1] + next_face * corr1_ref[p + 1]
            + plane_terms(corr1_ref[p], f11_ref[p], f12_ref[p])
        )
    widen_level_1(m1_ref, wide_ref, 2, 14)

    def correct(q, carry):
        e = double_rows(t_ref, wide_ref, q)
        for i in range(2):
            p = 2 * q + i - 4
            corr_ref[p] = w_ref[p] * s_ref[p] + e
        return carry

    lax.fori_loop(2, 14, correct, 0, unroll=2)

    def relax(p, carry):
        fp_ref[p] = KEEP * corr_ref[p] + w_ref[p] * (
            s_ref[p] + neighbours(corr_ref, f0_ref, f1_ref, f2_ref, p)
        )
        return carry

    lax.fori_loop(2, 22, relax, 0, unroll=4)

    def image(p, carry):
        im = d_ref[p] * fp_ref[p] - neighbours(fp_ref, f0_ref, f1_ref, f2_ref, p)
        im_ref[p] = im
        sm_ref[p] = w_ref[p] * im
        return carry

    lax.fori_loop(3, 21, image, 0, unroll=3)

    rs_ref[...] = jnp.zeros_like(rs_ref)
    inside = (iota((40, 128), 0) >= 12) & (iota((40, 128), 0) < 28)

    def leftovers(q, sums):
        total = jnp.zeros((40, 256), F32)
        for i in range(2):
            p = 2 * q + i - 4
            left = KEEP * im_ref[p] + neighbours(sm_ref, f0_ref, f1_ref, f2_ref, p)
            total += left
            own = jnp.where(inside & (p >= 8) & (p < 16), 1.0, 0.0)
            fp, im = fp_ref[p, :, 0:128], im_ref[p, :, 0:128]
            sums = (
                sums[0] + own * s_ref[p, :, 0:128] * fp,
                sums[1] + own * fp * im,
                sums[2] + own * sm_ref[p, :, 0:128] * (im + left[:, 0:128]),
            )
        put_rows(rs_ref, q - 4, row_pairs(t_ref, total, True))
        return sums

    zero = jnp.zeros((40, 128), F32)
    sums = lax.fori_loop(4, 12, leftovers, (zero, zero, zero), unroll=2)

    for p in range(8):
        fp_out[p] = fp_ref[8 + p, pl.ds(12, 16), 0:128]
        im_out[p] = im_ref[8 + p, pl.ds(12, 16), 0:128]

    pairs = one_hot(256, 128, lambda r, c: lax.shift_right_logical(r, 1) == c, 0.5)
    t1s_ref[...] = jnp.zeros_like(t1s_ref)
    t1s_ref[pl.ds(4, 8)] = spread(rs_ref[...].reshape(192, 256), pairs).reshape(8, 24, 128)
    for p in range(5, 11):
        sm1_ref[p] = w1_ref[p] * t1s_ref[p]
    inside_1 = jnp.where(
        (iota((24, 128), 0) >= 6) & (iota((24, 128), 0) < 14) & (iota((24, 128), 1) < 64), 1.0, 0.0
    )
    second = jnp.zeros((24, 128), F32)
    halves = [jnp.zeros((8, 128), F32)] * 2
    tq_ref[...] = jnp.zeros_like(tq_ref)
    for i in range(2):
        total = jnp.zeros((24, 128), F32)
        for j in range(2):
            p = 6 + 2 * i + j
            s1 = t1s_ref[p]
            left = KEEP * s1 + neighbours(sm1_ref, f10_ref, f11_ref, f12_ref, p)
            second += inside_1 * sm1_ref[p] * (s1 + left)
            total += left
        tq_ref[pl.ds(0, 24), :] = total
        tq_ref[pl.ds(24, 4), :] = tq_ref[pl.ds(6, 4, 2), :] + tq_ref[pl.ds(7, 4, 2), :]
        for h in range(2):
            place = one_hot(
                128, 128,
                lambda r, c, i=i, h=h: (lax.shift_right_logical(r, 1) - 16 * h == (c & 15))
                & (r < 64) & ((lax.shift_right_logical(c, 4) & 1) == i), 0.5,
            )
            halves[h] += spread(tq_ref[pl.ds(24, 8), :], place)
    scalars = (jnp.sum(sums[0]), jnp.sum(sums[1]), jnp.sum(sums[2]) + 2.0 * jnp.sum(second))
    mine = lax.shift_right_logical(lane8, 5) == row8
    pay = jnp.zeros((8, 128), F32)
    for h in range(2):
        line = jnp.sum(jnp.where(mine, halves[h], 0.0), axis=0, keepdims=True)
        pay = jnp.where(row8 == h, line, pay)
    for k, value in enumerate(scalars):
        pay = jnp.where((lane8 == k) & (row8 == 2), value, pay)
    pay_ref[...] = pay[:4]


def third_kernel(
    f0_ref, f1_ref, f2_ref, w_ref, f10_ref, f11_ref, f12_ref, w1_ref,
    im_ref, t1s_ref, f20_ref, f21_ref, f22_ref, w2_ref, f30_ref, f31_ref, f32_ref, w3_ref,
    before_ref, own0_ref, own1_ref, after_ref, parts_ref,
    mi_out, scalar_out,
    v_ref, t3_ref, e_ref, m2_ref, pick_ref, corr1_ref, m1_ref, wide_ref, t_ref, corr_ref,
):
    nx2, ny2 = f20_ref.shape[:2]
    lane = iota((ny2 // 4, 128), 1)

    def assemble(x, carry):
        pieces = [turn(ref[x], 16 * k, 1) for k, ref in enumerate((before_ref, own0_ref, own1_ref, after_ref))]
        for i in range(2):
            for j in range(4):
                v_ref[2 * x + i, pl.ds(j, ny2 // 4, 4), :] = window(pieces, 32 * j + 16 * i, lane)
        return carry

    lax.fori_loop(0, nx2 // 2, assemble, 0, unroll=2)
    s2 = v_ref[...]
    level_2 = (f20_ref[...], f21_ref[...], f22_ref[...], w2_ref[...])
    level_3 = (f30_ref[...], f31_ref[...], f32_ref[...], w3_ref[...])
    m2 = solve_2(s2, level_2, level_3, t3_ref, e_ref)
    lane3 = iota(s2.shape, 2)
    part = 4.0 * jnp.sum(jnp.where((lane3 >= 16) & (lane3 < 48), s2 * m2, 0.0))
    sums = jnp.sum(jnp.sum(parts_ref[...], axis=0), axis=0, keepdims=True)
    scalar_out[...] = jnp.where(iota((1, 128), 1) == 3, part, sums)
    m2_ref[...] = jnp.zeros_like(m2_ref)
    m2_ref[pl.ds(3, nx2)] = m2
    fetch_level_2(m2_ref, range(2, 6), pick_ref)

    for p in range(4, 12):
        corr1_ref[p] = w1_ref[p] * t1s_ref[p] + pick_ref[p // 2]
    for p in range(5, 11):
        m1_ref[p] = KEEP * corr1_ref[p] + w1_ref[p] * (
            t1s_ref[p] + neighbours(corr1_ref, f10_ref, f11_ref, f12_ref, p)
        )
    widen_level_1(m1_ref, wide_ref, 5, 11)

    def correct(q, carry):
        e = double_rows(t_ref, wide_ref, q)
        for i in range(2):
            p = 2 * q + i - 4
            corr_ref[p] = w_ref[p] * im_ref[p] + e
        return carry

    lax.fori_loop(5, 11, correct, 0, unroll=2)

    for p in range(8):
        q = 8 + p
        mi = KEEP * corr_ref[q] + w_ref[q] * (
            im_ref[q] + neighbours(corr_ref, f0_ref, f1_ref, f2_ref, q)
        )
        t_ref[0] = mi[:, 0:128]
        mi_out[p] = t_ref[0, pl.ds(12, 16), :]


def last_kernel(sums_ref, s_ref, fp_ref, im_ref, mi_ref, solution_ref, residual_ref, direction_ref):
    total = jnp.sum(sums_ref[...], axis=0)
    lane = iota((1, 128), 1)

    def value(lanes):
        keep = lane == lanes[0]
        for k in lanes[1:]:
            keep = keep | (lane == k)
        return jnp.sum(jnp.where(keep, total, 0.0), axis=1, keepdims=True)

    projected, curvature, product = value((0,)), value((1,)), value((2, 3))
    step = projected / curvature
    share = product / curvature
    for p in range(8):
        fp = fp_ref[p]
        solution_ref[p] = step * fp
        residual_ref[p] = s_ref[p] - step * im_ref[p]
        direction_ref[p] = step * (share * fp - mi_ref[p])


def call(kernel, inputs, outs, scratch=(), keep_in=(), keep_out=(), space=pltpu.VMEM):
    vmem = pl.BlockSpec(memory_space=pltpu.VMEM)
    inputs = [
        pltpu.with_memory_space_constraint(value, space) if i in keep_in else value
        for i, value in enumerate(inputs)
    ]
    shapes = [
        pltpu.VMEM(shape, dtype) if i in keep_out else jax.ShapeDtypeStruct(shape, dtype)
        for i, (shape, dtype) in enumerate(outs)
    ]
    return pl.pallas_call(
        kernel,
        out_shape=shapes,
        in_specs=[pl.BlockSpec(memory_space=space)] * len(inputs),
        out_specs=[vmem] * len(outs),
        scratch_shapes=[pltpu.VMEM(shape, F32) if isinstance(shape, tuple) else shape for shape in scratch],
        compiler_params=pltpu.CompilerParams(vmem_limit_bytes=VMEM_LIMIT),
    )(*inputs)


def shift_along(value, axis, by):
    size = lax.axis_size(axis)
    return lax.ppermute(value, axis, [(i, i + by) for i in range(size) if 0 <= i + by < size])


def gather_plane(value):
    peers = lax.axis_size(("gx", "gy"))
    copies = jnp.broadcast_to(value.reshape(1, 1, -1), (peers, 1, value.size))
    return lax.all_to_all(copies, ("gx", "gy"), 0, 0, tiled=True)


def local(right_side, face_coefficients, solid):
    nx2, ny2 = 2 * lax.axis_size("gx"), 4 * lax.axis_size("gy")
    own, ends = call(
        prepare_kernel,
        [right_side, face_coefficients, solid],
        [((8, 5, 16, 128), BF16), ((8, 16, 128), BF16)],
        [
            (8, 16, 128),
            pltpu.VMEM((3, 8, 16, 128), BF16),
            pltpu.VMEM((8, 16, 128), jnp.int32),
            pltpu.SemaphoreType.DMA((3,)),
        ],
        keep_in=range(3),
        space=pltpu.HBM,
    )
    before, after = shift_along(ends, "gz", 1), shift_along(ends, "gz", -1)
    (own,) = call(rim_kernel, [own, before, after], [((8, 6, 16, 128), BF16)])
    block = jnp.concatenate([shift_along(own, "gx", 1), own, shift_along(own, "gx", -1)], axis=0)
    before, after = shift_along(block, "gy", 1), shift_along(block, "gy", -1)

    fine, fine_up = (24, 40, 256), (25, 40, 256)
    mid, mid_up = (16, 24, 128), (17, 24, 128)
    rows, wide, edge = (12, 24, 256), (16, 24, 256), (6, 24, 128)
    slim, slim_up, slim_mid, slim_mid_up, slim_rows = (
        (20, 24, 256), (21, 24, 256), (16, 16, 128), (17, 16, 128), (12, 16, 256)
    )
    up, down, pay = call(
        functools.partial(fine_kernel, True),
        [block, before, after],
        [(edge, F32), (edge, F32), ((8, 128), F32)],
        [slim, slim_up, slim, slim, slim_mid, slim_mid_up, slim_mid, slim_mid, slim_mid,
         slim, slim, slim, slim, (2, 24, 128), slim_rows, slim_rows, slim_rows, slim_rows,
         slim_mid, slim_mid, slim_mid, slim_mid, (16, 128), (4, 8, 128)],
    )
    state = call(
        functools.partial(fine_kernel, False),
        [block, before, after],
        [(shape, F32) for shape in (fine, fine_up, fine, fine, fine, fine, mid, mid_up, mid, mid, mid)],
        [fine, fine, fine, fine, (2, 40, 128), rows, rows, rows, rows, mid, mid, mid],
        keep_out=range(11),
    )
    low, high = shift_along(up, "gx", 1), shift_along(down, "gx", -1)
    own = gather_plane(pay)
    pairs = (nx2 * ny2 // 16, 8, 128)
    own, low, high = lax.optimization_barrier((own, low, high))
    own0, own1 = own[..., :512].reshape(pairs), own[..., 512:].reshape(pairs)
    before, after = shift_along(own1, "gz", 1), shift_along(own0, "gz", -1)
    level_2, level_3 = (nx2, ny2, 128), (nx2 // 2, ny2 // 2, 128)
    window = (nx2 + 6, ny2, 128)
    half = (nx2 // 2, ny2, 128)
    first_pre, image, *more, pay = call(
        second_kernel,
        [*state, low, high, before, own0, own1, after],
        [((8, 16, 128), F32)] * 2
        + [(shape, F32) for shape in (fine, mid, *[level_2] * 4, *[level_3] * 4, (4, 128))],
        [(4,) + level_2, half, half, window, (8, 24, 128), mid, mid, wide, (2, 40, 128),
         fine, fine, fine, (8, 24, 256), mid, (32, 128)],
        keep_in=range(11),
        keep_out=range(2, 12),
    )
    own = gather_plane(pay)
    plane = (nx2 // 2, ny2 // 4, 128)
    own0, own1, parts = (own[..., 128 * k : 128 * k + 128].reshape(plane) for k in range(3))
    before, after = shift_along(own1, "gz", 1), shift_along(own0, "gz", -1)
    _, f0, f1, f2, w, _, _, f10, f11, f12, w1 = state
    mapped, sums = call(
        third_kernel,
        [f0, f1, f2, w, f10, f11, f12, w1, *more, before, own0, own1, after, parts],
        [((8, 16, 128), F32), ((1, 128), F32)],
        [level_2, half, half, window, (8, 24, 128), mid, mid, wide, (2, 40, 128), fine],
        keep_in=range(18),
    )
    peers = lax.axis_size("gz")
    sums = lax.all_to_all(jnp.broadcast_to(sums[None], (peers, 1, 128)), "gz", 0, 0, tiled=True)
    return tuple(
        call(
            last_kernel,
            [sums, right_side, first_pre, image, mapped],
            [((8, 16, 128), F32)] * 3,
        )
    )


def solution(mesh):
    placed = P("gx", "gy", "gz")
    return jax.shard_map(
        local,
        mesh=mesh,
        in_specs=(placed, P(None, "gx", "gy", "gz"), placed),
        out_specs=(placed, placed, placed),
        check_vma=False,
    )
```

```python
import functools

import jax
import jax.numpy as jnp
from jax import lax
from jax.experimental import pallas as pl
from jax.experimental.pallas import tpu as pltpu
from jax.sharding import PartitionSpec as P

F32 = jnp.float32
BF16 = jnp.bfloat16
ABSORB = 0.001
RELAX = 0.8
KEEP = 0.2
SWEEPS = 6
VMEM_LIMIT = 24 * 1024 * 1024


def one_hot(rows, cols, rule, weight=1.0):
    r = lax.broadcasted_iota(jnp.int32, (rows, cols), 0)
    c = lax.broadcasted_iota(jnp.int32, (rows, cols), 1)
    return jnp.where(rule(r, c), weight, 0.0).astype(BF16)


def spread(values, matrix):
    high = values.astype(BF16)
    low = (values - high.astype(F32)).astype(BF16)
    return jnp.dot(high, matrix, preferred_element_type=F32) + jnp.dot(
        low, matrix, preferred_element_type=F32
    )


def pick(matrix, values):
    high = values.astype(BF16)
    low = (values - high.astype(F32)).astype(BF16)
    return jnp.dot(matrix, high, preferred_element_type=F32) + jnp.dot(
        matrix, low, preferred_element_type=F32
    )


def root(values):
    return values * lax.rsqrt(jnp.maximum(values, 1e-12))


def turn(values, shift, axis):
    return pltpu.roll(values, shift % values.shape[axis], axis)


def iota(shape, dim):
    return lax.broadcasted_iota(jnp.int32, shape, dim)


def plane_terms(v, f1, f2):
    return turn(v, 1, 0) * f1 + turn(v * f1, -1, 0) + turn(v, 1, 1) * f2 + turn(v * f2, -1, 1)


def neighbours(v_ref, f0_ref, f1_ref, f2_ref, p):
    return (
        f0_ref[p] * v_ref[p - 1]
        + f0_ref[p + 1] * v_ref[p + 1]
        + plane_terms(v_ref[p], f1_ref[p], f2_ref[p])
    )


def neighbours_3d(v, f0, f1, f2):
    zero = jnp.zeros_like(v[:1])
    up = f0 * v
    return (
        f0 * jnp.concatenate([zero, v[:-1]], 0)
        + jnp.concatenate([up[1:], zero], 0)
        + turn(v, 1, 1) * f1
        + turn(v * f1, -1, 1)
        + turn(v, 1, 2) * f2
        + turn(v * f2, -1, 2)
    )


def row_pairs(t_ref, values, both):
    out = []
    pairs = values.shape[0] // 2
    for half in range(2):
        t_ref[half] = values[:, 128 * half : 128 * half + 128]
        first = t_ref[half, pl.ds(0, pairs, 2), :]
        out.append(first + t_ref[half, pl.ds(1, pairs, 2), :] if both else first)
    return out


def put_rows(r_ref, q, halves):
    for half in range(2):
        r_ref[q, pl.ds(0, halves[half].shape[0]), pl.ds(128 * half, 128)] = halves[half]


def prepare_kernel(s_hbm, fc_hbm, solid_hbm, out_ref, ends_ref, s_ref, fc_ref, solid_ref, sems):
    copies = [
        pltpu.make_async_copy(source, target, sems.at[i])
        for i, (source, target) in enumerate(
            ((s_hbm, s_ref), (fc_hbm, fc_ref), (solid_hbm, solid_ref))
        )
    ]
    for copy in copies:
        copy.start()
    for copy in copies:
        copy.wait()
    s = s_ref[...]
    high = s.astype(BF16)
    out_ref[:, 0] = high
    out_ref[:, 1] = (s - high.astype(F32)).astype(BF16)
    weight = 1.0 - 0.75 * solid_ref[...].astype(F32)
    for a in range(3):
        out_ref[:, 2 + a] = (fc_ref[a].astype(F32) * weight).astype(BF16)
    lane = iota((16, 128), 1)

    def body(p, carry):
        ends = jnp.zeros((16, 128), F32)
        for f in range(5):
            t = turn(out_ref[p, f].astype(F32), 24 * f + 12, 1)
            ends = jnp.where((lane >= 24 * f) & (lane < 24 * f + 24), t, ends)
        ends_ref[p] = ends.astype(BF16)
        return carry

    lax.fori_loop(0, 8, body, 0, unroll=4)


def rim_kernel(own_ref, before_ref, after_ref, out_ref):
    lane = iota((8, 16, 128), 2)
    last = jnp.zeros((8, 16, 128), jnp.bool_)
    for f in range(5):
        last = last | ((lane >= 24 * f) & (lane < 24 * f + 12))
    out_ref[:, 0:5] = own_ref[...]
    rim = jnp.where(last, before_ref[...].astype(F32), after_ref[...].astype(F32))
    out_ref[:, 5] = rim.astype(BF16)


def edges_kernel(x_ref, up_ref, down_ref):
    row = iota((8, 128), 0)
    quarters = [(p, True) for p in range(5, 19)] + [(0, False), (23, False)]

    def body(f, carry):
        for t in range(11):
            pair = [x_ref[1 + 2 * t + k, f].astype(F32) for k in range(2)]
            up_ref[t, f] = jnp.concatenate([v[8:] for v in pair], 0).astype(BF16)
            down_ref[t, f] = jnp.concatenate([v[:8] for v in pair], 0).astype(BF16)
        for t in range(4):
            ups, downs = [], []
            for k in range(0, 4, 2):
                pair = []
                for p, inner in quarters[4 * t + k : 4 * t + k + 2]:
                    v = x_ref[p, f].astype(F32)
                    pair.append((v[:8], v[8:]) if inner else (v[8:], v[:8]))
                ups.append(jnp.where(row < 4, turn(pair[0][0], 4, 0), pair[1][0]))
                downs.append(jnp.where(row < 4, pair[0][1], turn(pair[1][1], 4, 0)))
            up_ref[11 + t, f] = jnp.concatenate(ups, 0).astype(BF16)
            down_ref[11 + t, f] = jnp.concatenate(downs, 0).astype(BF16)
        return carry

    lax.fori_loop(0, 6, body, 0)


def edge_rows(ym_ref, yp_ref, p, f, thin):
    row = iota((8, 128), 0)
    zero = jnp.zeros((8, 128), F32)

    def eight(ref, tile, k):
        return ref[tile, f].astype(F32)[8 * k : 8 * k + 8]

    def four(q, before):
        v = eight(ym_ref if before else yp_ref, 11 + q // 4, q % 4 // 2)
        moved = turn(v, 4, 0) if (q % 2 == 0) == before else v
        return jnp.where((row >= 4) == before, moved, 0.0)

    if p in (0, 23):
        q = 14 if p == 0 else 15
        near_before, near_after = four(q, True), four(q, False)
    else:
        near_before, near_after = (eight(ref, (p - 1) // 2, (p - 1) % 2) for ref in (ym_ref, yp_ref))
    if thin:
        return near_before, near_after
    if 5 <= p <= 18:
        far_before, far_after = four(p - 5, True), four(p - 5, False)
    else:
        far_before = far_after = zero
    return jnp.concatenate([far_before, near_before], 0), jnp.concatenate([near_after, far_after], 0)


def fine_kernel(thin, x_ref, ym_ref, yp_ref, *refs):
    if thin:
        (up_ref, down_ref, pay_ref,
         s_ref, f0_ref, f1_ref, f2_ref, s1_ref, f10_ref, f11_ref, f12_ref, w1_ref, *refs) = refs
    else:
        s_ref, f0_ref, f1_ref, f2_ref, w_ref, d_ref, s1_ref, f10_ref, f11_ref, f12_ref, w1_ref, *refs = refs
    (c0_ref, c1_ref, c2_ref, sm_ref, t_ref, r0_ref, r1_ref, r2_ref, rs_ref,
     l10_ref, l11_ref, l12_ref, *refs) = refs
    planes = range(4, 20) if thin else range(24)
    rows, rows_1 = s_ref.shape[1], s1_ref.shape[1]
    own = 4 if thin else 12
    shape, shape_1 = (rows, 256), (rows_1, 128)
    at_x = lax.axis_index("gx") == 0
    at_y = lax.axis_index("gy") == 0
    at_z = lax.axis_index("gz") == 0
    lane = iota((rows, 128), 1)
    side = (lane < 12) | (lane >= 116)

    for p in planes:
        tiles = []
        for f in range(6):
            before, after = edge_rows(ym_ref, yp_ref, p, f, thin)
            column = jnp.concatenate([before, x_ref[p, f].astype(F32), after], 0)
            tiles.append(turn(column, -4, 0)[:rows])
        rims = [
            jnp.where(side, turn(tiles[5], -(24 * f + 12), 1), 0.0) for f in range(5)
        ]
        s_ref[p, :, 0:128] = tiles[0] + tiles[1]
        s_ref[p, :, 128:256] = rims[0] + rims[1]
        for a, c_ref in enumerate((c0_ref, c1_ref, c2_ref)):
            c_ref[p, :, 0:128] = tiles[2 + a]
            c_ref[p, :, 128:256] = rims[2 + a]

    def faces(p, carry):
        before = jnp.maximum(p - 1, planes.start)
        f0_ref[p] = root(c0_ref[p] * c0_ref[before])
        c1 = c1_ref[p]
        f1_ref[p] = root(c1 * turn(c1, 1, 0))
        c2 = c2_ref[p]
        f2_ref[p] = root(c2 * turn(c2, 1, 1))
        return carry

    lax.fori_loop(planes.start, planes.stop, faces, 0, unroll=4)
    f0_ref[planes.stop] = jnp.zeros(shape, F32)

    first_row = (iota(shape, 0) == own) & at_y
    first_lane = (iota(shape, 1) == 0) & at_z
    for ref in (r0_ref, r1_ref, r2_ref, rs_ref):
        ref[...] = jnp.zeros_like(ref)

    def diagonals(q, carry):
        lows = []
        for i in range(2):
            p = 2 * q + i
            f0, f1, f2 = f0_ref[p], f1_ref[p], f2_ref[p]
            low0 = f0 + jnp.where((p == 8) & at_x, c0_ref[p], 0.0)
            low1 = f1 + jnp.where(first_row, c1_ref[p], 0.0)
            low2 = f2 + jnp.where(first_lane, c2_ref[p], 0.0)
            d = ABSORB + low0 + f0_ref[p + 1] + low1 + turn(f1, -1, 0) + low2 + turn(f2, -1, 1)
            w = RELAX / d
            if not thin:
                d_ref[p] = d
                w_ref[p] = w
            sm_ref[p] = w * s_ref[p]
            lows.append((low0, low1, low2))
        put_rows(r0_ref, q, row_pairs(t_ref, lows[0][0], True))
        put_rows(r1_ref, q, row_pairs(t_ref, lows[0][1] + lows[1][1], False))
        put_rows(r2_ref, q, row_pairs(t_ref, lows[0][2] + lows[1][2], True))
        return carry

    lax.fori_loop(planes.start // 2, planes.stop // 2, diagonals, 0, unroll=2)

    def leftovers(q, carry):
        total = jnp.zeros(shape, F32)
        for i in range(2):
            p = 2 * q + i
            total += KEEP * s_ref[p] + neighbours(sm_ref, f0_ref, f1_ref, f2_ref, p)
        put_rows(rs_ref, q, row_pairs(t_ref, total, True))
        return carry

    lax.fori_loop(planes.start // 2 + 1, planes.stop // 2 - 1, leftovers, 0, unroll=2)

    pairs = one_hot(256, 128, lambda r, c: lax.shift_right_logical(r, 1) == c, 0.25)
    evens = one_hot(256, 128, lambda r, c: r == 2 * c, 0.25)
    first, count = planes.start // 2, len(planes) // 2
    for target, source, matrix in (
        (l10_ref, r0_ref, pairs), (l11_ref, r1_ref, pairs), (l12_ref, r2_ref, evens), (s1_ref, rs_ref, pairs)
    ):
        target[...] = jnp.zeros_like(target)
        value = spread(source[pl.ds(first, count)].reshape(count * rows_1, 256), matrix)
        value = value.reshape(count, rows_1, 128)
        target[pl.ds(first + 2, count)] = 2.0 * value if target is s1_ref else value

    first_row_1 = (iota(shape_1, 0) == own // 2) & at_y
    first_lane_1 = (iota(shape_1, 1) == 0) & at_z
    planes_1 = range(first + 2, first + 2 + count)

    def faces_1(p, carry):
        f10_ref[p] = jnp.where((p == 6) & at_x, 0.0, l10_ref[p])
        f11_ref[p] = jnp.where(first_row_1, 0.0, l11_ref[p])
        f12_ref[p] = jnp.where(first_lane_1, 0.0, l12_ref[p])
        return carry

    lax.fori_loop(planes_1.start, planes_1.stop, faces_1, 0, unroll=4)
    f10_ref[planes_1.stop] = jnp.zeros(shape_1, F32)

    def diagonals_1(p, carry):
        d = (
            4.0 * ABSORB + l10_ref[p] + f10_ref[p + 1]
            + l11_ref[p] + turn(f11_ref[p], -1, 0)
            + l12_ref[p] + turn(f12_ref[p], -1, 1)
        )
        w1_ref[p] = RELAX / d
        return carry

    lax.fori_loop(planes_1.start, planes_1.stop, diagonals_1, 0, unroll=4)
    if thin:
        pack_level_2(
            up_ref, down_ref, pay_ref, s1_ref, f10_ref, f11_ref, f12_ref, w1_ref, l10_ref, l11_ref, l12_ref, *refs
        )


def pack_level_2(
    up_ref, down_ref, pay_ref, s1_ref, f10_ref, f11_ref, f12_ref, w1_ref, l10_ref, l11_ref, l12_ref,
    sm1_ref, t1_ref, u_ref,
):
    for target, start in ((up_ref, 5), (down_ref, 9)):
        target[...] = jnp.zeros_like(target)
        for i, ref in enumerate((s1_ref, w1_ref, f10_ref)):
            for k in range(2):
                target[2 * i + k, pl.ds(4, 12), :] = ref[start + k, pl.ds(0, 12), :]
    for p in range(5, 11):
        sm1_ref[p] = w1_ref[p] * s1_ref[p]

    def quad(values, both):
        t1_ref[...] = values
        first = t1_ref[pl.ds(2, 4, 2), :]
        return first + t1_ref[pl.ds(3, 4, 2), :] if both else first

    def leftover_1(p):
        return KEEP * s1_ref[p] + neighbours(sm1_ref, f10_ref, f11_ref, f12_ref, p)

    row8, lane8 = iota((8, 128), 0), iota((8, 128), 1)
    narrow = one_hot(128, 128, lambda r, c: (lax.shift_right_logical(r, 1) == c) & (r < 64))
    narrow_even = one_hot(128, 128, lambda r, c: (r == 2 * c) & (r < 64))
    total = jnp.zeros((8, 128), F32)
    for f in range(4):
        for i in range(2):
            p = 6 + 2 * i
            if f == 0:
                part = quad(leftover_1(p) + leftover_1(p + 1), True)
            elif f == 1:
                part = quad(l10_ref[p], True)
            elif f == 2:
                part = quad(l11_ref[p] + l11_ref[p + 1], False)
            else:
                part = quad(l12_ref[p] + l12_ref[p + 1], True)
            u_ref[f, pl.ds(4 * i, 4), :] = part * (0.5 if f == 0 else 0.25)
        part = spread(u_ref[f], narrow_even if f == 3 else narrow)
        for i in range(2):
            for h in range(2):
                to = 32 * f + 16 * i
                moved = turn(turn(part, 4 * (h - i), 0), to - 16 * h, 1)
                here = (lax.shift_right_logical(row8, 2) == h) & (lane8 >= to) & (lane8 < to + 16)
                total = jnp.where(here, moved, total)
    pay_ref[...] = jnp.broadcast_to(total[None], pay_ref.shape)


def window(pieces, to, lane):
    out = pieces[3]
    for k in range(3):
        start = (to + 16 * k) % 128
        here = (lane >= start) & (lane < start + 16)
        out = jnp.where(here, pieces[k], out)
    return jnp.where(lane < 64, turn(out, -to, 1), 0.0)


def solve_2(s2, level_2, level_3, t3_ref, e_ref):
    f0, f1, f2, w = level_2
    g0, g1, g2, w3 = level_3
    nx, ny, _ = s2.shape
    sm = w * s2
    left = KEEP * s2 + neighbours_3d(sm, f0, f1, f2)
    s3 = coarse_2(left.reshape(nx // 2, 2, ny, 128).sum(1), t3_ref, True, 0.5, False)
    e = w3 * s3
    for _ in range(SWEEPS - 1):
        e = KEEP * e + w3 * (s3 + neighbours_3d(e, g0, g1, g2))
    widen = one_hot(128, 128, lambda r, c: (r == lax.shift_right_logical(c, 1)) & (c < 64))
    wide = spread(e.reshape(nx * ny // 4, 128), widen).reshape(nx // 2, ny // 2, 128)
    for x in range(nx // 2):
        for i in range(2):
            e_ref[x, pl.ds(i, ny // 2, 2), :] = wide[x]
    e2 = e_ref[...]
    corrected = sm + jnp.concatenate([e2[:, None], e2[:, None]], 1).reshape(nx, ny, 128)
    return KEEP * corrected + w * (s2 + neighbours_3d(corrected, f0, f1, f2))


def coarse_2(values, t3_ref, both, weight, even):
    nx, ny, _ = values.shape
    t3_ref[...] = values
    first = t3_ref[:, pl.ds(0, ny // 2, 2), :]
    if both:
        first = first + t3_ref[:, pl.ds(1, ny // 2, 2), :]
    if even:
        rule = lambda r, c: (r == 2 * c) & (r < 64)
    else:
        rule = lambda r, c: (lax.shift_right_logical(r, 1) == c) & (r < 64)
    flat = spread(first.reshape(nx * ny // 2, 128), one_hot(128, 128, rule, weight))
    return flat.reshape(nx, ny // 2, 128)


def coefficients(low, mask_lane, absorb):
    shape = low[0].shape
    f0 = jnp.where(iota(shape, 0) == 0, 0.0, low[0])
    f1 = jnp.where(iota(shape, 1) == 0, 0.0, low[1])
    f2 = jnp.where((iota(shape, 2) == mask_lane) & (lax.axis_index("gz") == 0), 0.0, low[2])
    d = (
        absorb + low[0] + jnp.concatenate([f0[1:], jnp.zeros_like(f0[:1])], 0)
        + low[1] + turn(f1, -1, 1) + low[2] + turn(f2, -1, 2)
    )
    return f0, f1, f2, RELAX / d


def fetch_level_2(m2_ref, planes, pick_ref):
    gx, gy = lax.axis_index("gx"), lax.axis_index("gy")
    ny = m2_ref.shape[1]

    def source(c):
        return jnp.where(c < 96, 16, -48) + lax.shift_right_logical(c, 1)

    widen = one_hot(128, 128, lambda r, c: r == source(c))
    rows = one_hot(24, ny, lambda r, c: c == 4 * gy - 3 + lax.shift_right_logical(r, 1))
    for k in planes:
        pick_ref[k] = spread(pick(rows, m2_ref[2 * gx + k]), widen)


def widen_level_1(m1_ref, wide_ref, lo, hi):
    rows = 24 * (hi - lo)
    widen = one_hot(128, 256, lambda r, c: r == lax.shift_right_logical(c, 1))
    wide_ref[pl.ds(lo, hi - lo)] = spread(m1_ref[pl.ds(lo, hi - lo)].reshape(rows, 128), widen).reshape(
        hi - lo, 24, 256
    )


def double_rows(t_ref, wide_ref, q):
    for half in range(2):
        part = wide_ref[q, pl.ds(0, 20), pl.ds(128 * half, 128)]
        for i in range(2):
            t_ref[half, pl.ds(i, 20, 2), :] = part
    return jnp.concatenate([t_ref[0], t_ref[1]], 1)


def second_kernel(
    s_ref, f0_ref, f1_ref, f2_ref, w_ref, d_ref,
    s1_ref, f10_ref, f11_ref, f12_ref, w1_ref,
    low_ref, high_ref, before_ref, own0_ref, own1_ref, after_ref,
    fp_out, im_out, im_ref, t1s_ref, f20_ref, f21_ref, f22_ref, w2_ref,
    f30_ref, f31_ref, f32_ref, w3_ref, pay_ref,
    v_ref, t3_ref, e_ref, m2_ref, pick_ref, corr1_ref, m1_ref, wide_ref, t_ref,
    corr_ref, fp_ref, sm_ref, rs_ref, sm1_ref, tq_ref,
):
    nx2, ny2 = f20_ref.shape[:2]
    lane8 = iota((8, 128), 1)
    row8 = iota((8, 128), 0)

    def assemble(x, carry):
        for pair in range(ny2 // 8):
            g = x * (ny2 // 8) + pair
            pieces = [turn(ref[g], 16 * k, 1) for k, ref in enumerate((before_ref, own0_ref, own1_ref, after_ref))]
            for f in range(4):
                for i in range(2):
                    v_ref[f, 2 * x + i, pl.ds(8 * pair, 8), :] = window(pieces, 32 * f + 16 * i, lane8)
        return carry

    lax.fori_loop(0, nx2 // 2, assemble, 0, unroll=2)

    s2 = v_ref[0]
    low = (v_ref[1], v_ref[2], v_ref[3])
    level_2 = coefficients(low, 16, 16.0 * ABSORB)
    f20_ref[...], f21_ref[...], f22_ref[...], w2_ref[...] = level_2
    halves = [t.reshape(nx2 // 2, 2, ny2, 128) for t in low]
    low_3 = (
        coarse_2(halves[0][:, 0], t3_ref, True, 0.25, False),
        coarse_2(halves[1].sum(1), t3_ref, False, 0.25, False),
        coarse_2(halves[2].sum(1), t3_ref, True, 0.25, True),
    )
    level_3 = coefficients(low_3, 8, 64.0 * ABSORB)
    f30_ref[...], f31_ref[...], f32_ref[...], w3_ref[...] = level_3
    m2_ref[...] = jnp.zeros_like(m2_ref)
    m2_ref[pl.ds(3, nx2)] = solve_2(s2, level_2, level_3, t3_ref, e_ref)
    fetch_level_2(m2_ref, range(8), pick_ref)

    def correct_1(p, carry):
        corr1_ref[p] = w1_ref[p] * s1_ref[p] + pick_ref[lax.shift_right_logical(p, 1)]
        return carry

    lax.fori_loop(3, 13, correct_1, 0, unroll=5)
    for k in range(2):
        corr1_ref[1 + k] = low_ref[2 + k] * low_ref[k] + pick_ref[(1 + k) // 2]
        corr1_ref[13 + k] = high_ref[2 + k] * high_ref[k] + pick_ref[(13 + k) // 2]

    def relax_1(p, carry):
        m1_ref[p] = KEEP * corr1_ref[p] + w1_ref[p] * (
            s1_ref[p] + neighbours(corr1_ref, f10_ref, f11_ref, f12_ref, p)
        )
        return carry

    lax.fori_loop(3, 13, relax_1, 0, unroll=5)
    for p, source, w, face, next_face in (
        (2, low_ref[1], low_ref[3], low_ref[5], f10_ref[3]),
        (13, high_ref[0], high_ref[2], f10_ref[13], high_ref[5]),
    ):
        m1_ref[p] = KEEP * corr1_ref[p] + w * (
            source + face * corr1_ref[p - 1] + next_face * corr1_ref[p + 1]
            + plane_terms(corr1_ref[p], f11_ref[p], f12_ref[p])
        )
    widen_level_1(m1_ref, wide_ref, 2, 14)

    def correct(q, carry):
        e = double_rows(t_ref, wide_ref, q)
        for i in range(2):
            p = 2 * q + i - 4
            corr_ref[p] = w_ref[p] * s_ref[p] + e
        return carry

    lax.fori_loop(2, 14, correct, 0, unroll=2)

    def relax(p, carry):
        fp_ref[p] = KEEP * corr_ref[p] + w_ref[p] * (
            s_ref[p] + neighbours(corr_ref, f0_ref, f1_ref, f2_ref, p)
        )
        return carry

    lax.fori_loop(2, 22, relax, 0, unroll=4)

    def image(p, carry):
        im = d_ref[p] * fp_ref[p] - neighbours(fp_ref, f0_ref, f1_ref, f2_ref, p)
        im_ref[p] = im
        sm_ref[p] = w_ref[p] * im
        return carry

    lax.fori_loop(3, 21, image, 0, unroll=3)

    rs_ref[...] = jnp.zeros_like(rs_ref)
    inside = (iota((40, 128), 0) >= 12) & (iota((40, 128), 0) < 28)

    def leftovers(q, sums):
        total = jnp.zeros((40, 256), F32)
        for i in range(2):
            p = 2 * q + i - 4
            left = KEEP * im_ref[p] + neighbours(sm_ref, f0_ref, f1_ref, f2_ref, p)
            total += left
            own = jnp.where(inside & (p >= 8) & (p < 16), 1.0, 0.0)
            fp, im = fp_ref[p, :, 0:128], im_ref[p, :, 0:128]
            sums = (
                sums[0] + own * s_ref[p, :, 0:128] * fp,
                sums[1] + own * fp * im,
                sums[2] + own * sm_ref[p, :, 0:128] * (im + left[:, 0:128]),
            )
        put_rows(rs_ref, q - 4, row_pairs(t_ref, total, True))
        return sums

    zero = jnp.zeros((40, 128), F32)
    sums = lax.fori_loop(4, 12, leftovers, (zero, zero, zero), unroll=2)

    for p in range(8):
        fp_out[p] = fp_ref[8 + p, pl.ds(12, 16), 0:128]
        im_out[p] = im_ref[8 + p, pl.ds(12, 16), 0:128]

    pairs = one_hot(256, 128, lambda r, c: lax.shift_right_logical(r, 1) == c, 0.5)
    t1s_ref[...] = jnp.zeros_like(t1s_ref)
    t1s_ref[pl.ds(4, 8)] = spread(rs_ref[...].reshape(192, 256), pairs).reshape(8, 24, 128)
    for p in range(5, 11):
        sm1_ref[p] = w1_ref[p] * t1s_ref[p]
    inside_1 = jnp.where(
        (iota((24, 128), 0) >= 6) & (iota((24, 128), 0) < 14) & (iota((24, 128), 1) < 64), 1.0, 0.0
    )
    second = jnp.zeros((24, 128), F32)
    halves = [jnp.zeros((8, 128), F32)] * 2
    tq_ref[...] = jnp.zeros_like(tq_ref)
    for i in range(2):
        total = jnp.zeros((24, 128), F32)
        for j in range(2):
            p = 6 + 2 * i + j
            s1 = t1s_ref[p]
            left = KEEP * s1 + neighbours(sm1_ref, f10_ref, f11_ref, f12_ref, p)
            second += inside_1 * sm1_ref[p] * (s1 + left)
            total += left
        tq_ref[pl.ds(0, 24), :] = total
        tq_ref[pl.ds(24, 4), :] = tq_ref[pl.ds(6, 4, 2), :] + tq_ref[pl.ds(7, 4, 2), :]
        for h in range(2):
            place = one_hot(
                128, 128,
                lambda r, c, i=i, h=h: (lax.shift_right_logical(r, 1) - 16 * h == (c & 15))
                & (r < 64) & ((lax.shift_right_logical(c, 4) & 1) == i), 0.5,
            )
            halves[h] += spread(tq_ref[pl.ds(24, 8), :], place)
    scalars = (jnp.sum(sums[0]), jnp.sum(sums[1]), jnp.sum(sums[2]) + 2.0 * jnp.sum(second))
    mine = lax.shift_right_logical(lane8, 5) == row8
    pay = jnp.zeros((8, 128), F32)
    for h in range(2):
        line = jnp.sum(jnp.where(mine, halves[h], 0.0), axis=0, keepdims=True)
        pay = jnp.where(row8 == h, line, pay)
    for k, value in enumerate(scalars):
        pay = jnp.where((lane8 == k) & (row8 == 2), value, pay)
    pay_ref[...] = jnp.broadcast_to(pay[None, :4], pay_ref.shape)


def third_kernel(
    f0_ref, f1_ref, f2_ref, w_ref, f10_ref, f11_ref, f12_ref, w1_ref,
    im_ref, t1s_ref, f20_ref, f21_ref, f22_ref, w2_ref, f30_ref, f31_ref, f32_ref, w3_ref,
    before_ref, own0_ref, own1_ref, after_ref, parts_ref,
    mi_out, scalar_out,
    v_ref, t3_ref, e_ref, m2_ref, pick_ref, corr1_ref, m1_ref, wide_ref, t_ref, corr_ref,
):
    nx2, ny2 = f20_ref.shape[:2]
    lane = iota((ny2 // 4, 128), 1)

    def assemble(x, carry):
        pieces = [turn(ref[x], 16 * k, 1) for k, ref in enumerate((before_ref, own0_ref, own1_ref, after_ref))]
        for i in range(2):
            for j in range(4):
                v_ref[2 * x + i, pl.ds(j, ny2 // 4, 4), :] = window(pieces, 32 * j + 16 * i, lane)
        return carry

    lax.fori_loop(0, nx2 // 2, assemble, 0, unroll=2)
    s2 = v_ref[...]
    level_2 = (f20_ref[...], f21_ref[...], f22_ref[...], w2_ref[...])
    level_3 = (f30_ref[...], f31_ref[...], f32_ref[...], w3_ref[...])
    m2 = solve_2(s2, level_2, level_3, t3_ref, e_ref)
    lane3 = iota(s2.shape, 2)
    part = 4.0 * jnp.sum(jnp.where((lane3 >= 16) & (lane3 < 48), s2 * m2, 0.0))
    sums = jnp.sum(jnp.sum(parts_ref[...], axis=0), axis=0, keepdims=True)
    scalar_out[...] = jnp.where(iota((1, 128), 1) == 3, part, sums)
    m2_ref[...] = jnp.zeros_like(m2_ref)
    m2_ref[pl.ds(3, nx2)] = m2
    fetch_level_2(m2_ref, range(2, 6), pick_ref)

    for p in range(4, 12):
        corr1_ref[p] = w1_ref[p] * t1s_ref[p] + pick_ref[p // 2]
    for p in range(5, 11):
        m1_ref[p] = KEEP * corr1_ref[p] + w1_ref[p] * (
            t1s_ref[p] + neighbours(corr1_ref, f10_ref, f11_ref, f12_ref, p)
        )
    widen_level_1(m1_ref, wide_ref, 5, 11)

    def correct(q, carry):
        e = double_rows(t_ref, wide_ref, q)
        for i in range(2):
            p = 2 * q + i - 4
            corr_ref[p] = w_ref[p] * im_ref[p] + e
        return carry

    lax.fori_loop(5, 11, correct, 0, unroll=2)

    for p in range(8):
        q = 8 + p
        mi = KEEP * corr_ref[q] + w_ref[q] * (
            im_ref[q] + neighbours(corr_ref, f0_ref, f1_ref, f2_ref, q)
        )
        t_ref[0] = mi[:, 0:128]
        mi_out[p] = t_ref[0, pl.ds(12, 16), :]


def last_kernel(sums_ref, s_ref, fp_ref, im_ref, mi_ref, solution_ref, residual_ref, direction_ref):
    total = jnp.sum(sums_ref[...], axis=0)
    lane = iota((1, 128), 1)

    def value(lanes):
        keep = lane == lanes[0]
        for k in lanes[1:]:
            keep = keep | (lane == k)
        return jnp.sum(jnp.where(keep, total, 0.0), axis=1, keepdims=True)

    projected, curvature, product = value((0,)), value((1,)), value((2, 3))
    step = projected / curvature
    share = product / curvature
    for p in range(8):
        fp = fp_ref[p]
        solution_ref[p] = step * fp
        residual_ref[p] = s_ref[p] - step * im_ref[p]
        direction_ref[p] = step * (share * fp - mi_ref[p])


def call(kernel, inputs, outs, scratch=(), keep_in=(), keep_out=(), space=pltpu.VMEM):
    vmem = pl.BlockSpec(memory_space=pltpu.VMEM)
    inputs = [
        pltpu.with_memory_space_constraint(value, space) if i in keep_in else value
        for i, value in enumerate(inputs)
    ]
    shapes = [
        pltpu.VMEM(shape, dtype) if i in keep_out else jax.ShapeDtypeStruct(shape, dtype)
        for i, (shape, dtype) in enumerate(outs)
    ]
    return pl.pallas_call(
        kernel,
        out_shape=shapes,
        in_specs=[pl.BlockSpec(memory_space=space)] * len(inputs),
        out_specs=[vmem] * len(outs),
        scratch_shapes=[pltpu.VMEM(shape, F32) if isinstance(shape, tuple) else shape for shape in scratch],
        compiler_params=pltpu.CompilerParams(vmem_limit_bytes=VMEM_LIMIT),
    )(*inputs)


def shift_along(value, axis, by):
    size = lax.axis_size(axis)
    return lax.ppermute(value, axis, [(i, i + by) for i in range(size) if 0 <= i + by < size])


def gather_plane(copies):
    copies = copies.reshape(copies.shape[0], 1, -1)
    return lax.all_to_all(copies, ("gx", "gy"), 0, 0, tiled=True)


def local(right_side, face_coefficients, solid):
    nx2, ny2 = 2 * lax.axis_size("gx"), 4 * lax.axis_size("gy")
    own, ends = call(
        prepare_kernel,
        [right_side, face_coefficients, solid],
        [((8, 5, 16, 128), BF16), ((8, 16, 128), BF16)],
        [
            (8, 16, 128),
            pltpu.VMEM((3, 8, 16, 128), BF16),
            pltpu.VMEM((8, 16, 128), jnp.int32),
            pltpu.SemaphoreType.DMA((3,)),
        ],
        keep_in=range(3),
        space=pltpu.HBM,
    )
    before, after = shift_along(ends, "gz", 1), shift_along(ends, "gz", -1)
    (own,) = call(rim_kernel, [own, before, after], [((8, 6, 16, 128), BF16)])
    block = jnp.concatenate([shift_along(own, "gx", 1), own, shift_along(own, "gx", -1)], axis=0)
    to_up, to_down = call(edges_kernel, [block], [((15, 6, 16, 128), BF16)] * 2)
    before, after = shift_along(to_up, "gy", 1), shift_along(to_down, "gy", -1)

    fine, fine_up = (24, 40, 256), (25, 40, 256)
    mid, mid_up = (16, 24, 128), (17, 24, 128)
    rows, wide, edge = (12, 24, 256), (16, 24, 256), (6, 24, 128)
    slim, slim_up, slim_mid, slim_mid_up, slim_rows = (
        (20, 24, 256), (21, 24, 256), (16, 16, 128), (17, 16, 128), (12, 16, 256)
    )
    up, down, pay = call(
        functools.partial(fine_kernel, True),
        [block, before, after],
        [(edge, F32), (edge, F32), ((lax.axis_size(("gx", "gy")), 8, 128), F32)],
        [slim, slim_up, slim, slim, slim_mid, slim_mid_up, slim_mid, slim_mid, slim_mid,
         slim, slim, slim, slim, (2, 24, 128), slim_rows, slim_rows, slim_rows, slim_rows,
         slim_mid, slim_mid, slim_mid, slim_mid, (16, 128), (4, 8, 128)],
    )
    state = call(
        functools.partial(fine_kernel, False),
        [block, before, after],
        [(shape, F32) for shape in (fine, fine_up, fine, fine, fine, fine, mid, mid_up, mid, mid, mid)],
        [fine, fine, fine, fine, (2, 40, 128), rows, rows, rows, rows, mid, mid, mid],
        keep_out=range(11),
    )
    low, high = shift_along(up, "gx", 1), shift_along(down, "gx", -1)
    own = gather_plane(pay)
    pairs = (nx2 * ny2 // 16, 8, 128)
    own, low, high = lax.optimization_barrier((own, low, high))
    own0, own1 = own[..., :512].reshape(pairs), own[..., 512:].reshape(pairs)
    before, after = shift_along(own1, "gz", 1), shift_along(own0, "gz", -1)
    level_2, level_3 = (nx2, ny2, 128), (nx2 // 2, ny2 // 2, 128)
    window = (nx2 + 6, ny2, 128)
    half = (nx2 // 2, ny2, 128)
    first_pre, image, *more, pay = call(
        second_kernel,
        [*state, low, high, before, own0, own1, after],
        [((8, 16, 128), F32)] * 2
        + [(shape, F32) for shape in (fine, mid, *[level_2] * 4, *[level_3] * 4, (nx2 * ny2 // 8, 4, 128))],
        [(4,) + level_2, half, half, window, (8, 24, 128), mid, mid, wide, (2, 40, 128),
         fine, fine, fine, (8, 24, 256), mid, (32, 128)],
        keep_in=range(11),
        keep_out=range(2, 12),
    )
    own = gather_plane(pay)
    plane = (nx2 // 2, ny2 // 4, 128)
    own0, own1, parts = (own[..., 128 * k : 128 * k + 128].reshape(plane) for k in range(3))
    before, after = shift_along(own1, "gz", 1), shift_along(own0, "gz", -1)
    _, f0, f1, f2, w, _, _, f10, f11, f12, w1 = state
    mapped, sums = call(
        third_kernel,
        [f0, f1, f2, w, f10, f11, f12, w1, *more, before, own0, own1, after, parts],
        [((8, 16, 128), F32), ((1, 128), F32)],
        [level_2, half, half, window, (8, 24, 128), mid, mid, wide, (2, 40, 128), fine],
        keep_in=range(18),
    )
    peers = lax.axis_size("gz")
    sums = lax.all_to_all(jnp.broadcast_to(sums[None], (peers, 1, 128)), "gz", 0, 0, tiled=True)
    return tuple(
        call(
            last_kernel,
            [sums, right_side, first_pre, image, mapped],
            [((8, 16, 128), F32)] * 3,
        )
    )


def solution(mesh):
    placed = P("gx", "gy", "gz")
    return jax.shard_map(
        local,
        mesh=mesh,
        in_specs=(placed, P(None, "gx", "gy", "gz"), placed),
        out_specs=(placed, placed, placed),
        check_vma=False,
    )
```

```python
import functools

import jax
import jax.numpy as jnp
from jax import lax
from jax.experimental import pallas as pl
from jax.experimental.pallas import tpu as pltpu
from jax.sharding import PartitionSpec as P

F32 = jnp.float32
BF16 = jnp.bfloat16
ABSORB = 0.001
RELAX = 0.8
KEEP = 0.2
SWEEPS = 6
NEAR = pl.ds(8, 24)
VMEM_LIMIT = 24 * 1024 * 1024


def one_hot(rows, cols, rule, weight=1.0):
    r = lax.broadcasted_iota(jnp.int32, (rows, cols), 0)
    c = lax.broadcasted_iota(jnp.int32, (rows, cols), 1)
    return jnp.where(rule(r, c), weight, 0.0).astype(BF16)


def spread(values, matrix):
    high = values.astype(BF16)
    low = (values - high.astype(F32)).astype(BF16)
    return jnp.dot(high, matrix, preferred_element_type=F32) + jnp.dot(
        low, matrix, preferred_element_type=F32
    )


def pick(matrix, values):
    high = values.astype(BF16)
    low = (values - high.astype(F32)).astype(BF16)
    return jnp.dot(matrix, high, preferred_element_type=F32) + jnp.dot(
        matrix, low, preferred_element_type=F32
    )


def root(values):
    return values * lax.rsqrt(jnp.maximum(values, 1e-12))


def turn(values, shift, axis):
    return pltpu.roll(values, shift % values.shape[axis], axis)


def iota(shape, dim):
    return lax.broadcasted_iota(jnp.int32, shape, dim)


def plane_terms(v, f1, f2):
    return turn(v, 1, 0) * f1 + turn(v * f1, -1, 0) + turn(v, 1, 1) * f2 + turn(v * f2, -1, 1)


def neighbours(v_ref, f0_ref, f1_ref, f2_ref, p):
    return (
        f0_ref[p] * v_ref[p - 1]
        + f0_ref[p + 1] * v_ref[p + 1]
        + plane_terms(v_ref[p], f1_ref[p], f2_ref[p])
    )


def near_rows(v_ref, f0_ref, f1_ref, f2_ref, p):
    v, f2 = v_ref[p, NEAR, :], f2_ref[p, NEAR, :]
    return (
        f0_ref[p, NEAR, :] * v_ref[p - 1, NEAR, :]
        + f0_ref[p + 1, NEAR, :] * v_ref[p + 1, NEAR, :]
        + f1_ref[p, NEAR, :] * v_ref[p, pl.ds(7, 24), :]
        + f1_ref[p, pl.ds(9, 24), :] * v_ref[p, pl.ds(9, 24), :]
        + turn(v, 1, 1) * f2
        + turn(v * f2, -1, 1)
    )


def neighbours_3d(v, f0, f1, f2):
    zero = jnp.zeros_like(v[:1])
    up = f0 * v
    return (
        f0 * jnp.concatenate([zero, v[:-1]], 0)
        + jnp.concatenate([up[1:], zero], 0)
        + turn(v, 1, 1) * f1
        + turn(v * f1, -1, 1)
        + turn(v, 1, 2) * f2
        + turn(v * f2, -1, 2)
    )


def row_pairs(t_ref, values, both):
    out = []
    pairs = values.shape[0] // 2
    for half in range(2):
        t_ref[half, pl.ds(0, 2 * pairs), :] = values[:, 128 * half : 128 * half + 128]
        first = t_ref[half, pl.ds(0, pairs, 2), :]
        out.append(first + t_ref[half, pl.ds(1, pairs, 2), :] if both else first)
    return out


def put_rows(r_ref, q, halves, start=0):
    for half in range(2):
        r_ref[q, pl.ds(start, halves[half].shape[0]), pl.ds(128 * half, 128)] = halves[half]


def prepare_kernel(s_hbm, fc_hbm, solid_hbm, out_ref, ends_ref, s_ref, fc_ref, solid_ref, sems):
    copies = [
        pltpu.make_async_copy(source, target, sems.at[i])
        for i, (source, target) in enumerate(
            ((s_hbm, s_ref), (fc_hbm, fc_ref), (solid_hbm, solid_ref))
        )
    ]
    for copy in copies:
        copy.start()
    for copy in copies:
        copy.wait()
    s = s_ref[...]
    high = s.astype(BF16)
    out_ref[:, 0] = high
    out_ref[:, 1] = (s - high.astype(F32)).astype(BF16)
    weight = 1.0 - 0.75 * solid_ref[...].astype(F32)
    for a in range(3):
        out_ref[:, 2 + a] = (fc_ref[a].astype(F32) * weight).astype(BF16)
    lane = iota((16, 128), 1)

    def body(p, carry):
        ends = jnp.zeros((16, 128), F32)
        for f in range(5):
            t = turn(out_ref[p, f].astype(F32), 24 * f + 12, 1)
            ends = jnp.where((lane >= 24 * f) & (lane < 24 * f + 24), t, ends)
        ends_ref[p] = ends.astype(BF16)
        return carry

    lax.fori_loop(0, 8, body, 0, unroll=4)


def rim_kernel(own_ref, before_ref, after_ref, out_ref):
    lane = iota((8, 16, 128), 2)
    last = jnp.zeros((8, 16, 128), jnp.bool_)
    for f in range(5):
        last = last | ((lane >= 24 * f) & (lane < 24 * f + 12))
    out_ref[:, 0:5] = own_ref[...]
    rim = jnp.where(last, before_ref[...].astype(F32), after_ref[...].astype(F32))
    out_ref[:, 5] = rim.astype(BF16)


def edges_kernel(x_ref, up_ref, down_ref):
    row = iota((8, 128), 0)
    quarters = [(p, True) for p in range(5, 19)] + [(0, False), (23, False)]

    def body(f, carry):
        for t in range(11):
            pair = [x_ref[1 + 2 * t + k, f].astype(F32) for k in range(2)]
            up_ref[t, f] = jnp.concatenate([v[8:] for v in pair], 0).astype(BF16)
            down_ref[t, f] = jnp.concatenate([v[:8] for v in pair], 0).astype(BF16)
        for t in range(4):
            ups, downs = [], []
            for k in range(0, 4, 2):
                pair = []
                for p, inner in quarters[4 * t + k : 4 * t + k + 2]:
                    v = x_ref[p, f].astype(F32)
                    pair.append((v[:8], v[8:]) if inner else (v[8:], v[:8]))
                ups.append(jnp.where(row < 4, turn(pair[0][0], 4, 0), pair[1][0]))
                downs.append(jnp.where(row < 4, pair[0][1], turn(pair[1][1], 4, 0)))
            up_ref[11 + t, f] = jnp.concatenate(ups, 0).astype(BF16)
            down_ref[11 + t, f] = jnp.concatenate(downs, 0).astype(BF16)
        return carry

    lax.fori_loop(0, 6, body, 0)


def edge_rows(ym_ref, yp_ref, p, f, thin):
    row = iota((8, 128), 0)
    zero = jnp.zeros((8, 128), F32)

    def eight(ref, tile, k):
        return ref[tile, f].astype(F32)[8 * k : 8 * k + 8]

    def four(q, before):
        v = eight(ym_ref if before else yp_ref, 11 + q // 4, q % 4 // 2)
        moved = turn(v, 4, 0) if (q % 2 == 0) == before else v
        return jnp.where((row >= 4) == before, moved, 0.0)

    if p in (0, 23):
        q = 14 if p == 0 else 15
        near_before, near_after = four(q, True), four(q, False)
    else:
        near_before, near_after = (eight(ref, (p - 1) // 2, (p - 1) % 2) for ref in (ym_ref, yp_ref))
    if thin:
        return near_before, near_after
    if 5 <= p <= 18:
        far_before, far_after = four(p - 5, True), four(p - 5, False)
    else:
        far_before = far_after = zero
    return jnp.concatenate([far_before, near_before], 0), jnp.concatenate([near_after, far_after], 0)


def fine_kernel(thin, x_ref, ym_ref, yp_ref, *refs):
    if thin:
        (up_ref, down_ref, pay_ref,
         s_ref, f0_ref, f1_ref, f2_ref, s1_ref, f10_ref, f11_ref, f12_ref, w1_ref, *refs) = refs
    else:
        s_ref, f0_ref, f1_ref, f2_ref, w_ref, d_ref, s1_ref, f10_ref, f11_ref, f12_ref, w1_ref, *refs = refs
    (c0_ref, c1_ref, c2_ref, sm_ref, t_ref, r0_ref, r1_ref, r2_ref, rs_ref,
     l10_ref, l11_ref, l12_ref, *refs) = refs
    planes = range(4, 20) if thin else range(24)
    rows, rows_1 = s_ref.shape[1], s1_ref.shape[1]
    own = 4 if thin else 12
    shape, shape_1 = (rows, 256), (rows_1, 128)
    at_x = lax.axis_index("gx") == 0
    at_y = lax.axis_index("gy") == 0
    at_z = lax.axis_index("gz") == 0
    lane = iota((rows, 128), 1)
    side = (lane < 12) | (lane >= 116)

    for p in planes:
        tiles = []
        for f in range(6):
            before, after = edge_rows(ym_ref, yp_ref, p, f, thin)
            column = jnp.concatenate([before, x_ref[p, f].astype(F32), after], 0)
            tiles.append(turn(column, -4, 0)[:rows])
        rims = [
            jnp.where(side, turn(tiles[5], -(24 * f + 12), 1), 0.0) for f in range(5)
        ]
        s_ref[p, :, 0:128] = tiles[0] + tiles[1]
        s_ref[p, :, 128:256] = rims[0] + rims[1]
        for a, c_ref in enumerate((c0_ref, c1_ref, c2_ref)):
            c_ref[p, :, 0:128] = tiles[2 + a]
            c_ref[p, :, 128:256] = rims[2 + a]

    def faces(p, carry):
        before = jnp.maximum(p - 1, planes.start)
        f0_ref[p] = root(c0_ref[p] * c0_ref[before])
        c1 = c1_ref[p]
        f1_ref[p] = root(c1 * turn(c1, 1, 0))
        c2 = c2_ref[p]
        f2_ref[p] = root(c2 * turn(c2, 1, 1))
        return carry

    lax.fori_loop(planes.start, planes.stop, faces, 0, unroll=8)
    f0_ref[planes.stop] = jnp.zeros(shape, F32)

    first_row = (iota(shape, 0) == own) & at_y
    first_lane = (iota(shape, 1) == 0) & at_z
    for ref in (r0_ref, r1_ref, r2_ref, rs_ref):
        ref[...] = jnp.zeros_like(ref)

    def diagonals(q, carry):
        lows = []
        for i in range(2):
            p = 2 * q + i
            f0, f1, f2 = f0_ref[p], f1_ref[p], f2_ref[p]
            low0 = f0 + jnp.where((p == 8) & at_x, c0_ref[p], 0.0)
            low1 = f1 + jnp.where(first_row, c1_ref[p], 0.0)
            low2 = f2 + jnp.where(first_lane, c2_ref[p], 0.0)
            d = ABSORB + low0 + f0_ref[p + 1] + low1 + turn(f1, -1, 0) + low2 + turn(f2, -1, 1)
            w = RELAX / d
            if not thin:
                d_ref[p] = d
                w_ref[p] = w
            sm_ref[p] = w * s_ref[p]
            lows.append((low0, low1, low2))
        put_rows(r0_ref, q, row_pairs(t_ref, lows[0][0], True))
        put_rows(r1_ref, q, row_pairs(t_ref, lows[0][1] + lows[1][1], False))
        put_rows(r2_ref, q, row_pairs(t_ref, lows[0][2] + lows[1][2], True))
        return carry

    lax.fori_loop(planes.start // 2, planes.stop // 2, diagonals, 0, unroll=2)

    def leftovers(q, carry):
        total = jnp.zeros(shape, F32)
        for i in range(2):
            p = 2 * q + i
            total += KEEP * s_ref[p] + neighbours(sm_ref, f0_ref, f1_ref, f2_ref, p)
        put_rows(rs_ref, q, row_pairs(t_ref, total, True))
        return carry

    lax.fori_loop(planes.start // 2 + 1, planes.stop // 2 - 1, leftovers, 0, unroll=3 if thin else 5)

    pairs = one_hot(256, 128, lambda r, c: lax.shift_right_logical(r, 1) == c, 0.25)
    evens = one_hot(256, 128, lambda r, c: r == 2 * c, 0.25)
    first, count = planes.start // 2, len(planes) // 2
    for target, source, matrix in (
        (l10_ref, r0_ref, pairs), (l11_ref, r1_ref, pairs), (l12_ref, r2_ref, evens), (s1_ref, rs_ref, pairs)
    ):
        target[...] = jnp.zeros_like(target)
        value = spread(source[pl.ds(first, count)].reshape(count * rows_1, 256), matrix)
        value = value.reshape(count, rows_1, 128)
        target[pl.ds(first + 2, count)] = 2.0 * value if target is s1_ref else value

    first_row_1 = (iota(shape_1, 0) == own // 2) & at_y
    first_lane_1 = (iota(shape_1, 1) == 0) & at_z
    planes_1 = range(first + 2, first + 2 + count)

    def faces_1(p, carry):
        f10_ref[p] = jnp.where((p == 6) & at_x, 0.0, l10_ref[p])
        f11_ref[p] = jnp.where(first_row_1, 0.0, l11_ref[p])
        f12_ref[p] = jnp.where(first_lane_1, 0.0, l12_ref[p])
        return carry

    lax.fori_loop(planes_1.start, planes_1.stop, faces_1, 0, unroll=len(planes_1))
    f10_ref[planes_1.stop] = jnp.zeros(shape_1, F32)

    def diagonals_1(p, carry):
        d = (
            4.0 * ABSORB + l10_ref[p] + f10_ref[p + 1]
            + l11_ref[p] + turn(f11_ref[p], -1, 0)
            + l12_ref[p] + turn(f12_ref[p], -1, 1)
        )
        w1_ref[p] = RELAX / d
        return carry

    lax.fori_loop(planes_1.start, planes_1.stop, diagonals_1, 0, unroll=len(planes_1))
    if thin:
        pack_level_2(
            up_ref, down_ref, pay_ref, s1_ref, f10_ref, f11_ref, f12_ref, w1_ref, l10_ref, l11_ref, l12_ref, *refs
        )


def pack_level_2(
    up_ref, down_ref, pay_ref, s1_ref, f10_ref, f11_ref, f12_ref, w1_ref, l10_ref, l11_ref, l12_ref,
    sm1_ref, t1_ref, u_ref,
):
    for target, start in ((up_ref, 5), (down_ref, 9)):
        target[...] = jnp.zeros_like(target)
        for i, ref in enumerate((s1_ref, w1_ref, f10_ref)):
            for k in range(2):
                target[2 * i + k, pl.ds(4, 12), :] = ref[start + k, pl.ds(0, 12), :]
    for p in range(5, 11):
        sm1_ref[p] = w1_ref[p] * s1_ref[p]

    def quad(values, both):
        t1_ref[...] = values
        first = t1_ref[pl.ds(2, 4, 2), :]
        return first + t1_ref[pl.ds(3, 4, 2), :] if both else first

    def leftover_1(p):
        return KEEP * s1_ref[p] + neighbours(sm1_ref, f10_ref, f11_ref, f12_ref, p)

    row8, lane8 = iota((8, 128), 0), iota((8, 128), 1)
    narrow = one_hot(128, 128, lambda r, c: (lax.shift_right_logical(r, 1) == c) & (r < 64))
    narrow_even = one_hot(128, 128, lambda r, c: (r == 2 * c) & (r < 64))
    total = jnp.zeros((8, 128), F32)
    for f in range(4):
        for i in range(2):
            p = 6 + 2 * i
            if f == 0:
                part = quad(leftover_1(p) + leftover_1(p + 1), True)
            elif f == 1:
                part = quad(l10_ref[p], True)
            elif f == 2:
                part = quad(l11_ref[p] + l11_ref[p + 1], False)
            else:
                part = quad(l12_ref[p] + l12_ref[p + 1], True)
            u_ref[f, pl.ds(4 * i, 4), :] = part * (0.5 if f == 0 else 0.25)
        part = spread(u_ref[f], narrow_even if f == 3 else narrow)
        for i in range(2):
            for h in range(2):
                to = 32 * f + 16 * i
                moved = turn(turn(part, 4 * (h - i), 0), to - 16 * h, 1)
                here = (lax.shift_right_logical(row8, 2) == h) & (lane8 >= to) & (lane8 < to + 16)
                total = jnp.where(here, moved, total)
    pay_ref[...] = jnp.broadcast_to(total[None], pay_ref.shape)


def window(pieces, to, lane):
    out = pieces[3]
    for k in range(3):
        start = (to + 16 * k) % 128
        here = (lane >= start) & (lane < start + 16)
        out = jnp.where(here, pieces[k], out)
    return jnp.where(lane < 64, turn(out, -to, 1), 0.0)


def solve_2(s2, level_2, level_3, t3_ref, e_ref):
    f0, f1, f2, w = level_2
    g0, g1, g2, w3 = level_3
    nx, ny, _ = s2.shape
    sm = w * s2
    left = KEEP * s2 + neighbours_3d(sm, f0, f1, f2)
    s3 = coarse_2(left.reshape(nx // 2, 2, ny, 128).sum(1), t3_ref, True, 0.5, False)
    e = w3 * s3
    for _ in range(SWEEPS - 1):
        e = KEEP * e + w3 * (s3 + neighbours_3d(e, g0, g1, g2))
    widen = one_hot(128, 128, lambda r, c: (r == lax.shift_right_logical(c, 1)) & (c < 64))
    wide = spread(e.reshape(nx * ny // 4, 128), widen).reshape(nx // 2, ny // 2, 128)
    for x in range(nx // 2):
        for i in range(2):
            e_ref[x, pl.ds(i, ny // 2, 2), :] = wide[x]
    e2 = e_ref[...]
    corrected = sm + jnp.concatenate([e2[:, None], e2[:, None]], 1).reshape(nx, ny, 128)
    return KEEP * corrected + w * (s2 + neighbours_3d(corrected, f0, f1, f2))


def coarse_2(values, t3_ref, both, weight, even):
    nx, ny, _ = values.shape
    t3_ref[...] = values
    first = t3_ref[:, pl.ds(0, ny // 2, 2), :]
    if both:
        first = first + t3_ref[:, pl.ds(1, ny // 2, 2), :]
    if even:
        rule = lambda r, c: (r == 2 * c) & (r < 64)
    else:
        rule = lambda r, c: (lax.shift_right_logical(r, 1) == c) & (r < 64)
    flat = spread(first.reshape(nx * ny // 2, 128), one_hot(128, 128, rule, weight))
    return flat.reshape(nx, ny // 2, 128)


def coefficients(low, mask_lane, absorb):
    shape = low[0].shape
    f0 = jnp.where(iota(shape, 0) == 0, 0.0, low[0])
    f1 = jnp.where(iota(shape, 1) == 0, 0.0, low[1])
    f2 = jnp.where((iota(shape, 2) == mask_lane) & (lax.axis_index("gz") == 0), 0.0, low[2])
    d = (
        absorb + low[0] + jnp.concatenate([f0[1:], jnp.zeros_like(f0[:1])], 0)
        + low[1] + turn(f1, -1, 1) + low[2] + turn(f2, -1, 2)
    )
    return f0, f1, f2, RELAX / d


def fetch_level_2(m2_ref, planes, pick_ref):
    gx, gy = lax.axis_index("gx"), lax.axis_index("gy")
    ny = m2_ref.shape[1]

    def source(c):
        return jnp.where(c < 96, 16, -48) + lax.shift_right_logical(c, 1)

    widen = one_hot(128, 128, lambda r, c: r == source(c))
    rows = one_hot(24, ny, lambda r, c: c == 4 * gy - 3 + lax.shift_right_logical(r, 1))
    flat = m2_ref[pl.ds(2 * gx + planes.start, len(planes))].reshape(len(planes) * ny, 128)
    wide = spread(flat, widen).reshape(len(planes), ny, 128)
    for k in planes:
        pick_ref[k] = pick(rows, wide[k - planes.start])


def widen_level_1(m1_ref, wide_ref, lo, hi):
    rows = 24 * (hi - lo)
    widen = one_hot(128, 256, lambda r, c: r == lax.shift_right_logical(c, 1))
    wide_ref[pl.ds(lo, hi - lo)] = spread(m1_ref[pl.ds(lo, hi - lo)].reshape(rows, 128), widen).reshape(
        hi - lo, 24, 256
    )


def double_rows(t_ref, wide_ref, q, start=0, count=20):
    for half in range(2):
        part = wide_ref[q, pl.ds(start, count), pl.ds(128 * half, 128)]
        for i in range(2):
            t_ref[half, pl.ds(i, count, 2), :] = part
    return jnp.concatenate([t_ref[half, pl.ds(0, 2 * count), :] for half in range(2)], 1)


def second_kernel(
    s_ref, f0_ref, f1_ref, f2_ref, w_ref, d_ref,
    s1_ref, f10_ref, f11_ref, f12_ref, w1_ref,
    low_ref, high_ref, before_ref, own0_ref, own1_ref, after_ref,
    fp_out, im_out, im_ref, t1s_ref, f20_ref, f21_ref, f22_ref, w2_ref,
    f30_ref, f31_ref, f32_ref, w3_ref, pay_ref,
    v_ref, t3_ref, e_ref, m2_ref, pick_ref, corr1_ref, m1_ref, wide_ref, t_ref,
    corr_ref, fp_ref, sm_ref, rs_ref, sm1_ref, tq_ref,
):
    nx2, ny2 = f20_ref.shape[:2]
    lane8 = iota((8, 128), 1)
    row8 = iota((8, 128), 0)

    def assemble(x, carry):
        for pair in range(ny2 // 8):
            g = x * (ny2 // 8) + pair
            pieces = [turn(ref[g], 16 * k, 1) for k, ref in enumerate((before_ref, own0_ref, own1_ref, after_ref))]
            for f in range(4):
                for i in range(2):
                    v_ref[f, 2 * x + i, pl.ds(8 * pair, 8), :] = window(pieces, 32 * f + 16 * i, lane8)
        return carry

    lax.fori_loop(0, nx2 // 2, assemble, 0, unroll=4)

    s2 = v_ref[0]
    low = (v_ref[1], v_ref[2], v_ref[3])
    level_2 = coefficients(low, 16, 16.0 * ABSORB)
    f20_ref[...], f21_ref[...], f22_ref[...], w2_ref[...] = level_2
    halves = [t.reshape(nx2 // 2, 2, ny2, 128) for t in low]
    low_3 = (
        coarse_2(halves[0][:, 0], t3_ref, True, 0.25, False),
        coarse_2(halves[1].sum(1), t3_ref, False, 0.25, False),
        coarse_2(halves[2].sum(1), t3_ref, True, 0.25, True),
    )
    level_3 = coefficients(low_3, 8, 64.0 * ABSORB)
    f30_ref[...], f31_ref[...], f32_ref[...], w3_ref[...] = level_3
    m2_ref[...] = jnp.zeros_like(m2_ref)
    m2_ref[pl.ds(3, nx2)] = solve_2(s2, level_2, level_3, t3_ref, e_ref)
    fetch_level_2(m2_ref, range(8), pick_ref)

    def correct_1(p, carry):
        corr1_ref[p] = w1_ref[p] * s1_ref[p] + pick_ref[lax.shift_right_logical(p, 1)]
        return carry

    lax.fori_loop(3, 13, correct_1, 0, unroll=10)
    for k in range(2):
        corr1_ref[1 + k] = low_ref[2 + k] * low_ref[k] + pick_ref[(1 + k) // 2]
        corr1_ref[13 + k] = high_ref[2 + k] * high_ref[k] + pick_ref[(13 + k) // 2]

    def relax_1(p, carry):
        m1_ref[p] = KEEP * corr1_ref[p] + w1_ref[p] * (
            s1_ref[p] + neighbours(corr1_ref, f10_ref, f11_ref, f12_ref, p)
        )
        return carry

    lax.fori_loop(3, 13, relax_1, 0, unroll=10)
    for p, source, w, face, next_face in (
        (2, low_ref[1], low_ref[3], low_ref[5], f10_ref[3]),
        (13, high_ref[0], high_ref[2], f10_ref[13], high_ref[5]),
    ):
        m1_ref[p] = KEEP * corr1_ref[p] + w * (
            source + face * corr1_ref[p - 1] + next_face * corr1_ref[p + 1]
            + plane_terms(corr1_ref[p], f11_ref[p], f12_ref[p])
        )
    widen_level_1(m1_ref, wide_ref, 2, 14)

    def correct(q, carry):
        e = double_rows(t_ref, wide_ref, q)
        for i in range(2):
            p = 2 * q + i - 4
            corr_ref[p] = w_ref[p] * s_ref[p] + e
        return carry

    lax.fori_loop(2, 14, correct, 0, unroll=2)

    def relax(p, carry):
        fp_ref[p] = KEEP * corr_ref[p] + w_ref[p] * (
            s_ref[p] + neighbours(corr_ref, f0_ref, f1_ref, f2_ref, p)
        )
        return carry

    def relax_near(p, carry):
        fp_ref[p, NEAR, :] = KEEP * corr_ref[p, NEAR, :] + w_ref[p, NEAR, :] * (
            s_ref[p, NEAR, :] + near_rows(corr_ref, f0_ref, f1_ref, f2_ref, p)
        )
        return carry

    lax.fori_loop(2, 7, relax_near, 0, unroll=5)
    lax.fori_loop(7, 17, relax, 0, unroll=10)
    lax.fori_loop(17, 22, relax_near, 0, unroll=5)

    def image(p, carry):
        im = d_ref[p] * fp_ref[p] - neighbours(fp_ref, f0_ref, f1_ref, f2_ref, p)
        im_ref[p] = im
        sm_ref[p] = w_ref[p] * im
        return carry

    def image_near(p, carry):
        im = d_ref[p, NEAR, :] * fp_ref[p, NEAR, :] - near_rows(fp_ref, f0_ref, f1_ref, f2_ref, p)
        im_ref[p, NEAR, :] = im
        sm_ref[p, NEAR, :] = w_ref[p, NEAR, :] * im
        return carry

    lax.fori_loop(3, 8, image_near, 0, unroll=5)
    lax.fori_loop(8, 16, image, 0, unroll=8)
    lax.fori_loop(16, 21, image_near, 0, unroll=5)

    rs_ref[...] = jnp.zeros_like(rs_ref)
    inside = (iota((24, 128), 0) >= 4) & (iota((24, 128), 0) < 20)

    def leftovers(q, sums):
        total = jnp.zeros((24, 256), F32)
        for i in range(2):
            p = 2 * q + i - 4
            left = KEEP * im_ref[p, NEAR, :] + near_rows(sm_ref, f0_ref, f1_ref, f2_ref, p)
            total += left
            own = inside & (p >= 8) & (p < 16)
            fp, im = fp_ref[p, NEAR, 0:128], im_ref[p, NEAR, 0:128]
            terms = (s_ref[p, NEAR, 0:128] * fp, fp * im, sm_ref[p, NEAR, 0:128] * (im + left[:, 0:128]))
            sums = tuple(old + jnp.where(own, new, 0.0) for old, new in zip(sums, terms))
        put_rows(rs_ref, q - 4, row_pairs(t_ref, total, True), 4)
        return sums

    zero = jnp.zeros((24, 128), F32)
    sums = lax.fori_loop(4, 12, leftovers, (zero, zero, zero), unroll=8)

    for p in range(8):
        fp_out[p] = fp_ref[8 + p, pl.ds(12, 16), 0:128]
        im_out[p] = im_ref[8 + p, pl.ds(12, 16), 0:128]

    pairs = one_hot(256, 128, lambda r, c: lax.shift_right_logical(r, 1) == c, 0.5)
    t1s_ref[...] = jnp.zeros_like(t1s_ref)
    t1s_ref[pl.ds(4, 8)] = spread(rs_ref[...].reshape(192, 256), pairs).reshape(8, 24, 128)
    for p in range(5, 11):
        sm1_ref[p] = w1_ref[p] * t1s_ref[p]
    inside_1 = (iota((24, 128), 0) >= 6) & (iota((24, 128), 0) < 14) & (iota((24, 128), 1) < 64)
    second = jnp.zeros((24, 128), F32)
    halves = [jnp.zeros((8, 128), F32)] * 2
    tq_ref[...] = jnp.zeros_like(tq_ref)
    for i in range(2):
        total = jnp.zeros((24, 128), F32)
        for j in range(2):
            p = 6 + 2 * i + j
            s1 = t1s_ref[p]
            left = KEEP * s1 + neighbours(sm1_ref, f10_ref, f11_ref, f12_ref, p)
            second += jnp.where(inside_1, sm1_ref[p] * (s1 + left), 0.0)
            total += left
        tq_ref[pl.ds(0, 24), :] = total
        tq_ref[pl.ds(24, 4), :] = tq_ref[pl.ds(6, 4, 2), :] + tq_ref[pl.ds(7, 4, 2), :]
        for h in range(2):
            place = one_hot(
                128, 128,
                lambda r, c, i=i, h=h: (lax.shift_right_logical(r, 1) - 16 * h == (c & 15))
                & (r < 64) & ((lax.shift_right_logical(c, 4) & 1) == i), 0.5,
            )
            halves[h] += spread(tq_ref[pl.ds(24, 8), :], place)
    scalars = (jnp.sum(sums[0]), jnp.sum(sums[1]), jnp.sum(sums[2]) + 2.0 * jnp.sum(second))
    mine = lax.shift_right_logical(lane8, 5) == row8
    pay = jnp.zeros((8, 128), F32)
    for h in range(2):
        line = jnp.sum(jnp.where(mine, halves[h], 0.0), axis=0, keepdims=True)
        pay = jnp.where(row8 == h, line, pay)
    for k, value in enumerate(scalars):
        pay = jnp.where((lane8 == k) & (row8 == 2), value, pay)
    pay_ref[...] = jnp.broadcast_to(pay[None, :4], pay_ref.shape)


def third_kernel(
    f0_ref, f1_ref, f2_ref, w_ref, f10_ref, f11_ref, f12_ref, w1_ref,
    im_ref, t1s_ref, f20_ref, f21_ref, f22_ref, w2_ref, f30_ref, f31_ref, f32_ref, w3_ref,
    before_ref, own0_ref, own1_ref, after_ref, parts_ref,
    mi_out, scalar_out,
    v_ref, t3_ref, e_ref, m2_ref, pick_ref, corr1_ref, m1_ref, wide_ref, t_ref, corr_ref,
):
    nx2, ny2 = f20_ref.shape[:2]
    lane = iota((ny2 // 4, 128), 1)

    def assemble(x, carry):
        pieces = [turn(ref[x], 16 * k, 1) for k, ref in enumerate((before_ref, own0_ref, own1_ref, after_ref))]
        for i in range(2):
            for j in range(4):
                v_ref[2 * x + i, pl.ds(j, ny2 // 4, 4), :] = window(pieces, 32 * j + 16 * i, lane)
        return carry

    lax.fori_loop(0, nx2 // 2, assemble, 0, unroll=4)
    s2 = v_ref[...]
    level_2 = (f20_ref[...], f21_ref[...], f22_ref[...], w2_ref[...])
    level_3 = (f30_ref[...], f31_ref[...], f32_ref[...], w3_ref[...])
    m2 = solve_2(s2, level_2, level_3, t3_ref, e_ref)
    lane3 = iota(s2.shape, 2)
    part = 4.0 * jnp.sum(jnp.where((lane3 >= 16) & (lane3 < 48), s2 * m2, 0.0))
    sums = jnp.sum(jnp.sum(parts_ref[...], axis=0), axis=0, keepdims=True)
    scalar_out[...] = jnp.where(iota((1, 128), 1) == 3, part, sums)
    m2_ref[...] = jnp.zeros_like(m2_ref)
    m2_ref[pl.ds(3, nx2)] = m2
    fetch_level_2(m2_ref, range(2, 6), pick_ref)

    for p in range(4, 12):
        corr1_ref[p] = w1_ref[p] * t1s_ref[p] + pick_ref[p // 2]
    for p in range(5, 11):
        m1_ref[p] = KEEP * corr1_ref[p] + w1_ref[p] * (
            t1s_ref[p] + neighbours(corr1_ref, f10_ref, f11_ref, f12_ref, p)
        )
    widen_level_1(m1_ref, wide_ref, 5, 11)

    def correct(q, carry):
        e = double_rows(t_ref, wide_ref, q, 4, 12)
        for i in range(2):
            p = 2 * q + i - 4
            corr_ref[p, NEAR, :] = w_ref[p, NEAR, :] * im_ref[p, NEAR, :] + e
        return carry

    lax.fori_loop(5, 11, correct, 0, unroll=6)

    for p in range(8):
        q = 8 + p
        mi = KEEP * corr_ref[q, NEAR, :] + w_ref[q, NEAR, :] * (
            im_ref[q, NEAR, :] + near_rows(corr_ref, f0_ref, f1_ref, f2_ref, q)
        )
        mi_out[p] = mi[4:20, 0:128]


def last_kernel(sums_ref, s_ref, fp_ref, im_ref, mi_ref, solution_ref, residual_ref, direction_ref):
    total = jnp.sum(sums_ref[...], axis=0)
    lane = iota((1, 128), 1)

    def value(lanes):
        keep = lane == lanes[0]
        for k in lanes[1:]:
            keep = keep | (lane == k)
        return jnp.sum(jnp.where(keep, total, 0.0), axis=1, keepdims=True)

    projected, curvature, product = value((0,)), value((1,)), value((2, 3))
    step = projected / curvature
    share = product / curvature
    for p in range(8):
        fp = fp_ref[p]
        solution_ref[p] = step * fp
        residual_ref[p] = s_ref[p] - step * im_ref[p]
        direction_ref[p] = step * (share * fp - mi_ref[p])


def call(kernel, inputs, outs, scratch=(), keep_in=(), keep_out=(), space=pltpu.VMEM):
    vmem = pl.BlockSpec(memory_space=pltpu.VMEM)
    inputs = [
        pltpu.with_memory_space_constraint(value, space) if i in keep_in else value
        for i, value in enumerate(inputs)
    ]
    shapes = [
        pltpu.VMEM(shape, dtype) if i in keep_out else jax.ShapeDtypeStruct(shape, dtype)
        for i, (shape, dtype) in enumerate(outs)
    ]
    return pl.pallas_call(
        kernel,
        out_shape=shapes,
        in_specs=[pl.BlockSpec(memory_space=space)] * len(inputs),
        out_specs=[vmem] * len(outs),
        scratch_shapes=[pltpu.VMEM(shape, F32) if isinstance(shape, tuple) else shape for shape in scratch],
        compiler_params=pltpu.CompilerParams(vmem_limit_bytes=VMEM_LIMIT),
    )(*inputs)


def shift_along(value, axis, by):
    size = lax.axis_size(axis)
    return lax.ppermute(value, axis, [(i, i + by) for i in range(size) if 0 <= i + by < size])


def gather_plane(copies):
    copies = copies.reshape(copies.shape[0], 1, -1)
    return lax.all_to_all(copies, ("gx", "gy"), 0, 0, tiled=True)


def local(right_side, face_coefficients, solid):
    nx2, ny2 = 2 * lax.axis_size("gx"), 4 * lax.axis_size("gy")
    own, ends = call(
        prepare_kernel,
        [right_side, face_coefficients, solid],
        [((8, 5, 16, 128), BF16), ((8, 16, 128), BF16)],
        [
            (8, 16, 128),
            pltpu.VMEM((3, 8, 16, 128), BF16),
            pltpu.VMEM((8, 16, 128), jnp.int32),
            pltpu.SemaphoreType.DMA((3,)),
        ],
        keep_in=range(3),
        space=pltpu.HBM,
    )
    before, after = shift_along(ends, "gz", 1), shift_along(ends, "gz", -1)
    (own,) = call(rim_kernel, [own, before, after], [((8, 6, 16, 128), BF16)])
    block = jnp.concatenate([shift_along(own, "gx", 1), own, shift_along(own, "gx", -1)], axis=0)
    to_up, to_down = call(edges_kernel, [block], [((15, 6, 16, 128), BF16)] * 2)
    before, after = shift_along(to_up, "gy", 1), shift_along(to_down, "gy", -1)

    fine, fine_up = (24, 40, 256), (25, 40, 256)
    mid, mid_up = (16, 24, 128), (17, 24, 128)
    rows, wide, edge = (12, 24, 256), (16, 24, 256), (6, 24, 128)
    slim, slim_up, slim_mid, slim_mid_up, slim_rows = (
        (20, 24, 256), (21, 24, 256), (16, 16, 128), (17, 16, 128), (12, 16, 256)
    )
    up, down, pay = call(
        functools.partial(fine_kernel, True),
        [block, before, after],
        [(edge, F32), (edge, F32), ((lax.axis_size(("gx", "gy")), 8, 128), F32)],
        [slim, slim_up, slim, slim, slim_mid, slim_mid_up, slim_mid, slim_mid, slim_mid,
         slim, slim, slim, slim, (2, 24, 128), slim_rows, slim_rows, slim_rows, slim_rows,
         slim_mid, slim_mid, slim_mid, slim_mid, (16, 128), (4, 8, 128)],
    )
    state = call(
        functools.partial(fine_kernel, False),
        [block, before, after],
        [(shape, F32) for shape in (fine, fine_up, fine, fine, fine, fine, mid, mid_up, mid, mid, mid)],
        [fine, fine, fine, fine, (2, 40, 128), rows, rows, rows, rows, mid, mid, mid],
        keep_out=range(11),
    )
    low, high = shift_along(up, "gx", 1), shift_along(down, "gx", -1)
    own = gather_plane(pay)
    pairs = (nx2 * ny2 // 16, 8, 128)
    own, low, high = lax.optimization_barrier((own, low, high))
    own0, own1 = own[..., :512].reshape(pairs), own[..., 512:].reshape(pairs)
    before, after = shift_along(own1, "gz", 1), shift_along(own0, "gz", -1)
    level_2, level_3 = (nx2, ny2, 128), (nx2 // 2, ny2 // 2, 128)
    window = (nx2 + 6, ny2, 128)
    half = (nx2 // 2, ny2, 128)
    first_pre, image, *more, pay = call(
        second_kernel,
        [*state, low, high, before, own0, own1, after],
        [((8, 16, 128), F32)] * 2
        + [(shape, F32) for shape in (fine, mid, *[level_2] * 4, *[level_3] * 4, (nx2 * ny2 // 8, 4, 128))],
        [(4,) + level_2, half, half, window, (8, 24, 128), mid, mid, wide, (2, 40, 128),
         fine, fine, fine, (8, 24, 256), mid, (32, 128)],
        keep_in=range(11),
        keep_out=range(2, 12),
    )
    own = gather_plane(pay)
    plane = (nx2 // 2, ny2 // 4, 128)
    own0, own1, parts = (own[..., 128 * k : 128 * k + 128].reshape(plane) for k in range(3))
    before, after = shift_along(own1, "gz", 1), shift_along(own0, "gz", -1)
    _, f0, f1, f2, w, _, _, f10, f11, f12, w1 = state
    mapped, sums = call(
        third_kernel,
        [f0, f1, f2, w, f10, f11, f12, w1, *more, before, own0, own1, after, parts],
        [((8, 16, 128), F32), ((1, 128), F32)],
        [level_2, half, half, window, (8, 24, 128), mid, mid, wide, (2, 40, 128), fine],
        keep_in=range(18),
    )
    peers = lax.axis_size("gz")
    sums = lax.all_to_all(jnp.broadcast_to(sums[None], (peers, 1, 128)), "gz", 0, 0, tiled=True)
    return tuple(
        call(
            last_kernel,
            [sums, right_side, first_pre, image, mapped],
            [((8, 16, 128), F32)] * 3,
        )
    )


def solution(mesh):
    placed = P("gx", "gy", "gz")
    return jax.shard_map(
        local,
        mesh=mesh,
        in_specs=(placed, P(None, "gx", "gy", "gz"), placed),
        out_specs=(placed, placed, placed),
        check_vma=False,
    )
```

```python
import functools

import jax
import jax.numpy as jnp
from jax import lax
from jax.experimental import pallas as pl
from jax.experimental.pallas import tpu as pltpu
from jax.sharding import PartitionSpec as P

F32 = jnp.float32
BF16 = jnp.bfloat16
ABSORB = 0.001
RELAX = 0.8
KEEP = 0.2
SWEEPS = 6
NEAR = pl.ds(8, 24)
VMEM_LIMIT = 24 * 1024 * 1024


def one_hot(rows, cols, rule, weight=1.0):
    r = lax.broadcasted_iota(jnp.int32, (rows, cols), 0)
    c = lax.broadcasted_iota(jnp.int32, (rows, cols), 1)
    return jnp.where(rule(r, c), weight, 0.0).astype(BF16)


def spread(values, matrix):
    high = values.astype(BF16)
    low = (values - high.astype(F32)).astype(BF16)
    return jnp.dot(high, matrix, preferred_element_type=F32) + jnp.dot(
        low, matrix, preferred_element_type=F32
    )


def pick(matrix, values):
    high = values.astype(BF16)
    low = (values - high.astype(F32)).astype(BF16)
    return jnp.dot(matrix, high, preferred_element_type=F32) + jnp.dot(
        matrix, low, preferred_element_type=F32
    )


def root(values):
    return values * lax.rsqrt(jnp.maximum(values, 1e-12))


def turn(values, shift, axis):
    return pltpu.roll(values, shift % values.shape[axis], axis)


def iota(shape, dim):
    return lax.broadcasted_iota(jnp.int32, shape, dim)


def plane_terms(v, f1, f2):
    return turn(v, 1, 0) * f1 + turn(v * f1, -1, 0) + turn(v, 1, 1) * f2 + turn(v * f2, -1, 1)


def neighbours(v_ref, f0_ref, f1_ref, f2_ref, p):
    return (
        f0_ref[p] * v_ref[p - 1]
        + f0_ref[p + 1] * v_ref[p + 1]
        + plane_terms(v_ref[p], f1_ref[p], f2_ref[p])
    )


def near_rows(v_ref, f0_ref, f1_ref, f2_ref, p):
    v, f2 = v_ref[p, NEAR, :], f2_ref[p, NEAR, :]
    return (
        f0_ref[p, NEAR, :] * v_ref[p - 1, NEAR, :]
        + f0_ref[p + 1, NEAR, :] * v_ref[p + 1, NEAR, :]
        + f1_ref[p, NEAR, :] * v_ref[p, pl.ds(7, 24), :]
        + f1_ref[p, pl.ds(9, 24), :] * v_ref[p, pl.ds(9, 24), :]
        + turn(v, 1, 1) * f2
        + turn(v * f2, -1, 1)
    )


def neighbours_3d(v, f0, f1, f2):
    zero = jnp.zeros_like(v[:1])
    up = f0 * v
    return (
        f0 * jnp.concatenate([zero, v[:-1]], 0)
        + jnp.concatenate([up[1:], zero], 0)
        + turn(v, 1, 1) * f1
        + turn(v * f1, -1, 1)
        + turn(v, 1, 2) * f2
        + turn(v * f2, -1, 2)
    )


def row_pairs(t_ref, values, both):
    out = []
    pairs = values.shape[0] // 2
    for half in range(2):
        t_ref[half, pl.ds(0, 2 * pairs), :] = values[:, 128 * half : 128 * half + 128]
        first = t_ref[half, pl.ds(0, pairs, 2), :]
        out.append(first + t_ref[half, pl.ds(1, pairs, 2), :] if both else first)
    return out


def put_rows(r_ref, q, halves, start=0):
    for half in range(2):
        r_ref[q, pl.ds(start, halves[half].shape[0]), pl.ds(128 * half, 128)] = halves[half]


def prepare_kernel(s_hbm, fc_hbm, solid_hbm, out_ref, ends_ref, s_ref, fc_ref, solid_ref, sems):
    copies = [
        pltpu.make_async_copy(source, target, sems.at[i])
        for i, (source, target) in enumerate(
            ((s_hbm, s_ref), (fc_hbm, fc_ref), (solid_hbm, solid_ref))
        )
    ]
    for copy in copies:
        copy.start()
    for copy in copies:
        copy.wait()
    s = s_ref[...]
    high = s.astype(BF16)
    out_ref[:, 0] = high
    out_ref[:, 1] = (s - high.astype(F32)).astype(BF16)
    weight = 1.0 - 0.75 * solid_ref[...].astype(F32)
    for a in range(3):
        out_ref[:, 2 + a] = (fc_ref[a].astype(F32) * weight).astype(BF16)
    lane = iota((16, 128), 1)

    def body(p, carry):
        ends = jnp.zeros((16, 128), F32)
        for f in range(5):
            t = turn(out_ref[p, f].astype(F32), 24 * f + 12, 1)
            ends = jnp.where((lane >= 24 * f) & (lane < 24 * f + 24), t, ends)
        ends_ref[p] = ends.astype(BF16)
        return carry

    lax.fori_loop(0, 8, body, 0, unroll=4)


def rim_kernel(own_ref, before_ref, after_ref, out_ref):
    lane = iota((8, 16, 128), 2)
    last = jnp.zeros((8, 16, 128), jnp.bool_)
    for f in range(5):
        last = last | ((lane >= 24 * f) & (lane < 24 * f + 12))
    out_ref[:, 0:5] = own_ref[...]
    rim = jnp.where(last, before_ref[...].astype(F32), after_ref[...].astype(F32))
    out_ref[:, 5] = rim.astype(BF16)


def edges_kernel(x_ref, up_ref, down_ref):
    row = iota((8, 128), 0)
    quarters = [(p, True) for p in range(5, 19)] + [(0, False), (23, False)]

    def body(f, carry):
        for t in range(11):
            pair = [x_ref[1 + 2 * t + k, f].astype(F32) for k in range(2)]
            up_ref[t, f] = jnp.concatenate([v[8:] for v in pair], 0).astype(BF16)
            down_ref[t, f] = jnp.concatenate([v[:8] for v in pair], 0).astype(BF16)
        for t in range(4):
            ups, downs = [], []
            for k in range(0, 4, 2):
                pair = []
                for p, inner in quarters[4 * t + k : 4 * t + k + 2]:
                    v = x_ref[p, f].astype(F32)
                    pair.append((v[:8], v[8:]) if inner else (v[8:], v[:8]))
                ups.append(jnp.where(row < 4, turn(pair[0][0], 4, 0), pair[1][0]))
                downs.append(jnp.where(row < 4, pair[0][1], turn(pair[1][1], 4, 0)))
            up_ref[11 + t, f] = jnp.concatenate(ups, 0).astype(BF16)
            down_ref[11 + t, f] = jnp.concatenate(downs, 0).astype(BF16)
        return carry

    lax.fori_loop(0, 6, body, 0, unroll=2)


def edge_rows(ym_ref, yp_ref, p, f, thin):
    row = iota((8, 128), 0)
    zero = jnp.zeros((8, 128), F32)

    def eight(ref, tile, k):
        return ref[tile, f].astype(F32)[8 * k : 8 * k + 8]

    def four(q, before):
        v = eight(ym_ref if before else yp_ref, 11 + q // 4, q % 4 // 2)
        moved = turn(v, 4, 0) if (q % 2 == 0) == before else v
        return jnp.where((row >= 4) == before, moved, 0.0)

    if p in (0, 23):
        q = 14 if p == 0 else 15
        near_before, near_after = four(q, True), four(q, False)
    else:
        near_before, near_after = (eight(ref, (p - 1) // 2, (p - 1) % 2) for ref in (ym_ref, yp_ref))
    if thin:
        return near_before, near_after
    if 5 <= p <= 18:
        far_before, far_after = four(p - 5, True), four(p - 5, False)
    else:
        far_before = far_after = zero
    return jnp.concatenate([far_before, near_before], 0), jnp.concatenate([near_after, far_after], 0)


def fine_kernel(thin, x_ref, ym_ref, yp_ref, *refs):
    if thin:
        (up_ref, down_ref, pay_ref,
         s_ref, f0_ref, f1_ref, f2_ref, s1_ref, f10_ref, f11_ref, f12_ref, w1_ref, *refs) = refs
    else:
        s_ref, f0_ref, f1_ref, f2_ref, w_ref, d_ref, s1_ref, f10_ref, f11_ref, f12_ref, w1_ref, *refs = refs
    (c0_ref, c1_ref, c2_ref, sm_ref, t_ref, r0_ref, r1_ref, r2_ref, rs_ref,
     l10_ref, l11_ref, l12_ref, *refs) = refs
    planes = range(4, 20) if thin else range(24)
    rows, rows_1 = s_ref.shape[1], s1_ref.shape[1]
    own = 4 if thin else 12
    shape, shape_1 = (rows, 256), (rows_1, 128)
    at_x = lax.axis_index("gx") == 0
    at_y = lax.axis_index("gy") == 0
    at_z = lax.axis_index("gz") == 0
    lane = iota((rows, 128), 1)
    side = (lane < 12) | (lane >= 116)

    for p in planes:
        tiles = []
        for f in range(6):
            before, after = edge_rows(ym_ref, yp_ref, p, f, thin)
            column = jnp.concatenate([before, x_ref[p, f].astype(F32), after], 0)
            tiles.append(turn(column, -4, 0)[:rows])
        rims = [
            jnp.where(side, turn(tiles[5], -(24 * f + 12), 1), 0.0) for f in range(5)
        ]
        s_ref[p, :, 0:128] = tiles[0] + tiles[1]
        s_ref[p, :, 128:256] = rims[0] + rims[1]
        for a, c_ref in enumerate((c0_ref, c1_ref, c2_ref)):
            c_ref[p, :, 0:128] = tiles[2 + a]
            c_ref[p, :, 128:256] = rims[2 + a]

    def faces(p, carry):
        before = jnp.maximum(p - 1, planes.start)
        f0_ref[p] = root(c0_ref[p] * c0_ref[before])
        c1 = c1_ref[p]
        f1_ref[p] = root(c1 * turn(c1, 1, 0))
        c2 = c2_ref[p]
        f2_ref[p] = root(c2 * turn(c2, 1, 1))
        return carry

    lax.fori_loop(planes.start, planes.stop, faces, 0, unroll=len(planes))
    f0_ref[planes.stop] = jnp.zeros(shape, F32)

    first_row = (iota(shape, 0) == own) & at_y
    first_lane = (iota(shape, 1) == 0) & at_z
    for ref in (r0_ref, r1_ref, r2_ref, rs_ref):
        ref[...] = jnp.zeros_like(ref)

    def diagonals(q, carry):
        lows = []
        for i in range(2):
            p = 2 * q + i
            f0, f1, f2 = f0_ref[p], f1_ref[p], f2_ref[p]
            low0 = f0 + jnp.where((p == 8) & at_x, c0_ref[p], 0.0)
            low1 = f1 + jnp.where(first_row, c1_ref[p], 0.0)
            low2 = f2 + jnp.where(first_lane, c2_ref[p], 0.0)
            d = ABSORB + low0 + f0_ref[p + 1] + low1 + turn(f1, -1, 0) + low2 + turn(f2, -1, 1)
            w = RELAX / d
            if not thin:
                d_ref[p] = d
                w_ref[p] = w
            sm_ref[p] = w * s_ref[p]
            lows.append((low0, low1, low2))
        put_rows(r0_ref, q, row_pairs(t_ref, lows[0][0], True))
        put_rows(r1_ref, q, row_pairs(t_ref, lows[0][1] + lows[1][1], False))
        put_rows(r2_ref, q, row_pairs(t_ref, lows[0][2] + lows[1][2], True))
        return carry

    lax.fori_loop(planes.start // 2, planes.stop // 2, diagonals, 0, unroll=len(planes) // 2)

    def leftovers(q, carry):
        total = jnp.zeros(shape, F32)
        for i in range(2):
            p = 2 * q + i
            total += KEEP * s_ref[p] + neighbours(sm_ref, f0_ref, f1_ref, f2_ref, p)
        put_rows(rs_ref, q, row_pairs(t_ref, total, True))
        return carry

    lax.fori_loop(planes.start // 2 + 1, planes.stop // 2 - 1, leftovers, 0, unroll=len(planes) // 2 - 2)

    pairs = one_hot(256, 128, lambda r, c: lax.shift_right_logical(r, 1) == c, 0.25)
    evens = one_hot(256, 128, lambda r, c: r == 2 * c, 0.25)
    first, count = planes.start // 2, len(planes) // 2
    for target, source, matrix in (
        (l10_ref, r0_ref, pairs), (l11_ref, r1_ref, pairs), (l12_ref, r2_ref, evens), (s1_ref, rs_ref, pairs)
    ):
        target[...] = jnp.zeros_like(target)
        value = spread(source[pl.ds(first, count)].reshape(count * rows_1, 256), matrix)
        value = value.reshape(count, rows_1, 128)
        target[pl.ds(first + 2, count)] = 2.0 * value if target is s1_ref else value

    first_row_1 = (iota(shape_1, 0) == own // 2) & at_y
    first_lane_1 = (iota(shape_1, 1) == 0) & at_z
    planes_1 = range(first + 2, first + 2 + count)

    def faces_1(p, carry):
        f10_ref[p] = jnp.where((p == 6) & at_x, 0.0, l10_ref[p])
        f11_ref[p] = jnp.where(first_row_1, 0.0, l11_ref[p])
        f12_ref[p] = jnp.where(first_lane_1, 0.0, l12_ref[p])
        return carry

    lax.fori_loop(planes_1.start, planes_1.stop, faces_1, 0, unroll=len(planes_1))
    f10_ref[planes_1.stop] = jnp.zeros(shape_1, F32)

    def diagonals_1(p, carry):
        d = (
            4.0 * ABSORB + l10_ref[p] + f10_ref[p + 1]
            + l11_ref[p] + turn(f11_ref[p], -1, 0)
            + l12_ref[p] + turn(f12_ref[p], -1, 1)
        )
        w1_ref[p] = RELAX / d
        return carry

    lax.fori_loop(planes_1.start, planes_1.stop, diagonals_1, 0, unroll=len(planes_1))
    if thin:
        pack_level_2(
            up_ref, down_ref, pay_ref, s1_ref, f10_ref, f11_ref, f12_ref, w1_ref, l10_ref, l11_ref, l12_ref, *refs
        )


def pack_level_2(
    up_ref, down_ref, pay_ref, s1_ref, f10_ref, f11_ref, f12_ref, w1_ref, l10_ref, l11_ref, l12_ref,
    sm1_ref, t1_ref, u_ref,
):
    for target, start in ((up_ref, 5), (down_ref, 9)):
        target[...] = jnp.zeros_like(target)
        for i, ref in enumerate((s1_ref, w1_ref, f10_ref)):
            for k in range(2):
                target[2 * i + k, pl.ds(4, 12), :] = ref[start + k, pl.ds(0, 12), :]
    for p in range(5, 11):
        sm1_ref[p] = w1_ref[p] * s1_ref[p]

    def quad(values, both):
        t1_ref[...] = values
        first = t1_ref[pl.ds(2, 4, 2), :]
        return first + t1_ref[pl.ds(3, 4, 2), :] if both else first

    def leftover_1(p):
        return KEEP * s1_ref[p] + neighbours(sm1_ref, f10_ref, f11_ref, f12_ref, p)

    row8, lane8 = iota((8, 128), 0), iota((8, 128), 1)
    narrow = one_hot(128, 128, lambda r, c: (lax.shift_right_logical(r, 1) == c) & (r < 64))
    narrow_even = one_hot(128, 128, lambda r, c: (r == 2 * c) & (r < 64))
    total = jnp.zeros((8, 128), F32)
    for f in range(4):
        for i in range(2):
            p = 6 + 2 * i
            if f == 0:
                part = quad(leftover_1(p) + leftover_1(p + 1), True)
            elif f == 1:
                part = quad(l10_ref[p], True)
            elif f == 2:
                part = quad(l11_ref[p] + l11_ref[p + 1], False)
            else:
                part = quad(l12_ref[p] + l12_ref[p + 1], True)
            u_ref[f, pl.ds(4 * i, 4), :] = part * (0.5 if f == 0 else 0.25)
        part = spread(u_ref[f], narrow_even if f == 3 else narrow)
        for i in range(2):
            for h in range(2):
                to = 32 * f + 16 * i
                moved = turn(turn(part, 4 * (h - i), 0), to - 16 * h, 1)
                here = (lax.shift_right_logical(row8, 2) == h) & (lane8 >= to) & (lane8 < to + 16)
                total = jnp.where(here, moved, total)
    pay_ref[...] = jnp.broadcast_to(total[None], pay_ref.shape)


def window(pieces, to, lane):
    out = pieces[3]
    for k in range(3):
        start = (to + 16 * k) % 128
        here = (lane >= start) & (lane < start + 16)
        out = jnp.where(here, pieces[k], out)
    return jnp.where(lane < 64, turn(out, -to, 1), 0.0)


def solve_2(s2, level_2, level_3, t3_ref, e_ref):
    f0, f1, f2, w = level_2
    g0, g1, g2, w3 = level_3
    nx, ny, _ = s2.shape
    sm = w * s2
    left = KEEP * s2 + neighbours_3d(sm, f0, f1, f2)
    s3 = coarse_2(left.reshape(nx // 2, 2, ny, 128).sum(1), t3_ref, True, 0.5, False)
    e = w3 * s3
    for _ in range(SWEEPS - 1):
        e = KEEP * e + w3 * (s3 + neighbours_3d(e, g0, g1, g2))
    widen = one_hot(128, 128, lambda r, c: (r == lax.shift_right_logical(c, 1)) & (c < 64))
    wide = spread(e.reshape(nx * ny // 4, 128), widen).reshape(nx // 2, ny // 2, 128)
    for x in range(nx // 2):
        for i in range(2):
            e_ref[x, pl.ds(i, ny // 2, 2), :] = wide[x]
    e2 = e_ref[...]
    corrected = sm + jnp.concatenate([e2[:, None], e2[:, None]], 1).reshape(nx, ny, 128)
    return KEEP * corrected + w * (s2 + neighbours_3d(corrected, f0, f1, f2))


def coarse_2(values, t3_ref, both, weight, even):
    nx, ny, _ = values.shape
    t3_ref[...] = values
    first = t3_ref[:, pl.ds(0, ny // 2, 2), :]
    if both:
        first = first + t3_ref[:, pl.ds(1, ny // 2, 2), :]
    if even:
        rule = lambda r, c: (r == 2 * c) & (r < 64)
    else:
        rule = lambda r, c: (lax.shift_right_logical(r, 1) == c) & (r < 64)
    flat = spread(first.reshape(nx * ny // 2, 128), one_hot(128, 128, rule, weight))
    return flat.reshape(nx, ny // 2, 128)


def coefficients(low, mask_lane, absorb):
    shape = low[0].shape
    f0 = jnp.where(iota(shape, 0) == 0, 0.0, low[0])
    f1 = jnp.where(iota(shape, 1) == 0, 0.0, low[1])
    f2 = jnp.where((iota(shape, 2) == mask_lane) & (lax.axis_index("gz") == 0), 0.0, low[2])
    d = (
        absorb + low[0] + jnp.concatenate([f0[1:], jnp.zeros_like(f0[:1])], 0)
        + low[1] + turn(f1, -1, 1) + low[2] + turn(f2, -1, 2)
    )
    return f0, f1, f2, RELAX / d


def fetch_level_2(m2_ref, planes, pick_ref):
    gx, gy = lax.axis_index("gx"), lax.axis_index("gy")
    ny = m2_ref.shape[1]

    def source(c):
        return jnp.where(c < 96, 16, -48) + lax.shift_right_logical(c, 1)

    widen = one_hot(128, 128, lambda r, c: r == source(c))
    rows = one_hot(24, ny, lambda r, c: c == 4 * gy - 3 + lax.shift_right_logical(r, 1))
    flat = m2_ref[pl.ds(2 * gx + planes.start, len(planes))].reshape(len(planes) * ny, 128)
    wide = spread(flat, widen).reshape(len(planes), ny, 128)
    for k in planes:
        pick_ref[k] = pick(rows, wide[k - planes.start])


def widen_level_1(m1_ref, wide_ref, lo, hi):
    rows = 24 * (hi - lo)
    widen = one_hot(128, 256, lambda r, c: r == lax.shift_right_logical(c, 1))
    wide_ref[pl.ds(lo, hi - lo)] = spread(m1_ref[pl.ds(lo, hi - lo)].reshape(rows, 128), widen).reshape(
        hi - lo, 24, 256
    )


def double_rows(t_ref, wide_ref, q, start=0, count=20):
    for half in range(2):
        part = wide_ref[q, pl.ds(start, count), pl.ds(128 * half, 128)]
        for i in range(2):
            t_ref[half, pl.ds(i, count, 2), :] = part
    return jnp.concatenate([t_ref[half, pl.ds(0, 2 * count), :] for half in range(2)], 1)


def second_kernel(
    s_ref, f0_ref, f1_ref, f2_ref, w_ref, d_ref,
    s1_ref, f10_ref, f11_ref, f12_ref, w1_ref,
    low_ref, high_ref, before_ref, own0_ref, own1_ref, after_ref,
    fp_out, im_out, im_ref, t1s_ref, f20_ref, f21_ref, f22_ref, w2_ref,
    f30_ref, f31_ref, f32_ref, w3_ref, pay_ref,
    v_ref, t3_ref, e_ref, m2_ref, pick_ref, corr1_ref, m1_ref, wide_ref, t_ref,
    corr_ref, fp_ref, sm_ref, rs_ref, sm1_ref, tq_ref,
):
    nx2, ny2 = f20_ref.shape[:2]
    lane8 = iota((8, 128), 1)
    row8 = iota((8, 128), 0)

    def assemble(x, carry):
        for pair in range(ny2 // 8):
            g = x * (ny2 // 8) + pair
            pieces = [turn(ref[g], 16 * k, 1) for k, ref in enumerate((before_ref, own0_ref, own1_ref, after_ref))]
            for f in range(4):
                for i in range(2):
                    v_ref[f, 2 * x + i, pl.ds(8 * pair, 8), :] = window(pieces, 32 * f + 16 * i, lane8)
        return carry

    lax.fori_loop(0, nx2 // 2, assemble, 0, unroll=8)

    s2 = v_ref[0]
    low = (v_ref[1], v_ref[2], v_ref[3])
    level_2 = coefficients(low, 16, 16.0 * ABSORB)
    f20_ref[...], f21_ref[...], f22_ref[...], w2_ref[...] = level_2
    halves = [t.reshape(nx2 // 2, 2, ny2, 128) for t in low]
    low_3 = (
        coarse_2(halves[0][:, 0], t3_ref, True, 0.25, False),
        coarse_2(halves[1].sum(1), t3_ref, False, 0.25, False),
        coarse_2(halves[2].sum(1), t3_ref, True, 0.25, True),
    )
    level_3 = coefficients(low_3, 8, 64.0 * ABSORB)
    f30_ref[...], f31_ref[...], f32_ref[...], w3_ref[...] = level_3
    m2_ref[...] = jnp.zeros_like(m2_ref)
    m2_ref[pl.ds(3, nx2)] = solve_2(s2, level_2, level_3, t3_ref, e_ref)
    fetch_level_2(m2_ref, range(8), pick_ref)

    def correct_1(p, carry):
        corr1_ref[p] = w1_ref[p] * s1_ref[p] + pick_ref[lax.shift_right_logical(p, 1)]
        return carry

    lax.fori_loop(3, 13, correct_1, 0, unroll=10)
    for k in range(2):
        corr1_ref[1 + k] = low_ref[2 + k] * low_ref[k] + pick_ref[(1 + k) // 2]
        corr1_ref[13 + k] = high_ref[2 + k] * high_ref[k] + pick_ref[(13 + k) // 2]

    def relax_1(p, carry):
        m1_ref[p] = KEEP * corr1_ref[p] + w1_ref[p] * (
            s1_ref[p] + neighbours(corr1_ref, f10_ref, f11_ref, f12_ref, p)
        )
        return carry

    lax.fori_loop(3, 13, relax_1, 0, unroll=10)
    for p, source, w, face, next_face in (
        (2, low_ref[1], low_ref[3], low_ref[5], f10_ref[3]),
        (13, high_ref[0], high_ref[2], f10_ref[13], high_ref[5]),
    ):
        m1_ref[p] = KEEP * corr1_ref[p] + w * (
            source + face * corr1_ref[p - 1] + next_face * corr1_ref[p + 1]
            + plane_terms(corr1_ref[p], f11_ref[p], f12_ref[p])
        )
    widen_level_1(m1_ref, wide_ref, 2, 14)

    def correct(q, carry):
        e = double_rows(t_ref, wide_ref, q)
        for i in range(2):
            p = 2 * q + i - 4
            corr_ref[p] = w_ref[p] * s_ref[p] + e
        return carry

    lax.fori_loop(2, 14, correct, 0, unroll=12)

    def relax(p, carry):
        fp_ref[p] = KEEP * corr_ref[p] + w_ref[p] * (
            s_ref[p] + neighbours(corr_ref, f0_ref, f1_ref, f2_ref, p)
        )
        return carry

    def relax_near(p, carry):
        fp_ref[p, NEAR, :] = KEEP * corr_ref[p, NEAR, :] + w_ref[p, NEAR, :] * (
            s_ref[p, NEAR, :] + near_rows(corr_ref, f0_ref, f1_ref, f2_ref, p)
        )
        return carry

    lax.fori_loop(2, 7, relax_near, 0, unroll=5)
    lax.fori_loop(7, 17, relax, 0, unroll=10)
    lax.fori_loop(17, 22, relax_near, 0, unroll=5)

    def image(p, carry):
        im = d_ref[p] * fp_ref[p] - neighbours(fp_ref, f0_ref, f1_ref, f2_ref, p)
        im_ref[p] = im
        sm_ref[p] = w_ref[p] * im
        return carry

    def image_near(p, carry):
        im = d_ref[p, NEAR, :] * fp_ref[p, NEAR, :] - near_rows(fp_ref, f0_ref, f1_ref, f2_ref, p)
        im_ref[p, NEAR, :] = im
        sm_ref[p, NEAR, :] = w_ref[p, NEAR, :] * im
        return carry

    lax.fori_loop(3, 8, image_near, 0, unroll=5)
    lax.fori_loop(8, 16, image, 0, unroll=8)
    lax.fori_loop(16, 21, image_near, 0, unroll=5)

    rs_ref[...] = jnp.zeros_like(rs_ref)
    inside = (iota((24, 128), 0) >= 4) & (iota((24, 128), 0) < 20)

    def leftovers(q, sums):
        total = jnp.zeros((24, 256), F32)
        for i in range(2):
            p = 2 * q + i - 4
            left = KEEP * im_ref[p, NEAR, :] + near_rows(sm_ref, f0_ref, f1_ref, f2_ref, p)
            total += left
            own = inside & (p >= 8) & (p < 16)
            fp, im = fp_ref[p, NEAR, 0:128], im_ref[p, NEAR, 0:128]
            terms = (s_ref[p, NEAR, 0:128] * fp, fp * im, sm_ref[p, NEAR, 0:128] * (im + left[:, 0:128]))
            sums = tuple(old + jnp.where(own, new, 0.0) for old, new in zip(sums, terms))
        put_rows(rs_ref, q - 4, row_pairs(t_ref, total, True), 4)
        return sums

    zero = jnp.zeros((24, 128), F32)
    sums = lax.fori_loop(4, 12, leftovers, (zero, zero, zero), unroll=8)

    for p in range(8):
        fp_out[p] = fp_ref[8 + p, pl.ds(12, 16), 0:128]
        im_out[p] = im_ref[8 + p, pl.ds(12, 16), 0:128]

    pairs = one_hot(256, 128, lambda r, c: lax.shift_right_logical(r, 1) == c, 0.5)
    t1s_ref[...] = jnp.zeros_like(t1s_ref)
    t1s_ref[pl.ds(4, 8)] = spread(rs_ref[...].reshape(192, 256), pairs).reshape(8, 24, 128)
    for p in range(5, 11):
        sm1_ref[p] = w1_ref[p] * t1s_ref[p]
    inside_1 = (iota((24, 128), 0) >= 6) & (iota((24, 128), 0) < 14) & (iota((24, 128), 1) < 64)
    second = jnp.zeros((24, 128), F32)
    halves = [jnp.zeros((8, 128), F32)] * 2
    tq_ref[...] = jnp.zeros_like(tq_ref)
    for i in range(2):
        total = jnp.zeros((24, 128), F32)
        for j in range(2):
            p = 6 + 2 * i + j
            s1 = t1s_ref[p]
            left = KEEP * s1 + neighbours(sm1_ref, f10_ref, f11_ref, f12_ref, p)
            second += jnp.where(inside_1, sm1_ref[p] * (s1 + left), 0.0)
            total += left
        tq_ref[pl.ds(0, 24), :] = total
        tq_ref[pl.ds(24, 4), :] = tq_ref[pl.ds(6, 4, 2), :] + tq_ref[pl.ds(7, 4, 2), :]
        for h in range(2):
            place = one_hot(
                128, 128,
                lambda r, c, i=i, h=h: (lax.shift_right_logical(r, 1) - 16 * h == (c & 15))
                & (r < 64) & ((lax.shift_right_logical(c, 4) & 1) == i), 0.5,
            )
            halves[h] += spread(tq_ref[pl.ds(24, 8), :], place)
    scalars = (jnp.sum(sums[0]), jnp.sum(sums[1]), jnp.sum(sums[2]) + 2.0 * jnp.sum(second))
    mine = lax.shift_right_logical(lane8, 5) == row8
    pay = jnp.zeros((8, 128), F32)
    for h in range(2):
        line = jnp.sum(jnp.where(mine, halves[h], 0.0), axis=0, keepdims=True)
        pay = jnp.where(row8 == h, line, pay)
    for k, value in enumerate(scalars):
        pay = jnp.where((lane8 == k) & (row8 == 2), value, pay)
    pay_ref[...] = jnp.broadcast_to(pay[None, :4], pay_ref.shape)


def third_kernel(
    f0_ref, f1_ref, f2_ref, w_ref, f10_ref, f11_ref, f12_ref, w1_ref,
    im_ref, t1s_ref, f20_ref, f21_ref, f22_ref, w2_ref, f30_ref, f31_ref, f32_ref, w3_ref,
    before_ref, own0_ref, own1_ref, after_ref, parts_ref,
    mi_out, scalar_out,
    v_ref, t3_ref, e_ref, m2_ref, pick_ref, corr1_ref, m1_ref, wide_ref, t_ref, corr_ref,
):
    nx2, ny2 = f20_ref.shape[:2]
    lane = iota((ny2 // 4, 128), 1)

    def assemble(x, carry):
        pieces = [turn(ref[x], 16 * k, 1) for k, ref in enumerate((before_ref, own0_ref, own1_ref, after_ref))]
        for i in range(2):
            for j in range(4):
                v_ref[2 * x + i, pl.ds(j, ny2 // 4, 4), :] = window(pieces, 32 * j + 16 * i, lane)
        return carry

    lax.fori_loop(0, nx2 // 2, assemble, 0, unroll=8)
    s2 = v_ref[...]
    level_2 = (f20_ref[...], f21_ref[...], f22_ref[...], w2_ref[...])
    level_3 = (f30_ref[...], f31_ref[...], f32_ref[...], w3_ref[...])
    m2 = solve_2(s2, level_2, level_3, t3_ref, e_ref)
    lane3 = iota(s2.shape, 2)
    part = 4.0 * jnp.sum(jnp.where((lane3 >= 16) & (lane3 < 48), s2 * m2, 0.0))
    sums = jnp.sum(jnp.sum(parts_ref[...], axis=0), axis=0, keepdims=True)
    scalar_out[...] = jnp.where(iota((1, 128), 1) == 3, part, sums)
    m2_ref[...] = jnp.zeros_like(m2_ref)
    m2_ref[pl.ds(3, nx2)] = m2
    fetch_level_2(m2_ref, range(2, 6), pick_ref)

    for p in range(4, 12):
        corr1_ref[p] = w1_ref[p] * t1s_ref[p] + pick_ref[p // 2]
    for p in range(5, 11):
        m1_ref[p] = KEEP * corr1_ref[p] + w1_ref[p] * (
            t1s_ref[p] + neighbours(corr1_ref, f10_ref, f11_ref, f12_ref, p)
        )
    widen_level_1(m1_ref, wide_ref, 5, 11)

    def correct(q, carry):
        e = double_rows(t_ref, wide_ref, q, 4, 12)
        for i in range(2):
            p = 2 * q + i - 4
            corr_ref[p, NEAR, :] = w_ref[p, NEAR, :] * im_ref[p, NEAR, :] + e
        return carry

    lax.fori_loop(5, 11, correct, 0, unroll=6)

    for p in range(8):
        q = 8 + p
        mi = KEEP * corr_ref[q, NEAR, :] + w_ref[q, NEAR, :] * (
            im_ref[q, NEAR, :] + near_rows(corr_ref, f0_ref, f1_ref, f2_ref, q)
        )
        mi_out[p] = mi[4:20, 0:128]


def last_kernel(sums_ref, s_ref, fp_ref, im_ref, mi_ref, solution_ref, residual_ref, direction_ref):
    total = jnp.sum(sums_ref[...], axis=0)
    lane = iota((1, 128), 1)

    def value(lanes):
        keep = lane == lanes[0]
        for k in lanes[1:]:
            keep = keep | (lane == k)
        return jnp.sum(jnp.where(keep, total, 0.0), axis=1, keepdims=True)

    projected, curvature, product = value((0,)), value((1,)), value((2, 3))
    step = projected / curvature
    share = product / curvature
    for p in range(8):
        fp = fp_ref[p]
        solution_ref[p] = step * fp
        residual_ref[p] = s_ref[p] - step * im_ref[p]
        direction_ref[p] = step * (share * fp - mi_ref[p])


def call(kernel, inputs, outs, scratch=(), keep_in=(), keep_out=(), space=pltpu.VMEM):
    vmem = pl.BlockSpec(memory_space=pltpu.VMEM)
    inputs = [
        pltpu.with_memory_space_constraint(value, space) if i in keep_in else value
        for i, value in enumerate(inputs)
    ]
    shapes = [
        pltpu.VMEM(shape, dtype) if i in keep_out else jax.ShapeDtypeStruct(shape, dtype)
        for i, (shape, dtype) in enumerate(outs)
    ]
    return pl.pallas_call(
        kernel,
        out_shape=shapes,
        in_specs=[pl.BlockSpec(memory_space=space)] * len(inputs),
        out_specs=[vmem] * len(outs),
        scratch_shapes=[pltpu.VMEM(shape, F32) if isinstance(shape, tuple) else shape for shape in scratch],
        compiler_params=pltpu.CompilerParams(vmem_limit_bytes=VMEM_LIMIT),
    )(*inputs)


def shift_along(value, axis, by):
    size = lax.axis_size(axis)
    return lax.ppermute(value, axis, [(i, i + by) for i in range(size) if 0 <= i + by < size])


def gather_plane(copies):
    copies = copies.reshape(copies.shape[0], 1, -1)
    return lax.all_to_all(copies, ("gx", "gy"), 0, 0, tiled=True)


def local(right_side, face_coefficients, solid):
    nx2, ny2 = 2 * lax.axis_size("gx"), 4 * lax.axis_size("gy")
    own, ends = call(
        prepare_kernel,
        [right_side, face_coefficients, solid],
        [((8, 5, 16, 128), BF16), ((8, 16, 128), BF16)],
        [
            (8, 16, 128),
            pltpu.VMEM((3, 8, 16, 128), BF16),
            pltpu.VMEM((8, 16, 128), jnp.int32),
            pltpu.SemaphoreType.DMA((3,)),
        ],
        keep_in=range(3),
        space=pltpu.HBM,
    )
    before, after = shift_along(ends, "gz", 1), shift_along(ends, "gz", -1)
    (own,) = call(rim_kernel, [own, before, after], [((8, 6, 16, 128), BF16)])
    block = jnp.concatenate([shift_along(own, "gx", 1), own, shift_along(own, "gx", -1)], axis=0)
    to_up, to_down = call(edges_kernel, [block], [((15, 6, 16, 128), BF16)] * 2)
    before, after = shift_along(to_up, "gy", 1), shift_along(to_down, "gy", -1)

    fine, fine_up = (24, 40, 256), (25, 40, 256)
    mid, mid_up = (16, 24, 128), (17, 24, 128)
    rows, wide, edge = (12, 24, 256), (16, 24, 256), (6, 24, 128)
    slim, slim_up, slim_mid, slim_mid_up, slim_rows = (
        (20, 24, 256), (21, 24, 256), (16, 16, 128), (17, 16, 128), (12, 16, 256)
    )
    up, down, pay = call(
        functools.partial(fine_kernel, True),
        [block, before, after],
        [(edge, F32), (edge, F32), ((lax.axis_size(("gx", "gy")), 8, 128), F32)],
        [slim, slim_up, slim, slim, slim_mid, slim_mid_up, slim_mid, slim_mid, slim_mid,
         slim, slim, slim, slim, (2, 24, 128), slim_rows, slim_rows, slim_rows, slim_rows,
         slim_mid, slim_mid, slim_mid, slim_mid, (16, 128), (4, 8, 128)],
    )
    state = call(
        functools.partial(fine_kernel, False),
        [block, before, after],
        [(shape, F32) for shape in (fine, fine_up, fine, fine, fine, fine, mid, mid_up, mid, mid, mid)],
        [fine, fine, fine, fine, (2, 40, 128), rows, rows, rows, rows, mid, mid, mid],
        keep_out=range(11),
    )
    low, high = shift_along(up, "gx", 1), shift_along(down, "gx", -1)
    own = gather_plane(pay)
    pairs = (nx2 * ny2 // 16, 8, 128)
    own, low, high = lax.optimization_barrier((own, low, high))
    own0, own1 = own[..., :512].reshape(pairs), own[..., 512:].reshape(pairs)
    before, after = shift_along(own1, "gz", 1), shift_along(own0, "gz", -1)
    level_2, level_3 = (nx2, ny2, 128), (nx2 // 2, ny2 // 2, 128)
    window = (nx2 + 6, ny2, 128)
    half = (nx2 // 2, ny2, 128)
    first_pre, image, *more, pay = call(
        second_kernel,
        [*state, low, high, before, own0, own1, after],
        [((8, 16, 128), F32)] * 2
        + [(shape, F32) for shape in (fine, mid, *[level_2] * 4, *[level_3] * 4, (nx2 * ny2 // 8, 4, 128))],
        [(4,) + level_2, half, half, window, (8, 24, 128), mid, mid, wide, (2, 40, 128),
         fine, fine, fine, (8, 24, 256), mid, (32, 128)],
        keep_in=range(11),
        keep_out=range(2, 12),
    )
    own = gather_plane(pay)
    plane = (nx2 // 2, ny2 // 4, 128)
    own0, own1, parts = (own[..., 128 * k : 128 * k + 128].reshape(plane) for k in range(3))
    before, after = shift_along(own1, "gz", 1), shift_along(own0, "gz", -1)
    _, f0, f1, f2, w, _, _, f10, f11, f12, w1 = state
    mapped, sums = call(
        third_kernel,
        [f0, f1, f2, w, f10, f11, f12, w1, *more, before, own0, own1, after, parts],
        [((8, 16, 128), F32), ((1, 128), F32)],
        [level_2, half, half, window, (8, 24, 128), mid, mid, wide, (2, 40, 128), fine],
        keep_in=range(18),
    )
    peers = lax.axis_size("gz")
    sums = lax.all_to_all(jnp.broadcast_to(sums[None], (peers, 1, 128)), "gz", 0, 0, tiled=True)
    return tuple(
        call(
            last_kernel,
            [sums, right_side, first_pre, image, mapped],
            [((8, 16, 128), F32)] * 3,
        )
    )


def solution(mesh):
    placed = P("gx", "gy", "gz")
    return jax.shard_map(
        local,
        mesh=mesh,
        in_specs=(placed, P(None, "gx", "gy", "gz"), placed),
        out_specs=(placed, placed, placed),
        check_vma=False,
    )
```

```python
import functools

import jax
import jax.numpy as jnp
from jax import lax
from jax.experimental import pallas as pl
from jax.experimental.pallas import tpu as pltpu
from jax.sharding import PartitionSpec as P

F32 = jnp.float32
BF16 = jnp.bfloat16
ABSORB = 0.001
RELAX = 0.8
KEEP = 0.2
SWEEPS = 6
NEAR = pl.ds(8, 24)
VMEM_LIMIT = 24 * 1024 * 1024


def one_hot(rows, cols, rule, weight=1.0):
    r = lax.broadcasted_iota(jnp.int32, (rows, cols), 0)
    c = lax.broadcasted_iota(jnp.int32, (rows, cols), 1)
    return jnp.where(rule(r, c), weight, 0.0).astype(BF16)


def spread(values, matrix):
    high = values.astype(BF16)
    low = (values - high.astype(F32)).astype(BF16)
    return jnp.dot(high, matrix, preferred_element_type=F32) + jnp.dot(
        low, matrix, preferred_element_type=F32
    )


def pick(matrix, values):
    high = values.astype(BF16)
    low = (values - high.astype(F32)).astype(BF16)
    return jnp.dot(matrix, high, preferred_element_type=F32) + jnp.dot(
        matrix, low, preferred_element_type=F32
    )


def root(values):
    return values * lax.rsqrt(jnp.maximum(values, 1e-12))


def turn(values, shift, axis):
    return pltpu.roll(values, shift % values.shape[axis], axis)


def iota(shape, dim):
    return lax.broadcasted_iota(jnp.int32, shape, dim)


def plane_terms(v, f1, f2):
    return turn(v, 1, 0) * f1 + turn(v * f1, -1, 0) + turn(v, 1, 1) * f2 + turn(v * f2, -1, 1)


def neighbours(v_ref, f0_ref, f1_ref, f2_ref, p):
    return (
        f0_ref[p] * v_ref[p - 1]
        + f0_ref[p + 1] * v_ref[p + 1]
        + plane_terms(v_ref[p], f1_ref[p], f2_ref[p])
    )


def near_rows(v_ref, f0_ref, f1_ref, f2_ref, p):
    v, f2 = v_ref[p, NEAR, :], f2_ref[p, NEAR, :]
    return (
        f0_ref[p, NEAR, :] * v_ref[p - 1, NEAR, :]
        + f0_ref[p + 1, NEAR, :] * v_ref[p + 1, NEAR, :]
        + f1_ref[p, NEAR, :] * v_ref[p, pl.ds(7, 24), :]
        + f1_ref[p, pl.ds(9, 24), :] * v_ref[p, pl.ds(9, 24), :]
        + turn(v, 1, 1) * f2
        + turn(v * f2, -1, 1)
    )


def neighbours_3d(v, f0, f1, f2):
    zero = jnp.zeros_like(v[:1])
    up = f0 * v
    return (
        f0 * jnp.concatenate([zero, v[:-1]], 0)
        + jnp.concatenate([up[1:], zero], 0)
        + turn(v, 1, 1) * f1
        + turn(v * f1, -1, 1)
        + turn(v, 1, 2) * f2
        + turn(v * f2, -1, 2)
    )


def row_pairs(t_ref, values, both):
    out = []
    pairs = values.shape[0] // 2
    for half in range(2):
        t_ref[half, pl.ds(0, 2 * pairs), :] = values[:, 128 * half : 128 * half + 128]
        first = t_ref[half, pl.ds(0, pairs, 2), :]
        out.append(first + t_ref[half, pl.ds(1, pairs, 2), :] if both else first)
    return out


def put_rows(r_ref, q, halves, start=0):
    for half in range(2):
        r_ref[q, pl.ds(start, halves[half].shape[0]), pl.ds(128 * half, 128)] = halves[half]


def prepare_kernel(s_hbm, fc_hbm, solid_hbm, out_ref, ends_ref, s_ref, fc_ref, solid_ref, sems):
    copies = [
        pltpu.make_async_copy(source, target, sems.at[i])
        for i, (source, target) in enumerate(
            ((s_hbm, s_ref), (fc_hbm, fc_ref), (solid_hbm, solid_ref))
        )
    ]
    for copy in copies:
        copy.start()
    for copy in copies:
        copy.wait()
    s = s_ref[...]
    high = s.astype(BF16)
    out_ref[:, 0] = high
    out_ref[:, 1] = (s - high.astype(F32)).astype(BF16)
    weight = 1.0 - 0.75 * solid_ref[...].astype(F32)
    for a in range(3):
        out_ref[:, 2 + a] = (fc_ref[a].astype(F32) * weight).astype(BF16)
    lane = iota((16, 128), 1)

    def body(p, carry):
        ends = jnp.zeros((16, 128), F32)
        for f in range(5):
            t = turn(out_ref[p, f].astype(F32), 24 * f + 12, 1)
            ends = jnp.where((lane >= 24 * f) & (lane < 24 * f + 24), t, ends)
        ends_ref[p] = ends.astype(BF16)
        return carry

    lax.fori_loop(0, 8, body, 0, unroll=4)


def rim_kernel(own_ref, before_ref, after_ref, out_ref):
    lane = iota((8, 16, 128), 2)
    last = jnp.zeros((8, 16, 128), jnp.bool_)
    for f in range(5):
        last = last | ((lane >= 24 * f) & (lane < 24 * f + 12))
    out_ref[:, 0:5] = own_ref[...]
    rim = jnp.where(last, before_ref[...].astype(F32), after_ref[...].astype(F32))
    out_ref[:, 5] = rim.astype(BF16)


def edges_kernel(x_ref, up_ref, down_ref):
    row = iota((8, 128), 0)
    quarters = [(p, True) for p in range(5, 19)] + [(0, False), (23, False)]

    def body(f, carry):
        for t in range(11):
            pair = [x_ref[1 + 2 * t + k, f].astype(F32) for k in range(2)]
            up_ref[t, f] = jnp.concatenate([v[8:] for v in pair], 0).astype(BF16)
            down_ref[t, f] = jnp.concatenate([v[:8] for v in pair], 0).astype(BF16)
        for t in range(4):
            ups, downs = [], []
            for k in range(0, 4, 2):
                pair = []
                for p, inner in quarters[4 * t + k : 4 * t + k + 2]:
                    v = x_ref[p, f].astype(F32)
                    pair.append((v[:8], v[8:]) if inner else (v[8:], v[:8]))
                ups.append(jnp.where(row < 4, turn(pair[0][0], 4, 0), pair[1][0]))
                downs.append(jnp.where(row < 4, pair[0][1], turn(pair[1][1], 4, 0)))
            up_ref[11 + t, f] = jnp.concatenate(ups, 0).astype(BF16)
            down_ref[11 + t, f] = jnp.concatenate(downs, 0).astype(BF16)
        return carry

    lax.fori_loop(0, 6, body, 0, unroll=2)


def edge_rows(ym_ref, yp_ref, p, f, thin):
    row = iota((8, 128), 0)
    zero = jnp.zeros((8, 128), F32)

    def eight(ref, tile, k):
        return ref[tile, f].astype(F32)[8 * k : 8 * k + 8]

    def four(q, before):
        v = eight(ym_ref if before else yp_ref, 11 + q // 4, q % 4 // 2)
        moved = turn(v, 4, 0) if (q % 2 == 0) == before else v
        return jnp.where((row >= 4) == before, moved, 0.0)

    if p in (0, 23):
        q = 14 if p == 0 else 15
        near_before, near_after = four(q, True), four(q, False)
    else:
        near_before, near_after = (eight(ref, (p - 1) // 2, (p - 1) % 2) for ref in (ym_ref, yp_ref))
    if thin:
        return near_before, near_after
    if 5 <= p <= 18:
        far_before, far_after = four(p - 5, True), four(p - 5, False)
    else:
        far_before = far_after = zero
    return jnp.concatenate([far_before, near_before], 0), jnp.concatenate([near_after, far_after], 0)


def fine_kernel(thin, x_ref, yp_ref, ym_ref, *refs):
    if thin:
        (up_ref, down_ref, pay_ref,
         s_ref, f0_ref, f1_ref, f2_ref, s1_ref, f10_ref, f11_ref, f12_ref, w1_ref, *refs) = refs
    else:
        s_ref, f0_ref, f1_ref, f2_ref, w_ref, d_ref, s1_ref, f10_ref, f11_ref, f12_ref, w1_ref, *refs = refs
    (c0_ref, c1_ref, c2_ref, sm_ref, t_ref, r0_ref, r1_ref, r2_ref, rs_ref,
     l10_ref, l11_ref, l12_ref, *refs) = refs
    planes = range(4, 20) if thin else range(24)
    rows, rows_1 = s_ref.shape[1], s1_ref.shape[1]
    own = 4 if thin else 12
    shape, shape_1 = (rows, 256), (rows_1, 128)
    at_x = lax.axis_index("gx") == 0
    at_y = lax.axis_index("gy") == 0
    at_z = lax.axis_index("gz") == 0
    lane = iota((rows, 128), 1)
    side = (lane < 12) | (lane >= 116)

    for p in planes:
        tiles = []
        for f in range(6):
            before, after = edge_rows(ym_ref, yp_ref, p, f, thin)
            column = jnp.concatenate([before, x_ref[p, f].astype(F32), after], 0)
            tiles.append(turn(column, -4, 0)[:rows])
        rims = [
            jnp.where(side, turn(tiles[5], -(24 * f + 12), 1), 0.0) for f in range(5)
        ]
        s_ref[p, :, 0:128] = tiles[0] + tiles[1]
        s_ref[p, :, 128:256] = rims[0] + rims[1]
        for a, c_ref in enumerate((c0_ref, c1_ref, c2_ref)):
            c_ref[p, :, 0:128] = tiles[2 + a]
            c_ref[p, :, 128:256] = rims[2 + a]

    def faces(p, carry):
        before = jnp.maximum(p - 1, planes.start)
        f0_ref[p] = root(c0_ref[p] * c0_ref[before])
        c1 = c1_ref[p]
        f1_ref[p] = root(c1 * turn(c1, 1, 0))
        c2 = c2_ref[p]
        f2_ref[p] = root(c2 * turn(c2, 1, 1))
        return carry

    lax.fori_loop(planes.start, planes.stop, faces, 0, unroll=len(planes))
    f0_ref[planes.stop] = jnp.zeros(shape, F32)

    first_row = (iota(shape, 0) == own) & at_y
    first_lane = (iota(shape, 1) == 0) & at_z
    for ref in (r0_ref, r1_ref, r2_ref, rs_ref):
        ref[...] = jnp.zeros_like(ref)

    def diagonals(q, carry):
        lows = []
        for i in range(2):
            p = 2 * q + i
            f0, f1, f2 = f0_ref[p], f1_ref[p], f2_ref[p]
            low0 = f0 + jnp.where((p == 8) & at_x, c0_ref[p], 0.0)
            low1 = f1 + jnp.where(first_row, c1_ref[p], 0.0)
            low2 = f2 + jnp.where(first_lane, c2_ref[p], 0.0)
            d = ABSORB + low0 + f0_ref[p + 1] + low1 + turn(f1, -1, 0) + low2 + turn(f2, -1, 1)
            w = RELAX / d
            if not thin:
                d_ref[p] = d
                w_ref[p] = w
            sm_ref[p] = w * s_ref[p]
            lows.append((low0, low1, low2))
        put_rows(r0_ref, q, row_pairs(t_ref, lows[0][0], True))
        put_rows(r1_ref, q, row_pairs(t_ref, lows[0][1] + lows[1][1], False))
        put_rows(r2_ref, q, row_pairs(t_ref, lows[0][2] + lows[1][2], True))
        return carry

    lax.fori_loop(planes.start // 2, planes.stop // 2, diagonals, 0, unroll=len(planes) // 2)

    def leftovers(q, carry):
        total = jnp.zeros(shape, F32)
        for i in range(2):
            p = 2 * q + i
            total += KEEP * s_ref[p] + neighbours(sm_ref, f0_ref, f1_ref, f2_ref, p)
        put_rows(rs_ref, q, row_pairs(t_ref, total, True))
        return carry

    lax.fori_loop(planes.start // 2 + 1, planes.stop // 2 - 1, leftovers, 0, unroll=len(planes) // 2 - 2)

    pairs = one_hot(256, 128, lambda r, c: lax.shift_right_logical(r, 1) == c, 0.25)
    evens = one_hot(256, 128, lambda r, c: r == 2 * c, 0.25)
    first, count = planes.start // 2, len(planes) // 2
    for target, source, matrix in (
        (l10_ref, r0_ref, pairs), (l11_ref, r1_ref, pairs), (l12_ref, r2_ref, evens), (s1_ref, rs_ref, pairs)
    ):
        target[...] = jnp.zeros_like(target)
        value = spread(source[pl.ds(first, count)].reshape(count * rows_1, 256), matrix)
        value = value.reshape(count, rows_1, 128)
        target[pl.ds(first + 2, count)] = 2.0 * value if target is s1_ref else value

    first_row_1 = (iota(shape_1, 0) == own // 2) & at_y
    first_lane_1 = (iota(shape_1, 1) == 0) & at_z
    planes_1 = range(first + 2, first + 2 + count)

    def faces_1(p, carry):
        f10_ref[p] = jnp.where((p == 6) & at_x, 0.0, l10_ref[p])
        f11_ref[p] = jnp.where(first_row_1, 0.0, l11_ref[p])
        f12_ref[p] = jnp.where(first_lane_1, 0.0, l12_ref[p])
        return carry

    lax.fori_loop(planes_1.start, planes_1.stop, faces_1, 0, unroll=len(planes_1))
    f10_ref[planes_1.stop] = jnp.zeros(shape_1, F32)

    def diagonals_1(p, carry):
        d = (
            4.0 * ABSORB + l10_ref[p] + f10_ref[p + 1]
            + l11_ref[p] + turn(f11_ref[p], -1, 0)
            + l12_ref[p] + turn(f12_ref[p], -1, 1)
        )
        w1_ref[p] = RELAX / d
        return carry

    lax.fori_loop(planes_1.start, planes_1.stop, diagonals_1, 0, unroll=len(planes_1))
    if thin:
        pack_level_2(
            up_ref, down_ref, pay_ref, s1_ref, f10_ref, f11_ref, f12_ref, w1_ref, l10_ref, l11_ref, l12_ref, *refs
        )


def pack_level_2(
    up_ref, down_ref, pay_ref, s1_ref, f10_ref, f11_ref, f12_ref, w1_ref, l10_ref, l11_ref, l12_ref,
    sm1_ref, t1_ref, u_ref,
):
    for target, start in ((up_ref, 5), (down_ref, 9)):
        target[...] = jnp.zeros_like(target)
        for i, ref in enumerate((s1_ref, w1_ref, f10_ref)):
            for k in range(2):
                target[2 * i + k, pl.ds(4, 12), :] = ref[start + k, pl.ds(0, 12), :]
    for p in range(5, 11):
        sm1_ref[p] = w1_ref[p] * s1_ref[p]

    def quad(values, both):
        t1_ref[...] = values
        first = t1_ref[pl.ds(2, 4, 2), :]
        return first + t1_ref[pl.ds(3, 4, 2), :] if both else first

    def leftover_1(p):
        return KEEP * s1_ref[p] + neighbours(sm1_ref, f10_ref, f11_ref, f12_ref, p)

    row8, lane8 = iota((8, 128), 0), iota((8, 128), 1)
    narrow = one_hot(128, 128, lambda r, c: (lax.shift_right_logical(r, 1) == c) & (r < 64))
    narrow_even = one_hot(128, 128, lambda r, c: (r == 2 * c) & (r < 64))
    total = jnp.zeros((8, 128), F32)
    for f in range(4):
        for i in range(2):
            p = 6 + 2 * i
            if f == 0:
                part = quad(leftover_1(p) + leftover_1(p + 1), True)
            elif f == 1:
                part = quad(l10_ref[p], True)
            elif f == 2:
                part = quad(l11_ref[p] + l11_ref[p + 1], False)
            else:
                part = quad(l12_ref[p] + l12_ref[p + 1], True)
            u_ref[f, pl.ds(4 * i, 4), :] = part * (0.5 if f == 0 else 0.25)
        part = spread(u_ref[f], narrow_even if f == 3 else narrow)
        for i in range(2):
            for h in range(2):
                to = 32 * f + 16 * i
                moved = turn(turn(part, 4 * (h - i), 0), to - 16 * h, 1)
                here = (lax.shift_right_logical(row8, 2) == h) & (lane8 >= to) & (lane8 < to + 16)
                total = jnp.where(here, moved, total)
    pay_ref[...] = jnp.broadcast_to(total[None], pay_ref.shape)


def window(pieces, to, lane):
    out = pieces[3]
    for k in range(3):
        start = (to + 16 * k) % 128
        here = (lane >= start) & (lane < start + 16)
        out = jnp.where(here, pieces[k], out)
    return jnp.where(lane < 64, turn(out, -to, 1), 0.0)


def solve_2(s2, level_2, level_3, t3_ref, e_ref):
    f0, f1, f2, w = level_2
    g0, g1, g2, w3 = level_3
    nx, ny, _ = s2.shape
    sm = w * s2
    left = KEEP * s2 + neighbours_3d(sm, f0, f1, f2)
    s3 = coarse_2(left.reshape(nx // 2, 2, ny, 128).sum(1), t3_ref, True, 0.5, False)
    e = w3 * s3
    for _ in range(SWEEPS - 1):
        e = KEEP * e + w3 * (s3 + neighbours_3d(e, g0, g1, g2))
    widen = one_hot(128, 128, lambda r, c: (r == lax.shift_right_logical(c, 1)) & (c < 64))
    wide = spread(e.reshape(nx * ny // 4, 128), widen).reshape(nx // 2, ny // 2, 128)
    for x in range(nx // 2):
        for i in range(2):
            e_ref[x, pl.ds(i, ny // 2, 2), :] = wide[x]
    e2 = e_ref[...]
    corrected = sm + jnp.concatenate([e2[:, None], e2[:, None]], 1).reshape(nx, ny, 128)
    return KEEP * corrected + w * (s2 + neighbours_3d(corrected, f0, f1, f2))


def coarse_2(values, t3_ref, both, weight, even):
    nx, ny, _ = values.shape
    t3_ref[...] = values
    first = t3_ref[:, pl.ds(0, ny // 2, 2), :]
    if both:
        first = first + t3_ref[:, pl.ds(1, ny // 2, 2), :]
    if even:
        rule = lambda r, c: (r == 2 * c) & (r < 64)
    else:
        rule = lambda r, c: (lax.shift_right_logical(r, 1) == c) & (r < 64)
    flat = spread(first.reshape(nx * ny // 2, 128), one_hot(128, 128, rule, weight))
    return flat.reshape(nx, ny // 2, 128)


def coefficients(low, mask_lane, absorb):
    shape = low[0].shape
    f0 = jnp.where(iota(shape, 0) == 0, 0.0, low[0])
    f1 = jnp.where(iota(shape, 1) == 0, 0.0, low[1])
    f2 = jnp.where((iota(shape, 2) == mask_lane) & (lax.axis_index("gz") == 0), 0.0, low[2])
    d = (
        absorb + low[0] + jnp.concatenate([f0[1:], jnp.zeros_like(f0[:1])], 0)
        + low[1] + turn(f1, -1, 1) + low[2] + turn(f2, -1, 2)
    )
    return f0, f1, f2, RELAX / d


def fetch_level_2(m2_ref, planes, pick_ref):
    gx, gy = lax.axis_index("gx"), lax.axis_index("gy")
    ny = m2_ref.shape[1]

    def source(c):
        return jnp.where(c < 96, 16, -48) + lax.shift_right_logical(c, 1)

    widen = one_hot(128, 128, lambda r, c: r == source(c))
    rows = one_hot(24, ny, lambda r, c: c == 4 * gy - 3 + lax.shift_right_logical(r, 1))
    flat = m2_ref[pl.ds(2 * gx + planes.start, len(planes))].reshape(len(planes) * ny, 128)
    wide = spread(flat, widen).reshape(len(planes), ny, 128)
    for k in planes:
        pick_ref[k] = pick(rows, wide[k - planes.start])


def widen_level_1(m1_ref, wide_ref, lo, hi):
    rows = 24 * (hi - lo)
    widen = one_hot(128, 256, lambda r, c: r == lax.shift_right_logical(c, 1))
    wide_ref[pl.ds(lo, hi - lo)] = spread(m1_ref[pl.ds(lo, hi - lo)].reshape(rows, 128), widen).reshape(
        hi - lo, 24, 256
    )


def double_rows(t_ref, wide_ref, q, start=0, count=20):
    for half in range(2):
        part = wide_ref[q, pl.ds(start, count), pl.ds(128 * half, 128)]
        for i in range(2):
            t_ref[half, pl.ds(i, count, 2), :] = part
    return jnp.concatenate([t_ref[half, pl.ds(0, 2 * count), :] for half in range(2)], 1)


def second_kernel(
    s_ref, f0_ref, f1_ref, f2_ref, w_ref, d_ref,
    s1_ref, f10_ref, f11_ref, f12_ref, w1_ref,
    low_ref, high_ref, before_ref, own0_ref, own1_ref, after_ref,
    fp_out, im_out, im_ref, t1s_ref, f20_ref, f21_ref, f22_ref, w2_ref,
    f30_ref, f31_ref, f32_ref, w3_ref, pay_ref,
    v_ref, t3_ref, e_ref, m2_ref, pick_ref, corr1_ref, m1_ref, wide_ref, t_ref,
    corr_ref, fp_ref, sm_ref, rs_ref, sm1_ref, tq_ref,
):
    nx2, ny2 = f20_ref.shape[:2]
    lane8 = iota((8, 128), 1)
    row8 = iota((8, 128), 0)

    def assemble(x, carry):
        for pair in range(ny2 // 8):
            g = x * (ny2 // 8) + pair
            pieces = [turn(ref[g], 16 * k, 1) for k, ref in enumerate((before_ref, own0_ref, own1_ref, after_ref))]
            for f in range(4):
                for i in range(2):
                    v_ref[f, 2 * x + i, pl.ds(8 * pair, 8), :] = window(pieces, 32 * f + 16 * i, lane8)
        return carry

    lax.fori_loop(0, nx2 // 2, assemble, 0, unroll=8)

    s2 = v_ref[0]
    low = (v_ref[1], v_ref[2], v_ref[3])
    level_2 = coefficients(low, 16, 16.0 * ABSORB)
    f20_ref[...], f21_ref[...], f22_ref[...], w2_ref[...] = level_2
    halves = [t.reshape(nx2 // 2, 2, ny2, 128) for t in low]
    low_3 = (
        coarse_2(halves[0][:, 0], t3_ref, True, 0.25, False),
        coarse_2(halves[1].sum(1), t3_ref, False, 0.25, False),
        coarse_2(halves[2].sum(1), t3_ref, True, 0.25, True),
    )
    level_3 = coefficients(low_3, 8, 64.0 * ABSORB)
    f30_ref[...], f31_ref[...], f32_ref[...], w3_ref[...] = level_3
    m2_ref[...] = jnp.zeros_like(m2_ref)
    m2_ref[pl.ds(3, nx2)] = solve_2(s2, level_2, level_3, t3_ref, e_ref)
    fetch_level_2(m2_ref, range(8), pick_ref)

    def correct_1(p, carry):
        corr1_ref[p] = w1_ref[p] * s1_ref[p] + pick_ref[lax.shift_right_logical(p, 1)]
        return carry

    lax.fori_loop(3, 13, correct_1, 0, unroll=10)
    for k in range(2):
        corr1_ref[1 + k] = low_ref[2 + k] * low_ref[k] + pick_ref[(1 + k) // 2]
        corr1_ref[13 + k] = high_ref[2 + k] * high_ref[k] + pick_ref[(13 + k) // 2]

    def relax_1(p, carry):
        m1_ref[p] = KEEP * corr1_ref[p] + w1_ref[p] * (
            s1_ref[p] + neighbours(corr1_ref, f10_ref, f11_ref, f12_ref, p)
        )
        return carry

    lax.fori_loop(3, 13, relax_1, 0, unroll=10)
    for p, source, w, face, next_face in (
        (2, low_ref[1], low_ref[3], low_ref[5], f10_ref[3]),
        (13, high_ref[0], high_ref[2], f10_ref[13], high_ref[5]),
    ):
        m1_ref[p] = KEEP * corr1_ref[p] + w * (
            source + face * corr1_ref[p - 1] + next_face * corr1_ref[p + 1]
            + plane_terms(corr1_ref[p], f11_ref[p], f12_ref[p])
        )
    widen_level_1(m1_ref, wide_ref, 2, 14)

    def correct(q, carry):
        e = double_rows(t_ref, wide_ref, q)
        for i in range(2):
            p = 2 * q + i - 4
            corr_ref[p] = w_ref[p] * s_ref[p] + e
        return carry

    lax.fori_loop(2, 14, correct, 0, unroll=12)

    def relax(p, carry):
        fp_ref[p] = KEEP * corr_ref[p] + w_ref[p] * (
            s_ref[p] + neighbours(corr_ref, f0_ref, f1_ref, f2_ref, p)
        )
        return carry

    def relax_near(p, carry):
        fp_ref[p, NEAR, :] = KEEP * corr_ref[p, NEAR, :] + w_ref[p, NEAR, :] * (
            s_ref[p, NEAR, :] + near_rows(corr_ref, f0_ref, f1_ref, f2_ref, p)
        )
        return carry

    lax.fori_loop(2, 7, relax_near, 0, unroll=5)
    lax.fori_loop(7, 17, relax, 0, unroll=10)
    lax.fori_loop(17, 22, relax_near, 0, unroll=5)

    def image(p, carry):
        im = d_ref[p] * fp_ref[p] - neighbours(fp_ref, f0_ref, f1_ref, f2_ref, p)
        im_ref[p] = im
        sm_ref[p] = w_ref[p] * im
        return carry

    def image_near(p, carry):
        im = d_ref[p, NEAR, :] * fp_ref[p, NEAR, :] - near_rows(fp_ref, f0_ref, f1_ref, f2_ref, p)
        im_ref[p, NEAR, :] = im
        sm_ref[p, NEAR, :] = w_ref[p, NEAR, :] * im
        return carry

    lax.fori_loop(3, 8, image_near, 0, unroll=5)
    lax.fori_loop(8, 16, image, 0, unroll=8)
    lax.fori_loop(16, 21, image_near, 0, unroll=5)

    rs_ref[...] = jnp.zeros_like(rs_ref)
    inside = (iota((24, 128), 0) >= 4) & (iota((24, 128), 0) < 20)

    def leftovers(q, sums):
        total = jnp.zeros((24, 256), F32)
        for i in range(2):
            p = 2 * q + i - 4
            left = KEEP * im_ref[p, NEAR, :] + near_rows(sm_ref, f0_ref, f1_ref, f2_ref, p)
            total += left
            own = inside & (p >= 8) & (p < 16)
            fp, im = fp_ref[p, NEAR, 0:128], im_ref[p, NEAR, 0:128]
            terms = (s_ref[p, NEAR, 0:128] * fp, fp * im, sm_ref[p, NEAR, 0:128] * (im + left[:, 0:128]))
            sums = tuple(old + jnp.where(own, new, 0.0) for old, new in zip(sums, terms))
        put_rows(rs_ref, q - 4, row_pairs(t_ref, total, True), 4)
        return sums

    zero = jnp.zeros((24, 128), F32)
    sums = lax.fori_loop(4, 12, leftovers, (zero, zero, zero), unroll=8)

    for p in range(8):
        fp_out[p] = fp_ref[8 + p, pl.ds(12, 16), 0:128]
        im_out[p] = im_ref[8 + p, pl.ds(12, 16), 0:128]

    pairs = one_hot(256, 128, lambda r, c: lax.shift_right_logical(r, 1) == c, 0.5)
    t1s_ref[...] = jnp.zeros_like(t1s_ref)
    t1s_ref[pl.ds(4, 8)] = spread(rs_ref[...].reshape(192, 256), pairs).reshape(8, 24, 128)
    for p in range(5, 11):
        sm1_ref[p] = w1_ref[p] * t1s_ref[p]
    inside_1 = (iota((24, 128), 0) >= 6) & (iota((24, 128), 0) < 14) & (iota((24, 128), 1) < 64)
    second = jnp.zeros((24, 128), F32)
    halves = [jnp.zeros((8, 128), F32)] * 2
    tq_ref[...] = jnp.zeros_like(tq_ref)
    for i in range(2):
        total = jnp.zeros((24, 128), F32)
        for j in range(2):
            p = 6 + 2 * i + j
            s1 = t1s_ref[p]
            left = KEEP * s1 + neighbours(sm1_ref, f10_ref, f11_ref, f12_ref, p)
            second += jnp.where(inside_1, sm1_ref[p] * (s1 + left), 0.0)
            total += left
        tq_ref[pl.ds(0, 24), :] = total
        tq_ref[pl.ds(24, 4), :] = tq_ref[pl.ds(6, 4, 2), :] + tq_ref[pl.ds(7, 4, 2), :]
        for h in range(2):
            place = one_hot(
                128, 128,
                lambda r, c, i=i, h=h: (lax.shift_right_logical(r, 1) - 16 * h == (c & 15))
                & (r < 64) & ((lax.shift_right_logical(c, 4) & 1) == i), 0.5,
            )
            halves[h] += spread(tq_ref[pl.ds(24, 8), :], place)
    scalars = (jnp.sum(sums[0]), jnp.sum(sums[1]), jnp.sum(sums[2]) + 2.0 * jnp.sum(second))
    mine = lax.shift_right_logical(lane8, 5) == row8
    pay = jnp.zeros((8, 128), F32)
    for h in range(2):
        line = jnp.sum(jnp.where(mine, halves[h], 0.0), axis=0, keepdims=True)
        pay = jnp.where(row8 == h, line, pay)
    for k, value in enumerate(scalars):
        pay = jnp.where((lane8 == k) & (row8 == 2), value, pay)
    pay_ref[...] = jnp.broadcast_to(pay[None, :4], pay_ref.shape)


def third_kernel(
    f0_ref, f1_ref, f2_ref, w_ref, f10_ref, f11_ref, f12_ref, w1_ref,
    im_ref, t1s_ref, f20_ref, f21_ref, f22_ref, w2_ref, f30_ref, f31_ref, f32_ref, w3_ref,
    before_ref, own0_ref, own1_ref, after_ref, parts_ref,
    mi_out, scalar_out,
    v_ref, t3_ref, e_ref, m2_ref, pick_ref, corr1_ref, m1_ref, wide_ref, t_ref, corr_ref,
):
    nx2, ny2 = f20_ref.shape[:2]
    lane = iota((ny2 // 4, 128), 1)

    def assemble(x, carry):
        pieces = [turn(ref[x], 16 * k, 1) for k, ref in enumerate((before_ref, own0_ref, own1_ref, after_ref))]
        for i in range(2):
            for j in range(4):
                v_ref[2 * x + i, pl.ds(j, ny2 // 4, 4), :] = window(pieces, 32 * j + 16 * i, lane)
        return carry

    lax.fori_loop(0, nx2 // 2, assemble, 0, unroll=8)
    s2 = v_ref[...]
    level_2 = (f20_ref[...], f21_ref[...], f22_ref[...], w2_ref[...])
    level_3 = (f30_ref[...], f31_ref[...], f32_ref[...], w3_ref[...])
    m2 = solve_2(s2, level_2, level_3, t3_ref, e_ref)
    lane3 = iota(s2.shape, 2)
    part = 4.0 * jnp.sum(jnp.where((lane3 >= 16) & (lane3 < 48), s2 * m2, 0.0))
    sums = jnp.sum(jnp.sum(parts_ref[...], axis=0), axis=0, keepdims=True)
    scalar_out[...] = jnp.where(iota((1, 128), 1) == 3, part, sums)
    m2_ref[...] = jnp.zeros_like(m2_ref)
    m2_ref[pl.ds(3, nx2)] = m2
    fetch_level_2(m2_ref, range(2, 6), pick_ref)

    for p in range(4, 12):
        corr1_ref[p] = w1_ref[p] * t1s_ref[p] + pick_ref[p // 2]
    for p in range(5, 11):
        m1_ref[p] = KEEP * corr1_ref[p] + w1_ref[p] * (
            t1s_ref[p] + neighbours(corr1_ref, f10_ref, f11_ref, f12_ref, p)
        )
    widen_level_1(m1_ref, wide_ref, 5, 11)

    def correct(q, carry):
        e = double_rows(t_ref, wide_ref, q, 4, 12)
        for i in range(2):
            p = 2 * q + i - 4
            corr_ref[p, NEAR, :] = w_ref[p, NEAR, :] * im_ref[p, NEAR, :] + e
        return carry

    lax.fori_loop(5, 11, correct, 0, unroll=6)

    for p in range(8):
        q = 8 + p
        mi = KEEP * corr_ref[q, NEAR, :] + w_ref[q, NEAR, :] * (
            im_ref[q, NEAR, :] + near_rows(corr_ref, f0_ref, f1_ref, f2_ref, q)
        )
        mi_out[p] = mi[4:20, 0:128]


def last_kernel(sums_ref, s_ref, fp_ref, im_ref, mi_ref, solution_ref, residual_ref, direction_ref):
    total = jnp.sum(sums_ref[...], axis=0)
    lane = iota((1, 128), 1)

    def value(lanes):
        keep = lane == lanes[0]
        for k in lanes[1:]:
            keep = keep | (lane == k)
        return jnp.sum(jnp.where(keep, total, 0.0), axis=1, keepdims=True)

    projected, curvature, product = value((0,)), value((1,)), value((2, 3))
    step = projected / curvature
    share = product / curvature
    for p in range(8):
        fp = fp_ref[p]
        solution_ref[p] = step * fp
        residual_ref[p] = s_ref[p] - step * im_ref[p]
        direction_ref[p] = step * (share * fp - mi_ref[p])


def call(kernel, inputs, outs, scratch=(), keep_in=(), keep_out=(), space=pltpu.VMEM):
    vmem = pl.BlockSpec(memory_space=pltpu.VMEM)
    inputs = [
        pltpu.with_memory_space_constraint(value, space) if i in keep_in else value
        for i, value in enumerate(inputs)
    ]
    shapes = [
        pltpu.VMEM(shape, dtype) if i in keep_out else jax.ShapeDtypeStruct(shape, dtype)
        for i, (shape, dtype) in enumerate(outs)
    ]
    return pl.pallas_call(
        kernel,
        out_shape=shapes,
        in_specs=[pl.BlockSpec(memory_space=space)] * len(inputs),
        out_specs=[vmem] * len(outs),
        scratch_shapes=[pltpu.VMEM(shape, F32) if isinstance(shape, tuple) else shape for shape in scratch],
        compiler_params=pltpu.CompilerParams(vmem_limit_bytes=VMEM_LIMIT),
    )(*inputs)


def shift_along(value, axis, by):
    size = lax.axis_size(axis)
    return lax.ppermute(value, axis, [(i, i + by) for i in range(size) if 0 <= i + by < size])


def gather_plane(copies):
    copies = copies.reshape(copies.shape[0], 1, -1)
    return lax.all_to_all(copies, ("gx", "gy"), 0, 0, tiled=True)


def local(right_side, face_coefficients, solid):
    nx2, ny2 = 2 * lax.axis_size("gx"), 4 * lax.axis_size("gy")
    own, ends = call(
        prepare_kernel,
        [right_side, face_coefficients, solid],
        [((8, 5, 16, 128), BF16), ((8, 16, 128), BF16)],
        [
            (8, 16, 128),
            pltpu.VMEM((3, 8, 16, 128), BF16),
            pltpu.VMEM((8, 16, 128), jnp.int32),
            pltpu.SemaphoreType.DMA((3,)),
        ],
        keep_in=range(3),
        space=pltpu.HBM,
    )
    before, after = shift_along(ends, "gz", 1), shift_along(ends, "gz", -1)
    (own,) = call(rim_kernel, [own, before, after], [((8, 6, 16, 128), BF16)])
    block = jnp.concatenate([shift_along(own, "gx", 1), own, shift_along(own, "gx", -1)], axis=0)
    to_up, to_down = call(edges_kernel, [block], [((15, 6, 16, 128), BF16)] * 2)
    before, after = shift_along(to_up, "gy", 1), shift_along(to_down, "gy", -1)

    fine, fine_up = (24, 40, 256), (25, 40, 256)
    mid, mid_up = (16, 24, 128), (17, 24, 128)
    rows, wide, edge = (12, 24, 256), (16, 24, 256), (6, 24, 128)
    slim, slim_up, slim_mid, slim_mid_up, slim_rows = (
        (20, 24, 256), (21, 24, 256), (16, 16, 128), (17, 16, 128), (12, 16, 256)
    )
    up, down, pay = call(
        functools.partial(fine_kernel, True),
        [block, after, before],
        [(edge, F32), (edge, F32), ((lax.axis_size(("gx", "gy")), 8, 128), F32)],
        [slim, slim_up, slim, slim, slim_mid, slim_mid_up, slim_mid, slim_mid, slim_mid,
         slim, slim, slim, slim, (2, 24, 128), slim_rows, slim_rows, slim_rows, slim_rows,
         slim_mid, slim_mid, slim_mid, slim_mid, (16, 128), (4, 8, 128)],
    )
    state = call(
        functools.partial(fine_kernel, False),
        [block, after, before],
        [(shape, F32) for shape in (fine, fine_up, fine, fine, fine, fine, mid, mid_up, mid, mid, mid)],
        [fine, fine, fine, fine, (2, 40, 128), rows, rows, rows, rows, mid, mid, mid],
        keep_out=range(11),
    )
    low, high = shift_along(up, "gx", 1), shift_along(down, "gx", -1)
    own = gather_plane(pay)
    pairs = (nx2 * ny2 // 16, 8, 128)
    own, low, high = lax.optimization_barrier((own, low, high))
    own0, own1 = own[..., :512].reshape(pairs), own[..., 512:].reshape(pairs)
    before, after = shift_along(own1, "gz", 1), shift_along(own0, "gz", -1)
    level_2, level_3 = (nx2, ny2, 128), (nx2 // 2, ny2 // 2, 128)
    window = (nx2 + 6, ny2, 128)
    half = (nx2 // 2, ny2, 128)
    first_pre, image, *more, pay = call(
        second_kernel,
        [*state, low, high, before, own0, own1, after],
        [((8, 16, 128), F32)] * 2
        + [(shape, F32) for shape in (fine, mid, *[level_2] * 4, *[level_3] * 4, (nx2 * ny2 // 8, 4, 128))],
        [(4,) + level_2, half, half, window, (8, 24, 128), mid, mid, wide, (2, 40, 128),
         fine, fine, fine, (8, 24, 256), mid, (32, 128)],
        keep_in=range(11),
        keep_out=range(2, 12),
    )
    own = gather_plane(pay)
    plane = (nx2 // 2, ny2 // 4, 128)
    own0, own1, parts = (own[..., 128 * k : 128 * k + 128].reshape(plane) for k in range(3))
    before, after = shift_along(own1, "gz", 1), shift_along(own0, "gz", -1)
    _, f0, f1, f2, w, _, _, f10, f11, f12, w1 = state
    mapped, sums = call(
        third_kernel,
        [f0, f1, f2, w, f10, f11, f12, w1, *more, before, own0, own1, after, parts],
        [((8, 16, 128), F32), ((1, 128), F32)],
        [level_2, half, half, window, (8, 24, 128), mid, mid, wide, (2, 40, 128), fine],
        keep_in=range(18),
    )
    peers = lax.axis_size("gz")
    sums = lax.all_to_all(jnp.broadcast_to(sums[None], (peers, 1, 128)), "gz", 0, 0, tiled=True)
    return tuple(
        call(
            last_kernel,
            [sums, right_side, first_pre, image, mapped],
            [((8, 16, 128), F32)] * 3,
        )
    )


def solution(mesh):
    placed = P("gx", "gy", "gz")
    return jax.shard_map(
        local,
        mesh=mesh,
        in_specs=(placed, P(None, "gx", "gy", "gz"), placed),
        out_specs=(placed, placed, placed),
        check_vma=False,
    )
```

```python
import functools

import jax
import jax.numpy as jnp
from jax import lax
from jax.experimental import pallas as pl
from jax.experimental.pallas import tpu as pltpu
from jax.sharding import PartitionSpec as P

F32 = jnp.float32
BF16 = jnp.bfloat16
ABSORB = 0.001
RELAX = 0.8
KEEP = 0.2
SWEEPS = 6
NEAR = pl.ds(8, 24)
VMEM_LIMIT = 24 * 1024 * 1024


def one_hot(rows, cols, rule, weight=1.0):
    r = lax.broadcasted_iota(jnp.int32, (rows, cols), 0)
    c = lax.broadcasted_iota(jnp.int32, (rows, cols), 1)
    return jnp.where(rule(r, c), weight, 0.0).astype(BF16)


def spread(values, matrix):
    high = values.astype(BF16)
    low = (values - high.astype(F32)).astype(BF16)
    return jnp.dot(high, matrix, preferred_element_type=F32) + jnp.dot(
        low, matrix, preferred_element_type=F32
    )


def pick(matrix, values):
    high = values.astype(BF16)
    low = (values - high.astype(F32)).astype(BF16)
    return jnp.dot(matrix, high, preferred_element_type=F32) + jnp.dot(
        matrix, low, preferred_element_type=F32
    )


def root(values):
    return values * lax.rsqrt(jnp.maximum(values, 1e-12))


def turn(values, shift, axis):
    return pltpu.roll(values, shift % values.shape[axis], axis)


def iota(shape, dim):
    return lax.broadcasted_iota(jnp.int32, shape, dim)


def plane_terms(v, f1, f2):
    return turn(v, 1, 0) * f1 + turn(v * f1, -1, 0) + turn(v, 1, 1) * f2 + turn(v * f2, -1, 1)


def neighbours(v_ref, f0_ref, f1_ref, f2_ref, p):
    return (
        f0_ref[p] * v_ref[p - 1]
        + f0_ref[p + 1] * v_ref[p + 1]
        + plane_terms(v_ref[p], f1_ref[p], f2_ref[p])
    )


def near_rows(v_ref, f0_ref, f1_ref, f2_ref, p):
    v, f2 = v_ref[p, NEAR, :], f2_ref[p, NEAR, :]
    return (
        f0_ref[p, NEAR, :] * v_ref[p - 1, NEAR, :]
        + f0_ref[p + 1, NEAR, :] * v_ref[p + 1, NEAR, :]
        + f1_ref[p, NEAR, :] * v_ref[p, pl.ds(7, 24), :]
        + f1_ref[p, pl.ds(9, 24), :] * v_ref[p, pl.ds(9, 24), :]
        + turn(v, 1, 1) * f2
        + turn(v * f2, -1, 1)
    )


def neighbours_3d(v, f0, f1, f2):
    zero = jnp.zeros_like(v[:1])
    up = f0 * v
    return (
        f0 * jnp.concatenate([zero, v[:-1]], 0)
        + jnp.concatenate([up[1:], zero], 0)
        + turn(v, 1, 1) * f1
        + turn(v * f1, -1, 1)
        + turn(v, 1, 2) * f2
        + turn(v * f2, -1, 2)
    )


def row_pairs(t_ref, values, both):
    out = []
    pairs = values.shape[0] // 2
    for half in range(2):
        t_ref[half, pl.ds(0, 2 * pairs), :] = values[:, 128 * half : 128 * half + 128]
        first = t_ref[half, pl.ds(0, pairs, 2), :]
        out.append(first + t_ref[half, pl.ds(1, pairs, 2), :] if both else first)
    return out


def put_rows(r_ref, q, halves, start=0):
    for half in range(2):
        r_ref[q, pl.ds(start, halves[half].shape[0]), pl.ds(128 * half, 128)] = halves[half]


def prepare_kernel(s_hbm, fc_hbm, solid_hbm, out_ref, ends_ref, s_ref, fc_ref, solid_ref, sems):
    copies = [
        pltpu.make_async_copy(source, target, sems.at[i])
        for i, (source, target) in enumerate(
            ((s_hbm, s_ref), (fc_hbm, fc_ref), (solid_hbm, solid_ref))
        )
    ]
    for copy in copies:
        copy.start()
    for copy in copies:
        copy.wait()
    s = s_ref[...]
    high = s.astype(BF16)
    out_ref[:, 0] = high
    out_ref[:, 1] = (s - high.astype(F32)).astype(BF16)
    weight = 1.0 - 0.75 * solid_ref[...].astype(F32)
    for a in range(3):
        out_ref[:, 2 + a] = (fc_ref[a].astype(F32) * weight).astype(BF16)
    lane = iota((16, 128), 1)

    def body(p, carry):
        ends = jnp.zeros((16, 128), F32)
        for f in range(5):
            t = turn(out_ref[p, f].astype(F32), 24 * f + 12, 1)
            ends = jnp.where((lane >= 24 * f) & (lane < 24 * f + 24), t, ends)
        ends_ref[p] = ends.astype(BF16)
        return carry

    lax.fori_loop(0, 8, body, 0, unroll=4)


def rim_kernel(own_ref, before_ref, after_ref, out_ref):
    lane = iota((8, 16, 128), 2)
    last = jnp.zeros((8, 16, 128), jnp.bool_)
    for f in range(5):
        last = last | ((lane >= 24 * f) & (lane < 24 * f + 12))
    out_ref[:, 0:5] = own_ref[...]
    rim = jnp.where(last, before_ref[...].astype(F32), after_ref[...].astype(F32))
    out_ref[:, 5] = rim.astype(BF16)


def edges_kernel(x_ref, up_ref, down_ref):
    row = iota((8, 128), 0)
    quarters = [(p, True) for p in range(5, 19)] + [(0, False), (23, False)]

    def body(f, carry):
        for t in range(11):
            pair = [x_ref[1 + 2 * t + k, f].astype(F32) for k in range(2)]
            up_ref[t, f] = jnp.concatenate([v[8:] for v in pair], 0).astype(BF16)
            down_ref[t, f] = jnp.concatenate([v[:8] for v in pair], 0).astype(BF16)
        for t in range(4):
            ups, downs = [], []
            for k in range(0, 4, 2):
                pair = []
                for p, inner in quarters[4 * t + k : 4 * t + k + 2]:
                    v = x_ref[p, f].astype(F32)
                    pair.append((v[:8], v[8:]) if inner else (v[8:], v[:8]))
                ups.append(jnp.where(row < 4, turn(pair[0][0], 4, 0), pair[1][0]))
                downs.append(jnp.where(row < 4, pair[0][1], turn(pair[1][1], 4, 0)))
            up_ref[11 + t, f] = jnp.concatenate(ups, 0).astype(BF16)
            down_ref[11 + t, f] = jnp.concatenate(downs, 0).astype(BF16)
        return carry

    lax.fori_loop(0, 6, body, 0, unroll=2)


def edge_rows(ym_ref, yp_ref, p, f, thin):
    row = iota((8, 128), 0)
    zero = jnp.zeros((8, 128), F32)

    def eight(ref, tile, k):
        return ref[tile, f].astype(F32)[8 * k : 8 * k + 8]

    def four(q, before):
        v = eight(ym_ref if before else yp_ref, 11 + q // 4, q % 4 // 2)
        moved = turn(v, 4, 0) if (q % 2 == 0) == before else v
        return jnp.where((row >= 4) == before, moved, 0.0)

    if p in (0, 23):
        q = 14 if p == 0 else 15
        near_before, near_after = four(q, True), four(q, False)
    else:
        near_before, near_after = (eight(ref, (p - 1) // 2, (p - 1) % 2) for ref in (ym_ref, yp_ref))
    if thin:
        return near_before, near_after
    if 5 <= p <= 18:
        far_before, far_after = four(p - 5, True), four(p - 5, False)
    else:
        far_before = far_after = zero
    return jnp.concatenate([far_before, near_before], 0), jnp.concatenate([near_after, far_after], 0)


def fine_kernel(thin, x_ref, yp_ref, ym_ref, *refs):
    if thin:
        (up_ref, down_ref, pay_ref,
         s_ref, f0_ref, f1_ref, f2_ref, s1_ref, f10_ref, f11_ref, f12_ref, w1_ref, *refs) = refs
    else:
        s_ref, f0_ref, f1_ref, f2_ref, w_ref, d_ref, s1_ref, f10_ref, f11_ref, f12_ref, w1_ref, *refs = refs
    (c0_ref, c1_ref, c2_ref, sm_ref, t_ref, r0_ref, r1_ref, r2_ref, rs_ref,
     l10_ref, l11_ref, l12_ref, *refs) = refs
    planes = range(4, 20) if thin else range(24)
    rows, rows_1 = s_ref.shape[1], s1_ref.shape[1]
    own = 4 if thin else 12
    shape, shape_1 = (rows, 256), (rows_1, 128)
    at_x = lax.axis_index("gx") == 0
    at_y = lax.axis_index("gy") == 0
    at_z = lax.axis_index("gz") == 0
    lane = iota((rows, 128), 1)
    side = (lane < 12) | (lane >= 116)

    for p in planes:
        tiles = []
        for f in range(6):
            before, after = edge_rows(ym_ref, yp_ref, p, f, thin)
            column = jnp.concatenate([before, x_ref[p, f].astype(F32), after], 0)
            tiles.append(turn(column, -4, 0)[:rows])
        rims = [
            jnp.where(side, turn(tiles[5], -(24 * f + 12), 1), 0.0) for f in range(5)
        ]
        s_ref[p, :, 0:128] = tiles[0] + tiles[1]
        s_ref[p, :, 128:256] = rims[0] + rims[1]
        for a, c_ref in enumerate((c0_ref, c1_ref, c2_ref)):
            c_ref[p, :, 0:128] = tiles[2 + a]
            c_ref[p, :, 128:256] = rims[2 + a]

    def faces(p, carry):
        before = jnp.maximum(p - 1, planes.start)
        f0_ref[p] = root(c0_ref[p] * c0_ref[before])
        c1 = c1_ref[p]
        f1_ref[p] = root(c1 * turn(c1, 1, 0))
        c2 = c2_ref[p]
        f2_ref[p] = root(c2 * turn(c2, 1, 1))
        return carry

    lax.fori_loop(planes.start, planes.stop, faces, 0, unroll=len(planes))
    f0_ref[planes.stop] = jnp.zeros(shape, F32)

    first_row = (iota(shape, 0) == own) & at_y
    first_lane = (iota(shape, 1) == 0) & at_z
    for ref in (r0_ref, r1_ref, r2_ref, rs_ref):
        ref[...] = jnp.zeros_like(ref)

    def diagonals(q, carry):
        lows = []
        for i in range(2):
            p = 2 * q + i
            f0, f1, f2 = f0_ref[p], f1_ref[p], f2_ref[p]
            low0 = f0 + jnp.where((p == 8) & at_x, c0_ref[p], 0.0)
            low1 = f1 + jnp.where(first_row, c1_ref[p], 0.0)
            low2 = f2 + jnp.where(first_lane, c2_ref[p], 0.0)
            d = ABSORB + low0 + f0_ref[p + 1] + low1 + turn(f1, -1, 0) + low2 + turn(f2, -1, 1)
            w = RELAX / d
            if not thin:
                d_ref[p] = d
                w_ref[p] = w
            sm_ref[p] = w * s_ref[p]
            lows.append((low0, low1, low2))
        put_rows(r0_ref, q, row_pairs(t_ref, lows[0][0], True))
        put_rows(r1_ref, q, row_pairs(t_ref, lows[0][1] + lows[1][1], False))
        put_rows(r2_ref, q, row_pairs(t_ref, lows[0][2] + lows[1][2], True))
        return carry

    lax.fori_loop(planes.start // 2, planes.stop // 2, diagonals, 0, unroll=len(planes) // 2)

    def leftovers(q, carry):
        total = jnp.zeros(shape, F32)
        for i in range(2):
            p = 2 * q + i
            total += KEEP * s_ref[p] + neighbours(sm_ref, f0_ref, f1_ref, f2_ref, p)
        put_rows(rs_ref, q, row_pairs(t_ref, total, True))
        return carry

    lax.fori_loop(planes.start // 2 + 1, planes.stop // 2 - 1, leftovers, 0, unroll=len(planes) // 2 - 2)

    pairs = one_hot(256, 128, lambda r, c: lax.shift_right_logical(r, 1) == c, 0.25)
    evens = one_hot(256, 128, lambda r, c: r == 2 * c, 0.25)
    first, count = planes.start // 2, len(planes) // 2
    for target, source, matrix in (
        (l10_ref, r0_ref, pairs), (l11_ref, r1_ref, pairs), (l12_ref, r2_ref, evens), (s1_ref, rs_ref, pairs)
    ):
        target[...] = jnp.zeros_like(target)
        value = spread(source[pl.ds(first, count)].reshape(count * rows_1, 256), matrix)
        value = value.reshape(count, rows_1, 128)
        target[pl.ds(first + 2, count)] = 2.0 * value if target is s1_ref else value

    first_row_1 = (iota(shape_1, 0) == own // 2) & at_y
    first_lane_1 = (iota(shape_1, 1) == 0) & at_z
    planes_1 = range(first + 2, first + 2 + count)

    def faces_1(p, carry):
        f10_ref[p] = jnp.where((p == 6) & at_x, 0.0, l10_ref[p])
        f11_ref[p] = jnp.where(first_row_1, 0.0, l11_ref[p])
        f12_ref[p] = jnp.where(first_lane_1, 0.0, l12_ref[p])
        return carry

    lax.fori_loop(planes_1.start, planes_1.stop, faces_1, 0, unroll=len(planes_1))
    f10_ref[planes_1.stop] = jnp.zeros(shape_1, F32)

    def diagonals_1(p, carry):
        d = (
            4.0 * ABSORB + l10_ref[p] + f10_ref[p + 1]
            + l11_ref[p] + turn(f11_ref[p], -1, 0)
            + l12_ref[p] + turn(f12_ref[p], -1, 1)
        )
        w1_ref[p] = RELAX / d
        return carry

    lax.fori_loop(planes_1.start, planes_1.stop, diagonals_1, 0, unroll=len(planes_1))
    if thin:
        pack_level_2(
            up_ref, down_ref, pay_ref, s1_ref, f10_ref, f11_ref, f12_ref, w1_ref, l10_ref, l11_ref, l12_ref, *refs
        )


def pack_level_2(
    up_ref, down_ref, pay_ref, s1_ref, f10_ref, f11_ref, f12_ref, w1_ref, l10_ref, l11_ref, l12_ref,
    sm1_ref, t1_ref, u_ref,
):
    for target, start in ((up_ref, 5), (down_ref, 9)):
        for i, (ref, k) in enumerate(((s1_ref, 0), (s1_ref, 1), (w1_ref, 0), (w1_ref, 1), (f10_ref, 1))):
            target[i] = ref[start + k]
    for p in range(5, 11):
        sm1_ref[p] = w1_ref[p] * s1_ref[p]

    def quad(values, both):
        t1_ref[...] = values
        first = t1_ref[pl.ds(2, 4, 2), :]
        return first + t1_ref[pl.ds(3, 4, 2), :] if both else first

    def leftover_1(p):
        return KEEP * s1_ref[p] + neighbours(sm1_ref, f10_ref, f11_ref, f12_ref, p)

    row8, lane8 = iota((8, 128), 0), iota((8, 128), 1)
    narrow = one_hot(128, 128, lambda r, c: (lax.shift_right_logical(r, 1) == c) & (r < 64))
    narrow_even = one_hot(128, 128, lambda r, c: (r == 2 * c) & (r < 64))
    total = jnp.zeros((8, 128), F32)
    for f in range(4):
        for i in range(2):
            p = 6 + 2 * i
            if f == 0:
                part = quad(leftover_1(p) + leftover_1(p + 1), True)
            elif f == 1:
                part = quad(l10_ref[p], True)
            elif f == 2:
                part = quad(l11_ref[p] + l11_ref[p + 1], False)
            else:
                part = quad(l12_ref[p] + l12_ref[p + 1], True)
            u_ref[f, pl.ds(4 * i, 4), :] = part * (0.5 if f == 0 else 0.25)
        part = spread(u_ref[f], narrow_even if f == 3 else narrow)
        for i in range(2):
            for h in range(2):
                to = 32 * f + 16 * i
                moved = turn(turn(part, 4 * (h - i), 0), to - 16 * h, 1)
                here = (lax.shift_right_logical(row8, 2) == h) & (lane8 >= to) & (lane8 < to + 16)
                total = jnp.where(here, moved, total)
    pay_ref[...] = jnp.broadcast_to(total[None], pay_ref.shape)


def window(pieces, to, lane):
    out = pieces[3]
    for k in range(3):
        start = (to + 16 * k) % 128
        here = (lane >= start) & (lane < start + 16)
        out = jnp.where(here, pieces[k], out)
    return jnp.where(lane < 64, turn(out, -to, 1), 0.0)


def solve_2(s2, level_2, level_3, t3_ref, e_ref):
    f0, f1, f2, w = level_2
    g0, g1, g2, w3 = level_3
    nx, ny, _ = s2.shape
    sm = w * s2
    left = KEEP * s2 + neighbours_3d(sm, f0, f1, f2)
    s3 = coarse_2(left.reshape(nx // 2, 2, ny, 128).sum(1), t3_ref, True, 0.5, False)
    e = w3 * s3
    for _ in range(SWEEPS - 1):
        e = KEEP * e + w3 * (s3 + neighbours_3d(e, g0, g1, g2))
    widen = one_hot(128, 128, lambda r, c: (r == lax.shift_right_logical(c, 1)) & (c < 64))
    wide = spread(e.reshape(nx * ny // 4, 128), widen).reshape(nx // 2, ny // 2, 128)
    for x in range(nx // 2):
        for i in range(2):
            e_ref[x, pl.ds(i, ny // 2, 2), :] = wide[x]
    e2 = e_ref[...]
    corrected = sm + jnp.concatenate([e2[:, None], e2[:, None]], 1).reshape(nx, ny, 128)
    return KEEP * corrected + w * (s2 + neighbours_3d(corrected, f0, f1, f2))


def coarse_2(values, t3_ref, both, weight, even):
    nx, ny, _ = values.shape
    t3_ref[...] = values
    first = t3_ref[:, pl.ds(0, ny // 2, 2), :]
    if both:
        first = first + t3_ref[:, pl.ds(1, ny // 2, 2), :]
    if even:
        rule = lambda r, c: (r == 2 * c) & (r < 64)
    else:
        rule = lambda r, c: (lax.shift_right_logical(r, 1) == c) & (r < 64)
    flat = spread(first.reshape(nx * ny // 2, 128), one_hot(128, 128, rule, weight))
    return flat.reshape(nx, ny // 2, 128)


def coefficients(low, mask_lane, absorb):
    shape = low[0].shape
    f0 = jnp.where(iota(shape, 0) == 0, 0.0, low[0])
    f1 = jnp.where(iota(shape, 1) == 0, 0.0, low[1])
    f2 = jnp.where((iota(shape, 2) == mask_lane) & (lax.axis_index("gz") == 0), 0.0, low[2])
    d = (
        absorb + low[0] + jnp.concatenate([f0[1:], jnp.zeros_like(f0[:1])], 0)
        + low[1] + turn(f1, -1, 1) + low[2] + turn(f2, -1, 2)
    )
    return f0, f1, f2, RELAX / d


def fetch_level_2(m2_ref, planes, pick_ref):
    gx, gy = lax.axis_index("gx"), lax.axis_index("gy")
    ny = m2_ref.shape[1]

    def source(c):
        return jnp.where(c < 96, 16, -48) + lax.shift_right_logical(c, 1)

    widen = one_hot(128, 128, lambda r, c: r == source(c))
    rows = one_hot(24, ny, lambda r, c: c == 4 * gy - 3 + lax.shift_right_logical(r, 1))
    flat = m2_ref[pl.ds(2 * gx + planes.start, len(planes))].reshape(len(planes) * ny, 128)
    wide = spread(flat, widen).reshape(len(planes), ny, 128)
    for k in planes:
        pick_ref[k] = pick(rows, wide[k - planes.start])


def widen_level_1(m1_ref, wide_ref, lo, hi):
    rows = 24 * (hi - lo)
    widen = one_hot(128, 256, lambda r, c: r == lax.shift_right_logical(c, 1))
    wide_ref[pl.ds(lo, hi - lo)] = spread(m1_ref[pl.ds(lo, hi - lo)].reshape(rows, 128), widen).reshape(
        hi - lo, 24, 256
    )


def double_rows(t_ref, wide_ref, q, start=0, count=20):
    for half in range(2):
        part = wide_ref[q, pl.ds(start, count), pl.ds(128 * half, 128)]
        for i in range(2):
            t_ref[half, pl.ds(i, count, 2), :] = part
    return jnp.concatenate([t_ref[half, pl.ds(0, 2 * count), :] for half in range(2)], 1)


def second_kernel(
    s_ref, f0_ref, f1_ref, f2_ref, w_ref, d_ref,
    s1_ref, f10_ref, f11_ref, f12_ref, w1_ref,
    low_in, high_in, before_ref, own0_ref, own1_ref, after_ref,
    fp_out, im_out, im_ref, t1s_ref, f20_ref, f21_ref, f22_ref, w2_ref,
    f30_ref, f31_ref, f32_ref, w3_ref, pay_ref,
    v_ref, t3_ref, e_ref, m2_ref, pick_ref, corr1_ref, m1_ref, wide_ref, t_ref,
    corr_ref, fp_ref, sm_ref, rs_ref, sm1_ref, tq_ref, low_ref, high_ref,
):
    nx2, ny2 = f20_ref.shape[:2]
    lane8 = iota((8, 128), 1)
    row8 = iota((8, 128), 0)

    def assemble(x, carry):
        for pair in range(ny2 // 8):
            g = x * (ny2 // 8) + pair
            pieces = [turn(ref[g], 16 * k, 1) for k, ref in enumerate((before_ref, own0_ref, own1_ref, after_ref))]
            for f in range(4):
                for i in range(2):
                    v_ref[f, 2 * x + i, pl.ds(8 * pair, 8), :] = window(pieces, 32 * f + 16 * i, lane8)
        return carry

    lax.fori_loop(0, nx2 // 2, assemble, 0, unroll=8)

    s2 = v_ref[0]
    low = (v_ref[1], v_ref[2], v_ref[3])
    level_2 = coefficients(low, 16, 16.0 * ABSORB)
    f20_ref[...], f21_ref[...], f22_ref[...], w2_ref[...] = level_2
    halves = [t.reshape(nx2 // 2, 2, ny2, 128) for t in low]
    low_3 = (
        coarse_2(halves[0][:, 0], t3_ref, True, 0.25, False),
        coarse_2(halves[1].sum(1), t3_ref, False, 0.25, False),
        coarse_2(halves[2].sum(1), t3_ref, True, 0.25, True),
    )
    level_3 = coefficients(low_3, 8, 64.0 * ABSORB)
    f30_ref[...], f31_ref[...], f32_ref[...], w3_ref[...] = level_3
    m2_ref[...] = jnp.zeros_like(m2_ref)
    m2_ref[pl.ds(3, nx2)] = solve_2(s2, level_2, level_3, t3_ref, e_ref)
    fetch_level_2(m2_ref, range(8), pick_ref)

    def correct_1(p, carry):
        corr1_ref[p] = w1_ref[p] * s1_ref[p] + pick_ref[lax.shift_right_logical(p, 1)]
        return carry

    for target, source in ((low_ref, low_in), (high_ref, high_in)):
        target[...] = jnp.zeros_like(target)
        target[:, pl.ds(4, 12), :] = source[:, pl.ds(0, 12), :]
    lax.fori_loop(3, 13, correct_1, 0, unroll=10)
    for k in range(2):
        corr1_ref[1 + k] = low_ref[2 + k] * low_ref[k] + pick_ref[(1 + k) // 2]
        corr1_ref[13 + k] = high_ref[2 + k] * high_ref[k] + pick_ref[(13 + k) // 2]

    def relax_1(p, carry):
        m1_ref[p] = KEEP * corr1_ref[p] + w1_ref[p] * (
            s1_ref[p] + neighbours(corr1_ref, f10_ref, f11_ref, f12_ref, p)
        )
        return carry

    lax.fori_loop(3, 13, relax_1, 0, unroll=10)
    for p, source, w, face, next_face in (
        (2, low_ref[1], low_ref[3], low_ref[4], f10_ref[3]),
        (13, high_ref[0], high_ref[2], f10_ref[13], high_ref[4]),
    ):
        m1_ref[p] = KEEP * corr1_ref[p] + w * (
            source + face * corr1_ref[p - 1] + next_face * corr1_ref[p + 1]
            + plane_terms(corr1_ref[p], f11_ref[p], f12_ref[p])
        )
    widen_level_1(m1_ref, wide_ref, 2, 14)

    def correct(q, carry):
        e = double_rows(t_ref, wide_ref, q)
        for i in range(2):
            p = 2 * q + i - 4
            corr_ref[p] = w_ref[p] * s_ref[p] + e
        return carry

    lax.fori_loop(2, 14, correct, 0, unroll=12)

    def relax(p, carry):
        fp_ref[p] = KEEP * corr_ref[p] + w_ref[p] * (
            s_ref[p] + neighbours(corr_ref, f0_ref, f1_ref, f2_ref, p)
        )
        return carry

    def relax_near(p, carry):
        fp_ref[p, NEAR, :] = KEEP * corr_ref[p, NEAR, :] + w_ref[p, NEAR, :] * (
            s_ref[p, NEAR, :] + near_rows(corr_ref, f0_ref, f1_ref, f2_ref, p)
        )
        return carry

    lax.fori_loop(2, 7, relax_near, 0, unroll=5)
    lax.fori_loop(7, 17, relax, 0, unroll=10)
    lax.fori_loop(17, 22, relax_near, 0, unroll=5)

    def image(p, carry):
        im = d_ref[p] * fp_ref[p] - neighbours(fp_ref, f0_ref, f1_ref, f2_ref, p)
        im_ref[p] = im
        sm_ref[p] = w_ref[p] * im
        return carry

    def image_near(p, carry):
        im = d_ref[p, NEAR, :] * fp_ref[p, NEAR, :] - near_rows(fp_ref, f0_ref, f1_ref, f2_ref, p)
        im_ref[p, NEAR, :] = im
        sm_ref[p, NEAR, :] = w_ref[p, NEAR, :] * im
        return carry

    lax.fori_loop(3, 8, image_near, 0, unroll=5)
    lax.fori_loop(8, 16, image, 0, unroll=8)
    lax.fori_loop(16, 21, image_near, 0, unroll=5)

    rs_ref[...] = jnp.zeros_like(rs_ref)
    inside = (iota((24, 128), 0) >= 4) & (iota((24, 128), 0) < 20)

    def leftovers(q, sums):
        total = jnp.zeros((24, 256), F32)
        for i in range(2):
            p = 2 * q + i - 4
            left = KEEP * im_ref[p, NEAR, :] + near_rows(sm_ref, f0_ref, f1_ref, f2_ref, p)
            total += left
            own = inside & (p >= 8) & (p < 16)
            fp, im = fp_ref[p, NEAR, 0:128], im_ref[p, NEAR, 0:128]
            terms = (s_ref[p, NEAR, 0:128] * fp, fp * im, sm_ref[p, NEAR, 0:128] * (im + left[:, 0:128]))
            sums = tuple(old + jnp.where(own, new, 0.0) for old, new in zip(sums, terms))
        put_rows(rs_ref, q - 4, row_pairs(t_ref, total, True), 4)
        return sums

    zero = jnp.zeros((24, 128), F32)
    sums = lax.fori_loop(4, 12, leftovers, (zero, zero, zero), unroll=8)

    for p in range(8):
        fp_out[p] = fp_ref[8 + p, pl.ds(12, 16), 0:128]
        im_out[p] = im_ref[8 + p, pl.ds(12, 16), 0:128]

    pairs = one_hot(256, 128, lambda r, c: lax.shift_right_logical(r, 1) == c, 0.5)
    t1s_ref[...] = jnp.zeros_like(t1s_ref)
    t1s_ref[pl.ds(4, 8)] = spread(rs_ref[...].reshape(192, 256), pairs).reshape(8, 24, 128)
    for p in range(5, 11):
        sm1_ref[p] = w1_ref[p] * t1s_ref[p]
    inside_1 = (iota((24, 128), 0) >= 6) & (iota((24, 128), 0) < 14) & (iota((24, 128), 1) < 64)
    second = jnp.zeros((24, 128), F32)
    halves = [jnp.zeros((8, 128), F32)] * 2
    tq_ref[...] = jnp.zeros_like(tq_ref)
    for i in range(2):
        total = jnp.zeros((24, 128), F32)
        for j in range(2):
            p = 6 + 2 * i + j
            s1 = t1s_ref[p]
            left = KEEP * s1 + neighbours(sm1_ref, f10_ref, f11_ref, f12_ref, p)
            second += jnp.where(inside_1, sm1_ref[p] * (s1 + left), 0.0)
            total += left
        tq_ref[pl.ds(0, 24), :] = total
        tq_ref[pl.ds(24, 4), :] = tq_ref[pl.ds(6, 4, 2), :] + tq_ref[pl.ds(7, 4, 2), :]
        for h in range(2):
            place = one_hot(
                128, 128,
                lambda r, c, i=i, h=h: (lax.shift_right_logical(r, 1) - 16 * h == (c & 15))
                & (r < 64) & ((lax.shift_right_logical(c, 4) & 1) == i), 0.5,
            )
            halves[h] += spread(tq_ref[pl.ds(24, 8), :], place)
    scalars = (jnp.sum(sums[0]), jnp.sum(sums[1]), jnp.sum(sums[2]) + 2.0 * jnp.sum(second))
    mine = lax.shift_right_logical(lane8, 5) == row8
    pay = jnp.zeros((8, 128), F32)
    for h in range(2):
        line = jnp.sum(jnp.where(mine, halves[h], 0.0), axis=0, keepdims=True)
        pay = jnp.where(row8 == h, line, pay)
    for k, value in enumerate(scalars):
        pay = jnp.where((lane8 == k) & (row8 == 2), value, pay)
    pay_ref[...] = jnp.broadcast_to(pay[None, :4], pay_ref.shape)


def third_kernel(
    f0_ref, f1_ref, f2_ref, w_ref, f10_ref, f11_ref, f12_ref, w1_ref,
    im_ref, t1s_ref, f20_ref, f21_ref, f22_ref, w2_ref, f30_ref, f31_ref, f32_ref, w3_ref,
    before_ref, own0_ref, own1_ref, after_ref, parts_ref,
    mi_out, scalar_out,
    v_ref, t3_ref, e_ref, m2_ref, pick_ref, corr1_ref, m1_ref, wide_ref, t_ref, corr_ref,
):
    nx2, ny2 = f20_ref.shape[:2]
    lane = iota((ny2 // 4, 128), 1)

    def assemble(x, carry):
        pieces = [turn(ref[x], 16 * k, 1) for k, ref in enumerate((before_ref, own0_ref, own1_ref, after_ref))]
        for i in range(2):
            for j in range(4):
                v_ref[2 * x + i, pl.ds(j, ny2 // 4, 4), :] = window(pieces, 32 * j + 16 * i, lane)
        return carry

    lax.fori_loop(0, nx2 // 2, assemble, 0, unroll=8)
    s2 = v_ref[...]
    level_2 = (f20_ref[...], f21_ref[...], f22_ref[...], w2_ref[...])
    level_3 = (f30_ref[...], f31_ref[...], f32_ref[...], w3_ref[...])
    m2 = solve_2(s2, level_2, level_3, t3_ref, e_ref)
    lane3 = iota(s2.shape, 2)
    part = 4.0 * jnp.sum(jnp.where((lane3 >= 16) & (lane3 < 48), s2 * m2, 0.0))
    sums = jnp.sum(jnp.sum(parts_ref[...], axis=0), axis=0, keepdims=True)
    scalar_out[...] = jnp.where(iota((1, 128), 1) == 3, part, sums)
    m2_ref[...] = jnp.zeros_like(m2_ref)
    m2_ref[pl.ds(3, nx2)] = m2
    fetch_level_2(m2_ref, range(2, 6), pick_ref)

    for p in range(4, 12):
        corr1_ref[p] = w1_ref[p] * t1s_ref[p] + pick_ref[p // 2]
    for p in range(5, 11):
        m1_ref[p] = KEEP * corr1_ref[p] + w1_ref[p] * (
            t1s_ref[p] + neighbours(corr1_ref, f10_ref, f11_ref, f12_ref, p)
        )
    widen_level_1(m1_ref, wide_ref, 5, 11)

    def correct(q, carry):
        e = double_rows(t_ref, wide_ref, q, 4, 12)
        for i in range(2):
            p = 2 * q + i - 4
            corr_ref[p, NEAR, :] = w_ref[p, NEAR, :] * im_ref[p, NEAR, :] + e
        return carry

    lax.fori_loop(5, 11, correct, 0, unroll=6)

    for p in range(8):
        q = 8 + p
        mi = KEEP * corr_ref[q, NEAR, :] + w_ref[q, NEAR, :] * (
            im_ref[q, NEAR, :] + near_rows(corr_ref, f0_ref, f1_ref, f2_ref, q)
        )
        mi_out[p] = mi[4:20, 0:128]


def last_kernel(sums_ref, s_ref, fp_ref, im_ref, mi_ref, solution_ref, residual_ref, direction_ref):
    total = jnp.sum(sums_ref[...], axis=0)
    lane = iota((1, 128), 1)

    def value(lanes):
        keep = lane == lanes[0]
        for k in lanes[1:]:
            keep = keep | (lane == k)
        return jnp.sum(jnp.where(keep, total, 0.0), axis=1, keepdims=True)

    projected, curvature, product = value((0,)), value((1,)), value((2, 3))
    step = projected / curvature
    share = product / curvature
    for p in range(8):
        fp = fp_ref[p]
        solution_ref[p] = step * fp
        residual_ref[p] = s_ref[p] - step * im_ref[p]
        direction_ref[p] = step * (share * fp - mi_ref[p])


def call(kernel, inputs, outs, scratch=(), keep_in=(), keep_out=(), space=pltpu.VMEM):
    vmem = pl.BlockSpec(memory_space=pltpu.VMEM)
    inputs = [
        pltpu.with_memory_space_constraint(value, space) if i in keep_in else value
        for i, value in enumerate(inputs)
    ]
    shapes = [
        pltpu.VMEM(shape, dtype) if i in keep_out else jax.ShapeDtypeStruct(shape, dtype)
        for i, (shape, dtype) in enumerate(outs)
    ]
    return pl.pallas_call(
        kernel,
        out_shape=shapes,
        in_specs=[pl.BlockSpec(memory_space=space)] * len(inputs),
        out_specs=[vmem] * len(outs),
        scratch_shapes=[pltpu.VMEM(shape, F32) if isinstance(shape, tuple) else shape for shape in scratch],
        compiler_params=pltpu.CompilerParams(vmem_limit_bytes=VMEM_LIMIT),
    )(*inputs)


def shift_along(value, axis, by):
    size = lax.axis_size(axis)
    return lax.ppermute(value, axis, [(i, i + by) for i in range(size) if 0 <= i + by < size])


def gather_plane(copies):
    copies = copies.reshape(copies.shape[0], 1, -1)
    return lax.all_to_all(copies, ("gx", "gy"), 0, 0, tiled=True)


def local(right_side, face_coefficients, solid):
    nx2, ny2 = 2 * lax.axis_size("gx"), 4 * lax.axis_size("gy")
    own, ends = call(
        prepare_kernel,
        [right_side, face_coefficients, solid],
        [((8, 5, 16, 128), BF16), ((8, 16, 128), BF16)],
        [
            (8, 16, 128),
            pltpu.VMEM((3, 8, 16, 128), BF16),
            pltpu.VMEM((8, 16, 128), jnp.int32),
            pltpu.SemaphoreType.DMA((3,)),
        ],
        keep_in=range(3),
        space=pltpu.HBM,
    )
    before, after = shift_along(ends, "gz", 1), shift_along(ends, "gz", -1)
    (own,) = call(rim_kernel, [own, before, after], [((8, 6, 16, 128), BF16)])
    block = jnp.concatenate([shift_along(own, "gx", 1), own, shift_along(own, "gx", -1)], axis=0)
    to_up, to_down = call(edges_kernel, [block], [((15, 6, 16, 128), BF16)] * 2)
    before, after = shift_along(to_up, "gy", 1), shift_along(to_down, "gy", -1)

    fine, fine_up = (24, 40, 256), (25, 40, 256)
    mid, mid_up = (16, 24, 128), (17, 24, 128)
    rows, wide, edge = (12, 24, 256), (16, 24, 256), (5, 16, 128)
    slim, slim_up, slim_mid, slim_mid_up, slim_rows = (
        (20, 24, 256), (21, 24, 256), (16, 16, 128), (17, 16, 128), (12, 16, 256)
    )
    up, down, pay = call(
        functools.partial(fine_kernel, True),
        [block, after, before],
        [(edge, F32), (edge, F32), ((lax.axis_size(("gx", "gy")), 8, 128), F32)],
        [slim, slim_up, slim, slim, slim_mid, slim_mid_up, slim_mid, slim_mid, slim_mid,
         slim, slim, slim, slim, (2, 24, 128), slim_rows, slim_rows, slim_rows, slim_rows,
         slim_mid, slim_mid, slim_mid, slim_mid, (16, 128), (4, 8, 128)],
    )
    state = call(
        functools.partial(fine_kernel, False),
        [block, after, before],
        [(shape, F32) for shape in (fine, fine_up, fine, fine, fine, fine, mid, mid_up, mid, mid, mid)],
        [fine, fine, fine, fine, (2, 40, 128), rows, rows, rows, rows, mid, mid, mid],
        keep_out=range(11),
    )
    low, high = shift_along(up, "gx", 1), shift_along(down, "gx", -1)
    own = gather_plane(pay)
    pairs = (nx2 * ny2 // 16, 8, 128)
    own, low, high = lax.optimization_barrier((own, low, high))
    own0, own1 = own[..., :512].reshape(pairs), own[..., 512:].reshape(pairs)
    before, after = shift_along(own1, "gz", 1), shift_along(own0, "gz", -1)
    level_2, level_3 = (nx2, ny2, 128), (nx2 // 2, ny2 // 2, 128)
    window = (nx2 + 6, ny2, 128)
    half = (nx2 // 2, ny2, 128)
    first_pre, image, *more, pay = call(
        second_kernel,
        [*state, low, high, before, own0, own1, after],
        [((8, 16, 128), F32)] * 2
        + [(shape, F32) for shape in (fine, mid, *[level_2] * 4, *[level_3] * 4, (nx2 * ny2 // 8, 4, 128))],
        [(4,) + level_2, half, half, window, (8, 24, 128), mid, mid, wide, (2, 40, 128),
         fine, fine, fine, (8, 24, 256), mid, (32, 128), (5, 24, 128), (5, 24, 128)],
        keep_in=range(11),
        keep_out=range(2, 12),
    )
    own = gather_plane(pay)
    plane = (nx2 // 2, ny2 // 4, 128)
    own0, own1, parts = (own[..., 128 * k : 128 * k + 128].reshape(plane) for k in range(3))
    before, after = shift_along(own1, "gz", 1), shift_along(own0, "gz", -1)
    _, f0, f1, f2, w, _, _, f10, f11, f12, w1 = state
    mapped, sums = call(
        third_kernel,
        [f0, f1, f2, w, f10, f11, f12, w1, *more, before, own0, own1, after, parts],
        [((8, 16, 128), F32), ((1, 128), F32)],
        [level_2, half, half, window, (8, 24, 128), mid, mid, wide, (2, 40, 128), fine],
        keep_in=range(18),
    )
    peers = lax.axis_size("gz")
    sums = lax.all_to_all(jnp.broadcast_to(sums[None], (peers, 1, 128)), "gz", 0, 0, tiled=True)
    return tuple(
        call(
            last_kernel,
            [sums, right_side, first_pre, image, mapped],
            [((8, 16, 128), F32)] * 3,
        )
    )


def solution(mesh):
    placed = P("gx", "gy", "gz")
    return jax.shard_map(
        local,
        mesh=mesh,
        in_specs=(placed, P(None, "gx", "gy", "gz"), placed),
        out_specs=(placed, placed, placed),
        check_vma=False,
    )
```
